128 devices in a mesh: seq: 16 (over z, y), head: 8 (over x, core).
Axes of the slice: x: 4, y: 4, z: 4, core: 2. Of those that a mesh axis runs over, the one named last changes fastest.
Arguments:
- qkv: bfloat16 [16384, 3, 3072], P(('seq', 'head')), may hold values from -6 to 6
- eta: float32 [48], P('head'), may hold values from 1.8310548e-05 to 0.00390625
- initial: float32 [48, 64, 64], P('head'), may hold values from -0.75 to 0.75
- gain: float32 [3072], P('head'), may hold values from 0.25 to 1.75
- w_out: bfloat16 [3072, 3072], P('head'), may hold values from -0.109375 to 0.109375
Outputs:
- mixed: float32 [16384, 3072], P(('seq', 'head'))
The draws below stay inside these ranges and needn't reach their ends.
All inputs are finite; a program needn't handle non-finite values.
Results may differ from the reference program's by a relative error of at most 0.0029.
Values may be sent and summed in bfloat16 or wider, within the bound.
A program may use at most 128 MiB of HBM per device.

```python
import math
import jax
import jax.numpy as jnp
from jax import lax

D = 3072
HEADS = 48
HD = 64
MB = 64
TOKENS = 16384


def block_scale(own_key, shape, split, least, largest):
    loudness, own = 1.0, jax.random.fold_in(own_key, 6)
    for axis_at, blocks in split:
        heights = jnp.exp(jax.random.uniform(jax.random.fold_in(own, axis_at), (blocks,), jnp.float32, least / len(split), largest / len(split)))
        loudness = loudness * jnp.repeat(heights, shape[axis_at] // blocks).reshape([-1 if axis == axis_at else 1 for axis in range(len(shape))])
    return loudness


def noise(key, extent, deviation, most, cuts=(), kind=jnp.bfloat16):
    result = deviation * jax.random.normal(key, extent, jnp.float32)
    if cuts:
        result = result * block_scale(key, extent, cuts, -0.22, 0.18)
    return jnp.clip(result, -most, most).astype(kind)


def setup_inputs(seed: int = 0) -> dict:
    key_of = jax.random.split(jax.random.key(seed), 6)
    qkv = noise(key_of[0], (TOKENS, 3, HEADS * HD), 1.0, 6.0, ((0, 128),))
    eta = jnp.clip(jnp.exp(math.log(0.00390625) - 5.362856 * jax.random.uniform(key_of[1], (HEADS,), jnp.float32) ** block_scale(key_of[1], (HEADS,), ((0, 8),), -0.2, 0.2)), 1.831054760259576e-05, 0.00390625)
    initial = noise(key_of[2], (HEADS, HD, HD), HD ** -0.5, 0.75, ((0, 8),), jnp.float32)
    gain = jnp.clip(1.0 + 0.15 * jax.random.normal(key_of[3], (HEADS * HD,), jnp.float32), 0.25, 1.75)
    w_out = noise(key_of[4], (HEADS * HD, D), (HEADS * HD) ** -0.5, 0.109375, ((0, 8),))
    return {"qkv": qkv, "eta": eta, "initial": initial, "gain": gain, "w_out": w_out}


precise = lax.Precision.HIGHEST

def affine_parts(block, learn_rate):
    key_rows = block[:, 1].astype(jnp.float32)
    value_rows = block[:, 2].astype(jnp.float32)
    key_gram = jnp.einsum('mhi,mhj->hij', key_rows, key_rows, precision=precise)
    key_value = jnp.einsum('mhi,mhj->hij', key_rows, value_rows, precision=precise)
    identity = jnp.eye(key_gram.shape[-1], dtype=jnp.float32)
    return (identity - learn_rate[:, None, None] * key_gram, learn_rate[:, None, None] * key_value)

def reference(qkv, eta, initial, gain, w_out):
    blocks = qkv.reshape(TOKENS // MB, MB, 3, HEADS, HD)

    def advance(fast_state, block):
        linear, offset = affine_parts(block, eta)
        fresh = jnp.einsum('hij,hjk->hik', linear, fast_state, precision=precise) + offset
        return (fresh, fresh)
    _, forward_states = lax.scan(advance, initial, blocks)
    _, backward_states = lax.scan(advance, initial, blocks, reverse=True)
    combined = forward_states + backward_states
    queries = blocks[:, :, 0].astype(jnp.float32)
    read = jnp.einsum('bmhi,bhij->bmhj', queries, combined, precision=precise)
    mean_square = lax.optimization_barrier(jnp.mean(read * read, axis=-1, keepdims=True))
    normed = (read * lax.rsqrt(mean_square + 1e-06) * gain.reshape(HEADS, HD)).astype(jnp.bfloat16)
    normed = normed.reshape(TOKENS, HEADS * HD)
    return jnp.dot(normed, w_out, preferred_element_type=jnp.float32)
```

```python
import functools

import jax
import jax.numpy as jnp
from jax import lax
from jax.experimental import pallas as pl
from jax.experimental.pallas import tpu as pltpu
from jax.sharding import PartitionSpec as P

MESH = pl.DeviceIdType.MESH
MB = 64
HD = 64
PAIR = 2 * HD
BF = jnp.bfloat16
F32 = jnp.float32


def split(x):
    high = x.astype(BF)
    return high, (x - high.astype(F32)).astype(BF)


def dot(a, b):
    return lax.dot_general(a, b, (((1,), (0,)), ((), ())), preferred_element_type=F32)


def layer_kernel(
    seqs, heads, pairs,
    qkv, eta, initial, gain, out,
    recv, a_ref, b_ref, pre, totals, inbox, outbox, entry, q_high, q_low, r_ref, normed,
    kv_send, kv_recv, q_send, q_recv, tot_send, tot_recv, fin_send, fin_recv, nrm_send, nrm_recv,
):
    s = lax.axis_index("seq")
    h = lax.axis_index("head")
    x, c = h // 2, h % 2
    xs = heads // 2
    rows = qkv.shape[1]
    width = pairs * PAIR
    subs = rows // MB
    batches = heads * subs
    chains = 4 * pairs

    barrier = pltpu.get_barrier_semaphore()

    def greet_head(d, _):
        pl.semaphore_signal(barrier, inc=1, device_id=(s, (h + d) % heads), device_id_type=MESH)
        return 0

    def greet_seq(d, _):
        pl.semaphore_signal(barrier, inc=1, device_id=((s + d) % seqs, h), device_id_type=MESH)
        return 0

    lax.fori_loop(1, heads, greet_head, 0)
    lax.fori_loop(1, seqs, greet_seq, 0)
    pl.semaphore_wait(barrier, heads + seqs - 2)

    def peer(d, sign):
        dx, dc = d // 2, d % 2
        return ((x + sign * dx + xs) % xs) * 2 + (c + dc) % 2

    def near_first(i):
        step = i // 2
        dx = jnp.where(step < 2, step, xs + 1 - step)
        return dx * 2 + i % 2

    def kv_copy(d):
        to = peer(d, 1)
        return pltpu.make_async_remote_copy(
            src_ref=qkv.at[pl.ds(1, 2), :, pl.ds(pl.multiple_of(to * width, PAIR), width)],
            dst_ref=recv.at[pl.ds(1, 2), pl.ds(pl.multiple_of(h * rows, rows), rows), :],
            send_sem=kv_send.at[d], recv_sem=kv_recv.at[d],
            device_id=(s, to), device_id_type=MESH,
        )

    def q_copy(d):
        to = peer(d, 1)
        return pltpu.make_async_remote_copy(
            src_ref=qkv.at[pl.ds(0, 1), :, pl.ds(pl.multiple_of(to * width, PAIR), width)],
            dst_ref=recv.at[pl.ds(0, 1), pl.ds(pl.multiple_of(h * rows, rows), rows), :],
            send_sem=q_send.at[d], recv_sem=q_recv.at[d],
            device_id=(s, to), device_id_type=MESH,
        )

    def own_copy(first, count, sem):
        return pltpu.make_async_copy(
            qkv.at[pl.ds(first, count), :, pl.ds(pl.multiple_of(h * width, PAIR), width)],
            recv.at[pl.ds(first, count), pl.ds(pl.multiple_of(h * rows, rows), rows), :],
            sem,
        )

    own_copy(1, 2, kv_recv.at[0]).start()

    def start_kv(i, _):
        kv_copy(near_first(heads - i)).start()
        return 0

    def start_q(i, _):
        q_copy(near_first(heads - i)).start()
        return 0

    lax.fori_loop(1, heads, start_kv, 0)
    own_copy(0, 1, q_recv.at[0]).start()
    lax.fori_loop(1, heads, start_q, 0)

    row = lax.broadcasted_iota(jnp.int32, (PAIR, PAIR), 0)
    lane = lax.broadcasted_iota(jnp.int32, (PAIR, PAIR), 1)
    own = (row >= HD) == (lane >= HD)
    eye = jnp.where(row == lane, 1.0, 0.0).astype(F32)

    def grams(i, _):
        d = near_first(i)
        source = peer(d, -1)

        @pl.when(i == 0)
        def _():
            own_copy(1, 2, kv_recv.at[0]).wait()

        @pl.when(i > 0)
        def _():
            kv_copy(d).wait_recv()

        for sub in range(subs):
            at = pl.ds(pl.multiple_of(source * rows + sub * MB, MB), MB)
            b = source * subs + sub
            for p in range(pairs):
                lanes = slice(p * PAIR, (p + 1) * PAIR)
                keys = recv[1, at, lanes]
                values = recv[2, at, lanes]
                swapped = pltpu.roll(values.astype(F32), HD, 1).astype(BF)
                both = lax.dot_general(
                    keys, jnp.concatenate([keys, swapped], axis=1),
                    (((0,), (0,)), ((), ())), preferred_element_type=F32,
                )
                rate = jnp.where(row < HD, eta[2 * p], eta[2 * p + 1])
                high, low = split(jnp.where(own, rate * both[:, :PAIR], 0.0))
                a_ref[b, p, :, :PAIR] = high
                a_ref[b, p, :, PAIR:] = low
                b_ref[b, p] = jnp.where(own, 0.0, rate * both[:, PAIR:])
        return 0

    lax.fori_loop(0, heads, grams, 0)

    for way in range(2):
        b = 0 if way == 0 else batches - 1
        for p in range(pairs):
            a = a_ref[b, p, :, :PAIR].astype(F32) + a_ref[b, p, :, PAIR:].astype(F32)
            pre[way, b, p] = eye - a + b_ref[b, p]

    def advance(t, _):
        for p in range(pairs):
            for way in range(2):
                b = t if way == 0 else batches - 1 - t
                before = b - 1 if way == 0 else b + 1
                state = pre[way, before, p]
                high, low = split(state)
                a = a_ref[b, p]
                change = dot(
                    jnp.concatenate([a, a[:, :PAIR]], axis=1),
                    jnp.concatenate([high, high, low], axis=0),
                )
                pre[way, b, p] = state + b_ref[b, p] - change
        return 0

    lax.fori_loop(1, batches, advance, 0)

    for way in range(2):
        b = batches - 1 if way == 0 else 0
        for p in range(pairs):
            total = pre[way, b, p]
            totals[4 * p + way] = total[:HD]
            totals[4 * p + 2 + way] = total[HD:]

    shift = c * (seqs // 2)
    my_chain = (s + seqs - shift) % seqs
    is_owner = my_chain < chains

    def chain_at(k):
        return (k + shift) % seqs

    def tot_copy(k):
        return pltpu.make_async_remote_copy(
            src_ref=totals.at[k], dst_ref=inbox.at[s],
            send_sem=tot_send.at[k], recv_sem=tot_recv.at[s],
            device_id=(chain_at(k), h), device_id_type=MESH,
        )

    def tot_arrival(source):
        return pltpu.make_async_remote_copy(
            src_ref=totals.at[0], dst_ref=inbox.at[source],
            send_sem=tot_send.at[0], recv_sem=tot_recv.at[source],
            device_id=((s + 1) % seqs, h), device_id_type=MESH,
        )

    def send_total(d, _):
        k = (my_chain + d) % seqs

        @pl.when(k < chains)
        def _():
            tot_copy(k).start()

        return 0

    lax.fori_loop(1, seqs, send_total, 0)

    def fin_copy(k, to):
        return pltpu.make_async_remote_copy(
            src_ref=outbox.at[to], dst_ref=entry.at[k],
            send_sem=fin_send.at[to], recv_sem=fin_recv.at[k],
            device_id=(to, h), device_id_type=MESH,
        )

    def multiply_queries(i):
        source = i // subs
        b = i
        at = pl.ds(pl.multiple_of(b * MB, MB), MB)
        for p in range(pairs):
            query = recv[0, at, p * PAIR:(p + 1) * PAIR]
            ahead, behind = pre[0, b, p], pre[1, b, p]
            high, low = split(jnp.concatenate(
                [jnp.where(own, ahead, 0.0), jnp.where(own, behind, 0.0), jnp.where(own, 0.0, ahead + behind)],
                axis=1,
            ))
            product = dot(jnp.concatenate([query, query], axis=1), jnp.concatenate([high, low], axis=0))
            high, low = split(product[:, :2 * PAIR])
            q_high[p, at, :] = high
            q_low[p, at, :] = low
            r_ref[p, at, :] = product[:, 2 * PAIR:]

    own_copy(0, 1, q_recv.at[0]).wait()

    def wait_q(d, _):
        q_copy(d).wait_recv()
        return 0

    lax.fori_loop(1, heads, wait_q, 0)

    half_lane = lax.broadcasted_iota(jnp.int32, (HD, PAIR), 1)
    half_upper = half_lane >= HD

    @pl.when(is_owner)
    def _():
        inbox[s] = totals[my_chain]
        way = my_chain % 2
        number = my_chain // 2
        odd = number % 2
        mine = half_lane // HD != odd
        start = initial[number]
        state = jnp.where(mine, jnp.concatenate([start, start], axis=1), 0.0)

        def hop(t, state):
            at = jnp.where(way == 0, t, seqs - 1 - t)
            high, low = split(state)
            packed = (high.astype(F32) + pltpu.roll(low.astype(F32), HD, 1)).astype(BF)
            outbox[at] = packed

            @pl.when(at != s)
            def _():
                fin_copy(my_chain, at).start()

            @pl.when(at == s)
            def _():
                entry[my_chain] = packed

            @pl.when(at != s)
            def _():
                tot_arrival(at).wait_recv()

            total = inbox[at]
            linear_high, linear_low = split(jnp.where(mine, 0.0, total))
            change = dot(
                jnp.concatenate([linear_high, linear_low, linear_high], axis=1),
                jnp.concatenate([high, high, high, high, low, low], axis=0),
            )
            multiply_queries(t)
            return jnp.where(mine, total + change, 0.0)

        lax.fori_loop(0, seqs, hop, state)

    @pl.when(jnp.logical_not(is_owner))
    def _():
        def only(t, _):
            multiply_queries(t)
            return 0

        lax.fori_loop(0, batches, only, 0)

    def wait_entry(k, _):
        @pl.when(chain_at(k) != s)
        def _():
            fin_copy(k, (s + 1) % seqs).wait_recv()

        return 0

    lax.fori_loop(0, chains, wait_entry, 0)

    weights = []
    for p in range(pairs):
        highs, lows = [], []
        for way in range(2):
            for odd in range(2):
                packed = entry[4 * p + 2 * odd + way].astype(F32)
                mine = half_upper if odd == 0 else jnp.logical_not(half_upper)
                highs.append(jnp.where(mine, packed, 0.0).astype(BF))
                lows.append(jnp.where(mine, pltpu.roll(packed, HD, 1), 0.0).astype(BF))
        weights.append(jnp.concatenate([jnp.concatenate(highs, axis=0), jnp.concatenate(lows, axis=0)], axis=1))
    mean = jnp.where(own, 1.0 / HD, 0.0).astype(BF)
    mean = jnp.concatenate([mean, mean], axis=0)

    def nrm_copy(d):
        to = peer(d, 1)
        return pltpu.make_async_remote_copy(
            src_ref=normed.at[pl.ds(pl.multiple_of(to * rows, rows), rows), :],
            dst_ref=out.at[:, pl.ds(pl.multiple_of(h * width, PAIR), width)],
            send_sem=nrm_send.at[d], recv_sem=nrm_recv.at[d],
            device_id=(s, to), device_id_type=MESH,
        )

    own_normed = pltpu.make_async_copy(
        normed.at[pl.ds(pl.multiple_of(h * rows, rows), rows), :],
        out.at[:, pl.ds(pl.multiple_of(h * width, PAIR), width)],
        nrm_recv.at[0],
    )

    def read_rows(i, _):
        d = near_first(heads - 1 - i)
        to = peer(d, 1)
        at = pl.ds(pl.multiple_of(to * rows, rows), rows)
        for p in range(pairs):
            product = dot(jnp.concatenate([q_high[p, at, :], q_low[p, at, :]], axis=0), weights[p])
            read = product[:rows, :PAIR] + product[:rows, PAIR:] + product[rows:, :PAIR] + r_ref[p, at, :]
            high, low = split(read * read)
            mean_square = dot(jnp.concatenate([high, low], axis=1), mean)
            value = pltpu.roll(read * lax.rsqrt(mean_square + 1e-06), HD, 1)
            value = value * gain[:, p * PAIR:(p + 1) * PAIR]
            normed[at, p * PAIR:(p + 1) * PAIR] = value.astype(BF)

        @pl.when(i < heads - 1)
        def _():
            nrm_copy(d).start()

        return 0

    lax.fori_loop(0, heads, read_rows, 0)
    own_normed.start()

    def drain_head(d, _):
        nrm_copy(d).wait_recv()
        kv_copy(d).wait_send()
        q_copy(d).wait_send()
        nrm_copy(d).wait_send()
        return 0

    def drain_total(k, _):
        @pl.when(chain_at(k) != s)
        def _():
            tot_copy(k).wait_send()

        return 0

    lax.fori_loop(0, chains, drain_total, 0)

    @pl.when(is_owner)
    def _():
        def drain_fin(to, _):
            @pl.when(to != s)
            def _():
                fin_copy(my_chain, to).wait_send()

            return 0

        lax.fori_loop(0, seqs, drain_fin, 0)

    lax.fori_loop(1, heads, drain_head, 0)
    own_normed.wait()


def layer(qkv, eta, initial, gain, seqs, heads):
    rows = qkv.shape[1]
    width = gain.shape[1]
    pairs = width // PAIR
    tokens = rows * heads
    batches = tokens // MB
    vmem = pl.BlockSpec(memory_space=pltpu.VMEM)
    return pl.pallas_call(
        functools.partial(layer_kernel, seqs, heads, pairs),
        out_shape=jax.ShapeDtypeStruct((rows, heads * width), BF),
        in_specs=[
            pl.BlockSpec(memory_space=pl.ANY), pl.BlockSpec(memory_space=pltpu.SMEM), vmem, vmem,
        ],
        out_specs=vmem,
        scratch_shapes=[
            pltpu.VMEM((3, tokens, width), BF),
            pltpu.VMEM((batches, pairs, PAIR, 2 * PAIR), BF),
            pltpu.VMEM((batches, pairs, PAIR, PAIR), F32),
            pltpu.VMEM((2, batches, pairs, PAIR, PAIR), F32),
            pltpu.VMEM((4 * pairs, HD, PAIR), F32),
            pltpu.VMEM((seqs, HD, PAIR), F32),
            pltpu.VMEM((seqs, HD, PAIR), BF),
            pltpu.VMEM((4 * pairs, HD, PAIR), BF),
            pltpu.VMEM((pairs, tokens, 2 * PAIR), BF),
            pltpu.VMEM((pairs, tokens, 2 * PAIR), BF),
            pltpu.VMEM((pairs, tokens, PAIR), F32),
            pltpu.VMEM((tokens, width), BF),
            pltpu.SemaphoreType.DMA((heads,)), pltpu.SemaphoreType.DMA((heads,)),
            pltpu.SemaphoreType.DMA((heads,)), pltpu.SemaphoreType.DMA((heads,)),
            pltpu.SemaphoreType.DMA((4 * pairs,)), pltpu.SemaphoreType.DMA((seqs,)),
            pltpu.SemaphoreType.DMA((seqs,)), pltpu.SemaphoreType.DMA((4 * pairs,)),
            pltpu.SemaphoreType.DMA((heads,)), pltpu.SemaphoreType.DMA((heads,)),
        ],
        compiler_params=pltpu.CompilerParams(
            collective_id=0, has_side_effects=True, vmem_limit_bytes=40 << 20
        ),
        cost_estimate=pl.CostEstimate(flops=2 << 30, bytes_accessed=200 << 20, transcendentals=0),
    )(qkv, eta, initial, gain)


def solution(mesh):
    seqs, heads = mesh.shape["seq"], mesh.shape["head"]

    def shards(qkv, eta, initial, gain, w_out):
        whole = lax.all_gather(w_out, "head", axis=0, tiled=True)
        normed = layer(jnp.transpose(qkv, (1, 0, 2)), eta, initial, gain[None, :], seqs, heads)
        return jnp.dot(normed, whole, preferred_element_type=F32)

    return jax.shard_map(
        shards,
        mesh=mesh,
        in_specs=(
            P(("seq", "head"), None, None),
            P("head"),
            P("head", None, None),
            P("head"),
            P("head", None),
        ),
        out_specs=P(("seq", "head"), None),
        check_vma=False,
    )
```

```python
import functools

import jax
import jax.numpy as jnp
from jax import lax
from jax.experimental import pallas as pl
from jax.experimental.pallas import tpu as pltpu
from jax.sharding import PartitionSpec as P

MESH = pl.DeviceIdType.MESH
MB = 64
HD = 64
PAIR = 2 * HD
BF = jnp.bfloat16
F32 = jnp.float32


def split(x):
    high = x.astype(BF)
    return high, (x - high.astype(F32)).astype(BF)


def dot(a, b):
    return lax.dot_general(a, b, (((1,), (0,)), ((), ())), preferred_element_type=F32)


def triple(high, low, axis):
    parts = [high, low, high] if axis == 1 else [high, high, low]
    return jnp.concatenate(parts, axis=axis)


def layer_kernel(
    seqs, heads, pairs,
    qkv, eta_hbm, initial_hbm, gain_hbm, w_hbm, out,
    eta, initial, gain, recv, a_ref, b_ref, pre, group, totals, inbox, outbox, entry,
    q_high, q_low, r_ref, normed, normed_in, whole,
    const_sem, own_sem, kv_send, kv_recv, q_send, q_recv, tot_send, tot_recv, fin_send, fin_recv, nrm_send, nrm_recv,
    wx_send, wx_recv, w1_send, w1_recv, w2_send, w2_recv, w3_send, w3_recv, sib_send, sib_recv,
):
    s = lax.axis_index("seq")
    h = lax.axis_index("head")
    x, c = h // 2, h % 2
    xs = heads // 2
    side = 4
    z, y = s // side, s % side
    rows = qkv.shape[1]
    width = pairs * PAIR
    chip_rows = 2 * rows
    group_batches = chip_rows // MB
    chains = 4 * pairs

    barrier = pltpu.get_barrier_semaphore()

    def greet_head(d, _):
        pl.semaphore_signal(barrier, inc=1, device_id=(s, (h + d) % heads), device_id_type=MESH)
        return 0

    def greet_seq(d, _):
        pl.semaphore_signal(barrier, inc=1, device_id=((s + d) % seqs, h), device_id_type=MESH)
        return 0

    lax.fori_loop(1, heads, greet_head, 0)
    lax.fori_loop(1, seqs, greet_seq, 0)

    constants = [
        pltpu.make_async_copy(eta_hbm, eta, const_sem.at[0]),
        pltpu.make_async_copy(initial_hbm, initial, const_sem.at[1]),
        pltpu.make_async_copy(gain_hbm, gain, const_sem.at[2]),
    ]
    for copy in constants:
        copy.start()

    def own_copy(first, count, sem):
        return pltpu.make_async_copy(
            qkv.at[pl.ds(first, count), :, pl.ds(pl.multiple_of(h * width, PAIR), width)],
            recv.at[pl.ds(first, count), pl.ds(pl.multiple_of(h * rows, rows), rows), :],
            sem,
        )

    own_kv = own_copy(1, 2, own_sem.at[0])
    own_q = own_copy(0, 1, own_sem.at[1])
    own_kv.start()
    own_q.start()
    base = c * width
    own_w = pltpu.make_async_copy(w_hbm, whole.at[0, pl.ds(pl.multiple_of(base, PAIR), width), :], own_sem.at[2])
    own_w.start()
    pl.semaphore_wait(barrier, heads + seqs - 2)

    def peer(d, sign):
        dx, dc = d // 2, d % 2
        return ((x + sign * dx + xs) % xs) * 2 + (c + dc) % 2

    half = width // 2
    step = half // side
    cols = w_hbm.shape[1] // side

    def piece(part, first, last, second):
        at = part * half + last * step
        return pl.ds(pl.multiple_of(first + at, 16), step), pl.ds(pl.multiple_of(second * cols, PAIR), cols)

    def wx_copy(part, i):
        last, second = (z, y) if part == 0 else (y, z)
        from_rows, at_cols = piece(part, 0, last, second)
        to_rows, _ = piece(part, base, last, second)
        return pltpu.make_async_remote_copy(
            src_ref=w_hbm.at[from_rows, at_cols],
            dst_ref=whole.at[i, to_rows, at_cols],
            send_sem=wx_send.at[part, i], recv_sem=wx_recv.at[part, i],
            device_id=(s, ((x + xs - i) % xs) * 2 + c), device_id_type=MESH,
        )

    def along(axis, d):
        return (z * side + (y + d) % side, h) if axis == 0 else (((z + d) % side) * side + y, h)

    def w1_copy(part, d):
        last, second = (z, y) if part == 0 else (y, z)
        at_rows, at_cols = piece(part, base, last, second)
        where = whole.at[pl.ds(1, xs - 1), at_rows, at_cols]
        return pltpu.make_async_remote_copy(
            src_ref=where, dst_ref=where,
            send_sem=w1_send.at[part, d], recv_sem=w1_recv.at[part, d],
            device_id=along(part, d), device_id_type=MESH,
        )

    def band(part, d):
        last = z if part == 0 else y
        at_rows, _ = piece(part, base, (last + side - d) % side, 0)
        return whole.at[pl.ds(1, xs - 1), at_rows, :]

    def w2_copy(part, d):
        return pltpu.make_async_remote_copy(
            src_ref=band(part, 0), dst_ref=band(part, 0),
            send_sem=w2_send.at[part, d], recv_sem=w2_recv.at[part, d],
            device_id=along(1 - part, d), device_id_type=MESH,
        )

    def w3_copy(part, d):
        at_cols = pl.ds(0 if d == 1 else 2 * cols, 2 * cols)
        last = z if part == 0 else y
        at_rows, _ = piece(part, base, (last + side - d) % side, 0)
        where = whole.at[pl.ds(1, xs - 1), at_rows, at_cols]
        return pltpu.make_async_remote_copy(
            src_ref=where, dst_ref=where,
            send_sem=w3_send.at[part, d], recv_sem=w3_recv.at[part, d],
            device_id=along(1 - part, d), device_id_type=MESH,
        )

    sibling = (s, x * 2 + 1 - c)

    def sibling_band(part, d):
        return pltpu.make_async_remote_copy(
            src_ref=band(part, d), dst_ref=band(part, d),
            send_sem=sib_send.at[part, d], recv_sem=sib_recv.at[part, d],
            device_id=sibling, device_id_type=MESH,
        )

    sibling_own = pltpu.make_async_remote_copy(
        src_ref=w_hbm, dst_ref=whole.at[0, pl.ds(pl.multiple_of(base, PAIR), width), :],
        send_sem=sib_send.at[2, 0], recv_sem=sib_recv.at[2, 0],
        device_id=sibling, device_id_type=MESH,
    )

    def kv_copy(d):
        to = peer(d, 1)
        return pltpu.make_async_remote_copy(
            src_ref=qkv.at[pl.ds(1, 2), :, pl.ds(pl.multiple_of(to * width, PAIR), width)],
            dst_ref=recv.at[pl.ds(1, 2), pl.ds(pl.multiple_of(h * rows, rows), rows), :],
            send_sem=kv_send.at[d], recv_sem=kv_recv.at[d],
            device_id=(s, to), device_id_type=MESH,
        )

    def q_copy(d):
        to = peer(d, 1)
        return pltpu.make_async_remote_copy(
            src_ref=qkv.at[pl.ds(0, 1), :, pl.ds(pl.multiple_of(to * width, PAIR), width)],
            dst_ref=recv.at[pl.ds(0, 1), pl.ds(pl.multiple_of(h * rows, rows), rows), :],
            send_sem=q_send.at[d], recv_sem=q_recv.at[d],
            device_id=(s, to), device_id_type=MESH,
        )

    def loop(first, last, act):
        def run(i, _):
            act(i)
            return 0

        lax.fori_loop(first, last, run, 0)

    hops = [0, 1, 3, 2]

    kv_copy(1).start()
    for part in range(2):
        for i in hops[1:]:
            wx_copy(part, i).start()
    for dx in (2, 1, 3):
        kv_copy(2 * dx).start()
        kv_copy(2 * dx + 1).start()
    q_copy(1).start()
    for dx in (2, 1, 3):
        q_copy(2 * dx).start()
        q_copy(2 * dx + 1).start()
    sibling_own.start()

    row = lax.broadcasted_iota(jnp.int32, (PAIR, PAIR), 0)
    lane = lax.broadcasted_iota(jnp.int32, (PAIR, PAIR), 1)
    own = (row >= HD) == (lane >= HD)
    eye = jnp.where(row == lane, 1.0, 0.0).astype(F32)

    for copy in constants:
        copy.wait()

    def chip_maps(dx):
        at_x = (x + xs - dx) % xs

        def grams(i):
            at = pl.ds(pl.multiple_of(at_x * chip_rows + i * MB, MB), MB)
            for p in range(pairs):
                lanes = slice(p * PAIR, (p + 1) * PAIR)
                keys = recv[1, at, lanes]
                values = recv[2, at, lanes]
                swapped = pltpu.roll(values.astype(F32), HD, 1).astype(BF)
                both = lax.dot_general(
                    keys, jnp.concatenate([keys, swapped], axis=1),
                    (((0,), (0,)), ((), ())), preferred_element_type=F32,
                )
                rate = jnp.where(row < HD, eta[2 * p], eta[2 * p + 1])
                linear = jnp.where(own, rate * both[:, :PAIR], 0.0)
                offset = jnp.where(own, 0.0, rate * both[:, PAIR:])
                high, low = split(linear)
                a_ref[i, p, :, :PAIR] = high
                a_ref[i, p, :, PAIR:] = low
                b_ref[i, p] = offset
                first = eye - linear + offset

                @pl.when(i == 0)
                def _():
                    pre[0, at_x * group_batches, p] = first

                @pl.when(i == group_batches - 1)
                def _():
                    pre[1, at_x * group_batches + i, p] = first

        loop(0, group_batches, grams)

        def advance(t):
            for p in range(pairs):
                for way in range(2):
                    i = t if way == 0 else group_batches - 1 - t
                    before = i - 1 if way == 0 else i + 1
                    state = pre[way, at_x * group_batches + before, p]
                    high, low = split(state)
                    a = a_ref[i, p]
                    change = dot(jnp.concatenate([a, a[:, :PAIR]], axis=1), triple(high, low, 0))
                    pre[way, at_x * group_batches + i, p] = state + b_ref[i, p] - change

        loop(1, group_batches, advance)

    own_kv.wait()
    kv_copy(1).wait_recv()
    chip_maps(0)

    for part in range(2):
        for i in hops[1:]:
            wx_copy(part, i).wait_recv()
    for part in range(2):
        for d in (2, 1, 3):
            w1_copy(part, d).start()

    for dx in (1, 3):
        kv_copy(2 * dx).wait_recv()
        kv_copy(2 * dx + 1).wait_recv()
        chip_maps(dx)

    for part in range(2):
        for d in (1, 2, 3):
            w1_copy(part, d).wait_recv()
    for part in range(2):
        for d in (1, 3):
            w2_copy(part, d).start()
    for part in range(2):
        sibling_band(part, 0).start()

    kv_copy(4).wait_recv()
    kv_copy(5).wait_recv()
    chip_maps(2)

    def linear_of(total):
        return triple(*split(jnp.where(own, total, 0.0)), 1)

    for p in range(pairs):
        group[0, 0, p] = pre[0, group_batches - 1, p]
        group[1, xs - 1, p] = pre[1, (xs - 1) * group_batches, p]

    def advance_chip(t):
        for p in range(pairs):
            for way in range(2):
                g = t if way == 0 else xs - 1 - t
                before = g - 1 if way == 0 else g + 1
                b = (g + 1) * group_batches - 1 if way == 0 else g * group_batches
                total = pre[way, b, p]
                change = dot(linear_of(total), triple(*split(group[way, before, p]), 0))
                group[way, g, p] = jnp.where(own, 0.0, total) + change

    loop(1, xs, advance_chip)

    for way in range(2):
        for p in range(pairs):
            total = group[way, xs - 1 if way == 0 else 0, p]
            totals[4 * p + way] = total[:HD]
            totals[4 * p + 2 + way] = total[HD:]

    shift = c * (seqs // 2)
    my_chain = (s + seqs - shift) % seqs
    is_owner = my_chain < chains

    def chain_at(k):
        return (k + shift) % seqs

    def tot_copy(k):
        return pltpu.make_async_remote_copy(
            src_ref=totals.at[k], dst_ref=inbox.at[s],
            send_sem=tot_send.at[k], recv_sem=tot_recv.at[s],
            device_id=(chain_at(k), h), device_id_type=MESH,
        )

    def tot_arrival(source):
        return pltpu.make_async_remote_copy(
            src_ref=totals.at[0], dst_ref=inbox.at[source],
            send_sem=tot_send.at[0], recv_sem=tot_recv.at[source],
            device_id=((s + 1) % seqs, h), device_id_type=MESH,
        )

    def send_total(d):
        k = (my_chain + d) % seqs

        @pl.when(k < chains)
        def _():
            tot_copy(k).start()

    loop(1, seqs, send_total)

    def fin_copy(k, to):
        return pltpu.make_async_remote_copy(
            src_ref=outbox.at[to], dst_ref=entry.at[k],
            send_sem=fin_send.at[to], recv_sem=fin_recv.at[k],
            device_id=(to, h), device_id_type=MESH,
        )

    def multiply_queries(dx):
        at_x = (x + xs - dx) % xs

        def one(i):
            b = at_x * group_batches + i
            at = pl.ds(pl.multiple_of(b * MB, MB), MB)
            for p in range(pairs):
                query = recv[0, at, p * PAIR:(p + 1) * PAIR]
                ahead, behind = pre[0, b, p], pre[1, b, p]
                high, low = split(jnp.concatenate(
                    [jnp.where(own, ahead, 0.0), jnp.where(own, behind, 0.0), jnp.where(own, 0.0, ahead + behind)],
                    axis=1,
                ))
                product = dot(jnp.concatenate([query, query], axis=1), jnp.concatenate([high, low], axis=0))
                high, low = split(product[:, :2 * PAIR])
                q_high[p, at, :] = high
                q_low[p, at, :] = low
                r_ref[p, at, :] = product[:, 2 * PAIR:]

        loop(0, group_batches, one)

    own_q.wait()
    q_copy(1).wait_recv()
    multiply_queries(0)
    for dx in (1, 3):
        q_copy(2 * dx).wait_recv()
        q_copy(2 * dx + 1).wait_recv()
        multiply_queries(dx)

    @pl.when(is_owner)
    def _():
        inbox[s] = totals[my_chain]
        way = my_chain % 2
        number = my_chain // 2
        odd = number % 2
        half_lane = lax.broadcasted_iota(jnp.int32, (HD, PAIR), 1)
        mine = half_lane // HD != odd
        start = initial[number]

        def place(t):
            return jnp.where(way == 0, t, seqs - 1 - t)

        def arrive(source):
            @pl.when(source != s)
            def _():
                tot_arrival(source).wait_recv()

        loop(0, seqs, arrive)

        def apply(total, high, low):
            linear_high, linear_low = split(jnp.where(mine, 0.0, total))
            return jnp.where(mine, total, 0.0) + dot(
                triple(linear_high, linear_low, 1),
                jnp.concatenate([high, high, high, high, low, low], axis=0),
            )

        def emit(t, state):
            at = place(t)
            high, low = split(state)
            packed = (high.astype(F32) + pltpu.roll(low.astype(F32), HD, 1)).astype(BF)
            outbox[at] = packed

            @pl.when(at != s)
            def _():
                fin_copy(my_chain, at).start()

            @pl.when(at == s)
            def _():
                entry[my_chain] = packed

        quads = seqs // side
        maps = [[None] * side for _ in range(quads)]
        for j in range(side):
            for g in range(quads):
                total = inbox[place(g * side + j)]
                maps[g][j] = total if j == 0 else apply(total, *split(maps[g][j - 1]))
        state = jnp.where(mine, jnp.concatenate([start, start], axis=1), 0.0)
        states = [state]
        for g in range(quads - 1):
            states.append(jnp.where(mine, apply(maps[g][side - 1], *split(states[-1])), 0.0))
        for g in range(quads):
            emit(g * side, states[g])
            parts = split(states[g])
            for j in range(side - 1):
                emit(g * side + j + 1, jnp.where(mine, apply(maps[g][j], *parts), 0.0))

    q_copy(4).wait_recv()
    q_copy(5).wait_recv()
    multiply_queries(2)

    def wait_entry(k):
        @pl.when(chain_at(k) != s)
        def _():
            fin_copy(k, (s + 1) % seqs).wait_recv()

    loop(0, chains, wait_entry)

    half_upper = lax.broadcasted_iota(jnp.int32, (HD, PAIR), 1) >= HD
    mean = jnp.where(own, 1.0 / HD, 0.0).astype(BF)
    mean = jnp.concatenate([mean, mean], axis=0)
    entered = []
    for p in range(pairs):
        ways = []
        for way in range(2):
            highs, lows = [], []
            for odd in range(2):
                packed = entry[4 * p + 2 * odd + way].astype(F32)
                mine = half_upper if odd == 0 else jnp.logical_not(half_upper)
                highs.append(jnp.where(mine, packed, 0.0).astype(BF))
                lows.append(jnp.where(mine, pltpu.roll(packed, HD, 1), 0.0).astype(BF))
            ways.append((jnp.concatenate(highs, axis=0), jnp.concatenate(lows, axis=0)))
        entered.append(ways)

    def nrm_copy(d):
        to = peer(d, 1)
        return pltpu.make_async_remote_copy(
            src_ref=normed.at[pl.ds(pl.multiple_of(to * rows, rows), rows), :],
            dst_ref=normed_in.at[(xs - d // 2) % xs, :, pl.ds(pl.multiple_of(c * width, PAIR), width)],
            send_sem=nrm_send.at[d], recv_sem=nrm_recv.at[d],
            device_id=(s, to), device_id_type=MESH,
        )

    own_normed = pltpu.make_async_copy(
        normed.at[pl.ds(pl.multiple_of(h * rows, rows), rows), :],
        normed_in.at[0, :, pl.ds(pl.multiple_of(c * width, PAIR), width)],
        own_sem.at[3],
    )

    def read_chip(dx):
        at_x = (x + dx) % xs
        at = pl.ds(pl.multiple_of(at_x * chip_rows, chip_rows), chip_rows)
        for p in range(pairs):
            highs, lows = [], []
            for way in range(2):
                high, low = entered[p][way]
                before = (at_x + xs - 1) % xs if way == 0 else (at_x + 1) % xs
                total = group[way, before, p]
                moved = jnp.where(own, 0.0, total) + dot(linear_of(total), triple(high, low, 0))
                edge = at_x == (0 if way == 0 else xs - 1)
                moved_high, moved_low = split(jnp.where(own, 0.0, moved))
                highs.append(jnp.where(edge, high, moved_high))
                lows.append(jnp.where(edge, low, moved_low))
            weight = jnp.concatenate([jnp.concatenate(highs, axis=0), jnp.concatenate(lows, axis=0)], axis=1)
            product = dot(q_high[p, at, :], weight)
            read = product[:, :PAIR] + product[:, PAIR:] + dot(q_low[p, at, :], weight[:, :PAIR]) + r_ref[p, at, :]
            high, low = split(read * read)
            mean_square = dot(jnp.concatenate([high, low], axis=1), mean)
            value = pltpu.roll(read * lax.rsqrt(mean_square + 1e-06), HD, 1)
            value = value * gain[:, p * PAIR:(p + 1) * PAIR]
            normed[at, p * PAIR:(p + 1) * PAIR] = value.astype(BF)

    for dx in (2, 1, 3, 0):
        read_chip(dx)
        if dx:
            nrm_copy(2 * dx).start()
        else:
            own_normed.start()
        nrm_copy(2 * dx + 1).start()

    for part in range(2):
        for d in (1, 3):
            w2_copy(part, d).wait_recv()
            w3_copy(part, d).start()
            sibling_band(part, d).start()
    for part in range(2):
        for d in (1, 3):
            w3_copy(part, d).wait_recv()
        sibling_band(part, 2).start()

    own_w.wait()
    sibling_own.wait_recv()
    own_normed.wait()
    for d in range(1, heads):
        nrm_copy(d).wait_recv()

    def sibling_arrival(part, d):
        last = z if part == 0 else y
        at_rows, _ = piece(part, width - base, (last + side - d) % side, 0)
        where = whole.at[pl.ds(1, xs - 1), at_rows, :]
        return pltpu.make_async_remote_copy(
            src_ref=where, dst_ref=where,
            send_sem=sib_send.at[part, d], recv_sem=sib_recv.at[part, d],
            device_id=sibling, device_id_type=MESH,
        )

    for part in range(2):
        for d in range(side):
            sibling_arrival(part, d).wait_recv()

    tile = 512

    def project(j):
        at = pl.ds(pl.multiple_of(j * tile, tile), tile)
        total = dot(normed_in[0], whole[0, :, at])
        for i in range(1, xs):
            total = total + dot(normed_in[i], whole[i, :, at])
        out[:, at] = total

    loop(0, w_hbm.shape[1] // tile, project)

    for part in range(2):
        for i in range(1, xs):
            wx_copy(part, i).wait_send()
            w1_copy(part, i).wait_send()
        for d in (1, 3):
            w2_copy(part, d).wait_send()
            w3_copy(part, d).wait_send()
        for d in range(side):
            sibling_band(part, d).wait_send()
    sibling_own.wait_send()

    def drain_head(d):
        kv_copy(d).wait_send()
        q_copy(d).wait_send()
        nrm_copy(d).wait_send()

    def drain_total(k):
        @pl.when(chain_at(k) != s)
        def _():
            tot_copy(k).wait_send()

    loop(1, heads, drain_head)
    loop(0, chains, drain_total)

    @pl.when(is_owner)
    def _():
        def drain_fin(to):
            @pl.when(to != s)
            def _():
                fin_copy(my_chain, to).wait_send()

        loop(0, seqs, drain_fin)


def layer(qkv, eta, initial, gain, w_out, seqs, heads):
    rows = qkv.shape[1]
    width, columns = w_out.shape
    pairs = width // PAIR
    tokens = rows * heads
    batches = tokens // MB
    xs = heads // 2
    anywhere = pl.BlockSpec(memory_space=pl.ANY)
    dma = pltpu.SemaphoreType.DMA
    return pl.pallas_call(
        functools.partial(layer_kernel, seqs, heads, pairs),
        out_shape=jax.ShapeDtypeStruct((rows, columns), F32),
        in_specs=[anywhere] * 5,
        out_specs=pl.BlockSpec(memory_space=pltpu.VMEM),
        scratch_shapes=[
            pltpu.SMEM(eta.shape, F32),
            pltpu.VMEM(initial.shape, F32),
            pltpu.VMEM(gain.shape, F32),
            pltpu.VMEM((3, tokens, width), BF),
            pltpu.VMEM((batches // xs, pairs, PAIR, 2 * PAIR), BF),
            pltpu.VMEM((batches // xs, pairs, PAIR, PAIR), F32),
            pltpu.VMEM((2, batches, pairs, PAIR, PAIR), F32),
            pltpu.VMEM((2, xs, pairs, PAIR, PAIR), F32),
            pltpu.VMEM((4 * pairs, HD, PAIR), F32),
            pltpu.VMEM((seqs, HD, PAIR), F32),
            pltpu.VMEM((seqs, HD, PAIR), BF),
            pltpu.VMEM((4 * pairs, HD, PAIR), BF),
            pltpu.VMEM((pairs, tokens, 2 * PAIR), BF),
            pltpu.VMEM((pairs, tokens, 2 * PAIR), BF),
            pltpu.VMEM((pairs, tokens, PAIR), F32),
            pltpu.VMEM((tokens, width), BF),
            pltpu.VMEM((xs, rows, 2 * width), BF),
            pltpu.VMEM((xs, 2 * width, columns), BF),
            dma((3,)), dma((4,)),
            dma((heads,)), dma((heads,)), dma((heads,)), dma((heads,)),
            dma((4 * pairs,)), dma((seqs,)), dma((seqs,)), dma((4 * pairs,)),
            dma((heads,)), dma((heads,)),
            dma((2, 4)), dma((2, 4)), dma((2, 4)), dma((2, 4)), dma((2, 4)), dma((2, 4)),
            dma((2, 4)), dma((2, 4)), dma((3, 4)), dma((3, 4)),
        ],
        compiler_params=pltpu.CompilerParams(
            collective_id=0, has_side_effects=True, vmem_limit_bytes=57 << 20
        ),
    )(qkv, eta, initial, gain, w_out)


def solution(mesh):
    seqs, heads = mesh.shape["seq"], mesh.shape["head"]

    def shards(qkv, eta, initial, gain, w_out):
        return layer(jnp.transpose(qkv, (1, 0, 2)), eta, initial, gain[None, :], w_out, seqs, heads)

    return jax.shard_map(
        shards,
        mesh=mesh,
        in_specs=(
            P(("seq", "head"), None, None),
            P("head"),
            P("head", None, None),
            P("head"),
            P("head", None),
        ),
        out_specs=P(("seq", "head"), None),
        check_vma=False,
    )
```

```python
import functools

import jax
import jax.numpy as jnp
from jax import lax
from jax.experimental import pallas as pl
from jax.experimental.pallas import tpu as pltpu
from jax.sharding import PartitionSpec as P

MESH = pl.DeviceIdType.MESH
MB = 64
HD = 64
PAIR = 2 * HD
BF = jnp.bfloat16
F32 = jnp.float32


def split(x):
    high = x.astype(BF)
    return high, (x - high.astype(F32)).astype(BF)


def dot(a, b):
    return lax.dot_general(a, b, (((1,), (0,)), ((), ())), preferred_element_type=F32)


def triple(high, low, axis):
    parts = [high, low, high] if axis == 1 else [high, high, low]
    return jnp.concatenate(parts, axis=axis)


def layer_kernel(
    seqs, heads, pairs,
    qkv, eta_hbm, initial_hbm, gain_hbm, w_hbm, out,
    eta, initial, gain, recv, a_ref, b_ref, pre, group, totals, inbox, outbox, entry,
    q_high, q_low, r_ref, normed, normed_in, whole,
    const_sem, own_sem, kv_send, kv_recv, q_send, q_recv, tot_send, tot_recv, fin_send, fin_recv, nrm_send, nrm_recv,
    wx_send, wx_recv, w1_send, w1_recv, w2_send, w2_recv, w3_send, w3_recv, sib_send, sib_recv,
):
    s = lax.axis_index("seq")
    h = lax.axis_index("head")
    x, c = h // 2, h % 2
    xs = heads // 2
    side = 4
    z, y = s // side, s % side
    rows = qkv.shape[1]
    width = pairs * PAIR
    chip_rows = 2 * rows
    group_batches = chip_rows // MB
    chains = 4 * pairs

    barrier = pltpu.get_barrier_semaphore()

    def greet_head(d, _):
        pl.semaphore_signal(barrier, inc=1, device_id=(s, (h + d) % heads), device_id_type=MESH)
        return 0

    def greet_seq(d, _):
        pl.semaphore_signal(barrier, inc=1, device_id=((s + d) % seqs, h), device_id_type=MESH)
        return 0

    lax.fori_loop(1, heads, greet_head, 0)
    lax.fori_loop(1, seqs, greet_seq, 0)

    constants = [
        pltpu.make_async_copy(eta_hbm, eta, const_sem.at[0]),
        pltpu.make_async_copy(initial_hbm, initial, const_sem.at[1]),
        pltpu.make_async_copy(gain_hbm, gain, const_sem.at[2]),
    ]
    for copy in constants:
        copy.start()

    def own_copy(first, count, sem):
        return pltpu.make_async_copy(
            qkv.at[pl.ds(first, count), :, pl.ds(pl.multiple_of(h * width, PAIR), width)],
            recv.at[pl.ds(first, count), pl.ds(pl.multiple_of(h * rows, rows), rows), :],
            sem,
        )

    own_kv = own_copy(1, 2, own_sem.at[0])
    own_q = own_copy(0, 1, own_sem.at[1])
    own_kv.start()
    own_q.start()
    base = c * width
    own_w = pltpu.make_async_copy(w_hbm, whole.at[0, pl.ds(pl.multiple_of(base, PAIR), width), :], own_sem.at[2])
    own_w.start()
    pl.semaphore_wait(barrier, heads + seqs - 2)

    def peer(d, sign):
        dx, dc = d // 2, d % 2
        return ((x + sign * dx + xs) % xs) * 2 + (c + dc) % 2

    half = width // 2
    step = half // side
    cols = w_hbm.shape[1] // side

    def piece(part, first, last, second):
        at = part * half + last * step
        return pl.ds(pl.multiple_of(first + at, 16), step), pl.ds(pl.multiple_of(second * cols, PAIR), cols)

    def wx_copy(part, i):
        last, second = (z, y) if part == 0 else (y, z)
        from_rows, at_cols = piece(part, 0, last, second)
        to_rows, _ = piece(part, base, last, second)
        return pltpu.make_async_remote_copy(
            src_ref=w_hbm.at[from_rows, at_cols],
            dst_ref=whole.at[i, to_rows, at_cols],
            send_sem=wx_send.at[part, i], recv_sem=wx_recv.at[part, i],
            device_id=(s, ((x + xs - i) % xs) * 2 + c), device_id_type=MESH,
        )

    def along(axis, d):
        return (z * side + (y + d) % side, h) if axis == 0 else (((z + d) % side) * side + y, h)

    def w1_copy(part, d):
        last, second = (z, y) if part == 0 else (y, z)
        at_rows, at_cols = piece(part, base, last, second)
        where = whole.at[pl.ds(1, xs - 1), at_rows, at_cols]
        return pltpu.make_async_remote_copy(
            src_ref=where, dst_ref=where,
            send_sem=w1_send.at[part, d], recv_sem=w1_recv.at[part, d],
            device_id=along(part, d), device_id_type=MESH,
        )

    def band(part, d):
        last = z if part == 0 else y
        at_rows, _ = piece(part, base, (last + side - d) % side, 0)
        return whole.at[pl.ds(1, xs - 1), at_rows, :]

    def w2_copy(part, d):
        return pltpu.make_async_remote_copy(
            src_ref=band(part, 0), dst_ref=band(part, 0),
            send_sem=w2_send.at[part, d], recv_sem=w2_recv.at[part, d],
            device_id=along(1 - part, d), device_id_type=MESH,
        )

    def w3_copy(part, d):
        at_cols = pl.ds(0 if d == 1 else 2 * cols, 2 * cols)
        last = z if part == 0 else y
        at_rows, _ = piece(part, base, (last + side - d) % side, 0)
        where = whole.at[pl.ds(1, xs - 1), at_rows, at_cols]
        return pltpu.make_async_remote_copy(
            src_ref=where, dst_ref=where,
            send_sem=w3_send.at[part, d], recv_sem=w3_recv.at[part, d],
            device_id=along(1 - part, d), device_id_type=MESH,
        )

    sibling = (s, x * 2 + 1 - c)

    def sibling_band(part, d):
        return pltpu.make_async_remote_copy(
            src_ref=band(part, d), dst_ref=band(part, d),
            send_sem=sib_send.at[part, d], recv_sem=sib_recv.at[part, d],
            device_id=sibling, device_id_type=MESH,
        )

    sibling_own = pltpu.make_async_remote_copy(
        src_ref=w_hbm, dst_ref=whole.at[0, pl.ds(pl.multiple_of(base, PAIR), width), :],
        send_sem=sib_send.at[2, 0], recv_sem=sib_recv.at[2, 0],
        device_id=sibling, device_id_type=MESH,
    )

    def kv_copy(d):
        to = peer(d, 1)
        return pltpu.make_async_remote_copy(
            src_ref=qkv.at[pl.ds(1, 2), :, pl.ds(pl.multiple_of(to * width, PAIR), width)],
            dst_ref=recv.at[pl.ds(1, 2), pl.ds(pl.multiple_of(h * rows, rows), rows), :],
            send_sem=kv_send.at[d], recv_sem=kv_recv.at[d],
            device_id=(s, to), device_id_type=MESH,
        )

    def q_copy(d):
        to = peer(d, 1)
        return pltpu.make_async_remote_copy(
            src_ref=qkv.at[pl.ds(0, 1), :, pl.ds(pl.multiple_of(to * width, PAIR), width)],
            dst_ref=recv.at[pl.ds(0, 1), pl.ds(pl.multiple_of(h * rows, rows), rows), :],
            send_sem=q_send.at[d], recv_sem=q_recv.at[d],
            device_id=(s, to), device_id_type=MESH,
        )

    def loop(first, last, act):
        def run(i, _):
            act(i)
            return 0

        lax.fori_loop(first, last, run, 0)

    kv_copy(1).start()
    for part in range(2):
        for i in (1, 3, 2):
            wx_copy(part, i).start()
    for d in (2, 3, 6, 7):
        kv_copy(d).start()
    q_copy(1).start()

    def near(i):
        return jnp.where(i < 2, i, xs + 1 - i)

    row = lax.broadcasted_iota(jnp.int32, (PAIR, PAIR), 0)
    lane = lax.broadcasted_iota(jnp.int32, (PAIR, PAIR), 1)
    own = (row >= HD) == (lane >= HD)
    eye = jnp.where(row == lane, 1.0, 0.0).astype(F32)

    for copy in constants:
        copy.wait()

    own_kv.wait()
    rates = [jnp.where(row < HD, eta[2 * p], eta[2 * p + 1]) for p in range(pairs)]

    def chip_maps(n):
        dx = near(n)
        at_x = (x + xs - dx) % xs

        @pl.when(n > 0)
        def _():
            kv_copy(2 * dx).wait_recv()

        kv_copy(2 * dx + 1).wait_recv()

        @pl.when(n == xs - 1)
        def _():
            for d in range(2, heads):
                q_copy(d).start()

        first = {}
        for i in range(group_batches):
            at = pl.ds(pl.multiple_of(at_x * chip_rows + i * MB, MB), MB)
            for p in range(pairs):
                lanes = slice(p * PAIR, (p + 1) * PAIR)
                keys = recv[1, at, lanes]
                values = recv[2, at, lanes]
                swapped = pltpu.roll(values.astype(F32), HD, 1).astype(BF)
                both = lax.dot_general(
                    keys, jnp.concatenate([keys, swapped], axis=1),
                    (((0,), (0,)), ((), ())), preferred_element_type=F32,
                )
                linear = jnp.where(own, rates[p] * both[:, :PAIR], 0.0)
                offset = jnp.where(own, 0.0, rates[p] * both[:, PAIR:])
                high, low = split(linear)
                a_ref[i, p, :, :PAIR] = high
                a_ref[i, p, :, PAIR:] = low
                b_ref[i, p] = offset
                if i in (0, group_batches - 1):
                    first[i, p] = eye - linear + offset
        base_batch = at_x * group_batches
        states = {}
        for p in range(pairs):
            for way in range(2):
                i = 0 if way == 0 else group_batches - 1
                states[way, p] = first[i, p]
                pre[way, base_batch + i, p] = first[i, p]
        for t in range(1, group_batches):
            for p in range(pairs):
                for way in range(2):
                    i = t if way == 0 else group_batches - 1 - t
                    state = states[way, p]
                    high, low = split(state)
                    a = a_ref[i, p]
                    change = dot(jnp.concatenate([a, a[:, :PAIR]], axis=1), triple(high, low, 0))
                    states[way, p] = state + b_ref[i, p] - change
                    pre[way, base_batch + i, p] = states[way, p]

        @pl.when(n == 0)
        def _():
            sibling_own.start()
            for part in range(2):
                for i in range(1, xs):
                    wx_copy(part, i).wait_send()
            for d in (4, 5):
                kv_copy(d).start()
            for part in range(2):
                for i in range(1, xs):
                    wx_copy(part, i).wait_recv()
            for part in range(2):
                for d in (2, 1, 3):
                    w1_copy(part, d).start()

        @pl.when(n == 2)
        def _():
            for part in range(2):
                for d in (1, 2, 3):
                    w1_copy(part, d).wait_recv()
            for part in range(2):
                for d in (1, 3):
                    w2_copy(part, d).start()
            for part in range(2):
                sibling_band(part, 0).start()

    loop(0, xs, chip_maps)

    def linear_of(total):
        return triple(*split(jnp.where(own, total, 0.0)), 1)

    states = {}
    for t in range(xs):
        for p in range(pairs):
            for way in range(2):
                g = t if way == 0 else xs - 1 - t
                b = (g + 1) * group_batches - 1 if way == 0 else g * group_batches
                total = pre[way, b, p]
                if t:
                    change = dot(linear_of(total), triple(*split(states[way, p]), 0))
                    total = jnp.where(own, 0.0, total) + change
                states[way, p] = total
                group[way, g, p] = total
    for way in range(2):
        for p in range(pairs):
            totals[4 * p + way] = states[way, p][:HD]
            totals[4 * p + 2 + way] = states[way, p][HD:]

    shift = c * (seqs // 2)
    my_chain = (s + seqs - shift) % seqs
    is_owner = my_chain < chains

    def chain_at(k):
        return (k + shift) % seqs

    def tot_copy(k):
        return pltpu.make_async_remote_copy(
            src_ref=totals.at[k], dst_ref=inbox.at[s],
            send_sem=tot_send.at[k], recv_sem=tot_recv.at[s],
            device_id=(chain_at(k), h), device_id_type=MESH,
        )

    def tot_arrival(source):
        return pltpu.make_async_remote_copy(
            src_ref=totals.at[0], dst_ref=inbox.at[source],
            send_sem=tot_send.at[0], recv_sem=tot_recv.at[source],
            device_id=((s + 1) % seqs, h), device_id_type=MESH,
        )

    def send_total(d):
        k = (my_chain + d) % seqs

        @pl.when(k < chains)
        def _():
            tot_copy(k).start()

    loop(1, seqs, send_total)

    def fin_copy(k, to):
        return pltpu.make_async_remote_copy(
            src_ref=outbox.at[to], dst_ref=entry.at[k],
            send_sem=fin_send.at[to], recv_sem=fin_recv.at[k],
            device_id=(to, h), device_id_type=MESH,
        )

    def multiply_queries(dx):
        at_x = (x + xs - dx) % xs

        @pl.when(dx > 0)
        def _():
            q_copy(2 * dx).wait_recv()

        q_copy(2 * dx + 1).wait_recv()

        def one(i):
            b = at_x * group_batches + i
            at = pl.ds(pl.multiple_of(b * MB, MB), MB)
            for p in range(pairs):
                query = recv[0, at, p * PAIR:(p + 1) * PAIR]
                ahead, behind = pre[0, b, p], pre[1, b, p]
                high, low = split(jnp.concatenate(
                    [jnp.where(own, ahead, 0.0), jnp.where(own, behind, 0.0), jnp.where(own, 0.0, ahead + behind)],
                    axis=1,
                ))
                product = dot(jnp.concatenate([query, query], axis=1), jnp.concatenate([high, low], axis=0))
                high, low = split(product[:, :2 * PAIR])
                q_high[p, at, :] = high
                q_low[p, at, :] = low
                r_ref[p, at, :] = product[:, 2 * PAIR:]

        loop(0, group_batches, one)

    own_q.wait()
    loop(0, xs - 1, lambda n: multiply_queries(near(n)))

    @pl.when(is_owner)
    def _():
        inbox[s] = totals[my_chain]
        way = my_chain % 2
        number = my_chain // 2
        odd = number % 2
        half_lane = lax.broadcasted_iota(jnp.int32, (HD, PAIR), 1)
        mine = half_lane // HD != odd
        start = initial[number]

        def place(t):
            return jnp.where(way == 0, t, seqs - 1 - t)

        def arrive(source):
            @pl.when(source != s)
            def _():
                tot_arrival(source).wait_recv()

        loop(0, seqs, arrive)

        def apply(total, high, low):
            linear_high, linear_low = split(jnp.where(mine, 0.0, total))
            return jnp.where(mine, total, 0.0) + dot(
                triple(linear_high, linear_low, 1),
                jnp.concatenate([high, high, high, high, low, low], axis=0),
            )

        def emit(t, state):
            high, low = split(state)
            outbox[place(t)] = (high.astype(F32) + pltpu.roll(low.astype(F32), HD, 1)).astype(BF)

        quads = seqs // side
        maps = [[None] * side for _ in range(quads)]
        for j in range(side):
            for g in range(quads):
                total = inbox[place(g * side + j)]
                maps[g][j] = total if j == 0 else apply(total, *split(maps[g][j - 1]))
        state = jnp.where(mine, jnp.concatenate([start, start], axis=1), 0.0)
        states = [state]
        for g in range(quads - 1):
            states.append(jnp.where(mine, apply(maps[g][side - 1], *split(states[-1])), 0.0))
        for g in range(quads):
            emit(g * side, states[g])
            parts = split(states[g])
            for j in range(side - 1):
                emit(g * side + j + 1, jnp.where(mine, apply(maps[g][j], *parts), 0.0))

        entry[my_chain] = outbox[s]
        loop(1, seqs, lambda d: fin_copy(my_chain, (s + d) % seqs).start())

    multiply_queries(jnp.int32(xs // 2))

    def wait_entry(k):
        @pl.when(chain_at(k) != s)
        def _():
            fin_copy(k, (s + 1) % seqs).wait_recv()

    loop(0, chains, wait_entry)

    half_upper = lax.broadcasted_iota(jnp.int32, (HD, PAIR), 1) >= HD
    mean = jnp.where(own, 1.0 / HD, 0.0).astype(BF)
    mean = jnp.concatenate([mean, mean], axis=0)
    entered = []
    for p in range(pairs):
        ways = []
        for way in range(2):
            highs, lows = [], []
            for odd in range(2):
                packed = entry[4 * p + 2 * odd + way].astype(F32)
                mine = half_upper if odd == 0 else jnp.logical_not(half_upper)
                highs.append(jnp.where(mine, packed, 0.0).astype(BF))
                lows.append(jnp.where(mine, pltpu.roll(packed, HD, 1), 0.0).astype(BF))
            ways.append((jnp.concatenate(highs, axis=0), jnp.concatenate(lows, axis=0)))
        entered.append(ways)

    def nrm_copy(d):
        to = peer(d, 1)
        return pltpu.make_async_remote_copy(
            src_ref=normed.at[pl.ds(pl.multiple_of(to * rows, rows), rows), :],
            dst_ref=normed_in.at[(xs - d // 2) % xs, :, pl.ds(pl.multiple_of(c * width, PAIR), width)],
            send_sem=nrm_send.at[d], recv_sem=nrm_recv.at[d],
            device_id=(s, to), device_id_type=MESH,
        )

    own_normed = pltpu.make_async_copy(
        normed.at[pl.ds(pl.multiple_of(h * rows, rows), rows), :],
        normed_in.at[0, :, pl.ds(pl.multiple_of(c * width, PAIR), width)],
        own_sem.at[3],
    )

    def read_chip(dx):
        at_x = (x + dx) % xs
        at = pl.ds(pl.multiple_of(at_x * chip_rows, chip_rows), chip_rows)
        for p in range(pairs):
            highs, lows = [], []
            for way in range(2):
                high, low = entered[p][way]
                before = (at_x + xs - 1) % xs if way == 0 else (at_x + 1) % xs
                total = group[way, before, p]
                moved = jnp.where(own, 0.0, total) + dot(linear_of(total), triple(high, low, 0))
                edge = at_x == (0 if way == 0 else xs - 1)
                moved_high, moved_low = split(jnp.where(own, 0.0, moved))
                highs.append(jnp.where(edge, high, moved_high))
                lows.append(jnp.where(edge, low, moved_low))
            weight = jnp.concatenate([jnp.concatenate(highs, axis=0), jnp.concatenate(lows, axis=0)], axis=1)
            product = dot(q_high[p, at, :], weight)
            read = product[:, :PAIR] + product[:, PAIR:] + dot(q_low[p, at, :], weight[:, :PAIR]) + r_ref[p, at, :]
            high, low = split(read * read)
            mean_square = dot(jnp.concatenate([high, low], axis=1), mean)
            value = pltpu.roll(read * lax.rsqrt(mean_square + 1e-06), HD, 1)
            value = value * gain[p * PAIR:(p + 1) * PAIR]
            normed[at, p * PAIR:(p + 1) * PAIR] = value.astype(BF)

    def read_and_send(n):
        dx = near(xs - 1 - n)
        read_chip(dx)

        @pl.when(dx > 0)
        def _():
            nrm_copy(2 * dx).start()

        nrm_copy(2 * dx + 1).start()

    loop(0, xs, read_and_send)
    own_normed.start()

    for part in range(2):
        for d in (1, 3):
            w2_copy(part, d).wait_recv()
            w3_copy(part, d).start()
            sibling_band(part, d).start()
    for part in range(2):
        for d in (1, 3):
            w3_copy(part, d).wait_recv()
        sibling_band(part, 2).start()

    own_w.wait()
    sibling_own.wait_recv()
    own_normed.wait()
    for d in range(1, heads):
        nrm_copy(d).wait_recv()

    def sibling_arrival(part, d):
        last = z if part == 0 else y
        at_rows, _ = piece(part, width - base, (last + side - d) % side, 0)
        where = whole.at[pl.ds(1, xs - 1), at_rows, :]
        return pltpu.make_async_remote_copy(
            src_ref=where, dst_ref=where,
            send_sem=sib_send.at[part, d], recv_sem=sib_recv.at[part, d],
            device_id=sibling, device_id_type=MESH,
        )

    for part in range(2):
        for d in range(side):
            sibling_arrival(part, d).wait_recv()

    tile = 512

    def project(j):
        at = pl.ds(pl.multiple_of(j * tile, tile), tile)
        total = dot(normed_in[0], whole[0, :, at])
        for i in range(1, xs):
            total = total + dot(normed_in[i], whole[i, :, at])
        out[:, at] = total

    loop(0, w_hbm.shape[1] // tile, project)

    for part in range(2):
        for i in range(1, xs):
            w1_copy(part, i).wait_send()
        for d in (1, 3):
            w2_copy(part, d).wait_send()
            w3_copy(part, d).wait_send()
        for d in range(side):
            sibling_band(part, d).wait_send()
    sibling_own.wait_send()

    def drain_head(d):
        kv_copy(d).wait_send()
        q_copy(d).wait_send()
        nrm_copy(d).wait_send()

    def drain_total(k):
        @pl.when(chain_at(k) != s)
        def _():
            tot_copy(k).wait_send()

    loop(1, heads, drain_head)
    loop(0, chains, drain_total)

    @pl.when(is_owner)
    def _():
        def drain_fin(to):
            @pl.when(to != s)
            def _():
                fin_copy(my_chain, to).wait_send()

        loop(0, seqs, drain_fin)


def layer(qkv, eta, initial, gain, w_out, seqs, heads):
    rows = qkv.shape[1]
    width, columns = w_out.shape
    pairs = width // PAIR
    tokens = rows * heads
    batches = tokens // MB
    xs = heads // 2
    anywhere = pl.BlockSpec(memory_space=pl.ANY)
    dma = pltpu.SemaphoreType.DMA
    return pl.pallas_call(
        functools.partial(layer_kernel, seqs, heads, pairs),
        out_shape=jax.ShapeDtypeStruct((rows, columns), F32),
        in_specs=[anywhere] * 5,
        out_specs=pl.BlockSpec(memory_space=pltpu.VMEM),
        scratch_shapes=[
            pltpu.SMEM(eta.shape, F32),
            pltpu.VMEM(initial.shape, F32),
            pltpu.VMEM(gain.shape, F32),
            pltpu.VMEM((3, tokens, width), BF),
            pltpu.VMEM((batches // xs, pairs, PAIR, 2 * PAIR), BF),
            pltpu.VMEM((batches // xs, pairs, PAIR, PAIR), F32),
            pltpu.VMEM((2, batches, pairs, PAIR, PAIR), F32),
            pltpu.VMEM((2, xs, pairs, PAIR, PAIR), F32),
            pltpu.VMEM((4 * pairs, HD, PAIR), F32),
            pltpu.VMEM((seqs, HD, PAIR), F32),
            pltpu.VMEM((seqs, HD, PAIR), BF),
            pltpu.VMEM((4 * pairs, HD, PAIR), BF),
            pltpu.VMEM((pairs, tokens, 2 * PAIR), BF),
            pltpu.VMEM((pairs, tokens, 2 * PAIR), BF),
            pltpu.VMEM((pairs, tokens, PAIR), F32),
            pltpu.VMEM((tokens, width), BF),
            pltpu.VMEM((xs, rows, 2 * width), BF),
            pltpu.VMEM((xs, 2 * width, columns), BF),
            dma((3,)), dma((4,)),
            dma((heads,)), dma((heads,)), dma((heads,)), dma((heads,)),
            dma((4 * pairs,)), dma((seqs,)), dma((seqs,)), dma((4 * pairs,)),
            dma((heads,)), dma((heads,)),
            dma((2, 4)), dma((2, 4)), dma((2, 4)), dma((2, 4)), dma((2, 4)), dma((2, 4)),
            dma((2, 4)), dma((2, 4)), dma((3, 4)), dma((3, 4)),
        ],
        compiler_params=pltpu.CompilerParams(
            collective_id=0, has_side_effects=True, vmem_limit_bytes=57 << 20
        ),
    )(qkv, eta, initial, gain, w_out)


def solution(mesh):
    seqs, heads = mesh.shape["seq"], mesh.shape["head"]

    def shards(qkv, eta, initial, gain, w_out):
        return layer(jnp.transpose(qkv, (1, 0, 2)), eta, initial, gain, w_out, seqs, heads)

    return jax.shard_map(
        shards,
        mesh=mesh,
        in_specs=(
            P(("seq", "head"), None, None),
            P("head"),
            P("head", None, None),
            P("head"),
            P("head", None),
        ),
        out_specs=P(("seq", "head"), None),
        check_vma=False,
    )
```

```python
import functools

import jax
import jax.numpy as jnp
from jax import lax
from jax.experimental import pallas as pl
from jax.experimental.pallas import tpu as pltpu
from jax.sharding import PartitionSpec as P

MESH = pl.DeviceIdType.MESH
MB = 64
HD = 64
PAIR = 2 * HD
BF = jnp.bfloat16
F32 = jnp.float32


def split(x):
    high = x.astype(BF)
    return high, (x - high.astype(F32)).astype(BF)


def dot(a, b):
    return lax.dot_general(a, b, (((1,), (0,)), ((), ())), preferred_element_type=F32)


def triple(high, low, axis):
    parts = [high, low, high] if axis == 1 else [high, high, low]
    return jnp.concatenate(parts, axis=axis)


def layer_kernel(
    seqs, heads, pairs,
    qkv, eta_hbm, initial_hbm, gain_hbm, w_hbm, out,
    eta, initial, gain, recv, a_ref, b_ref, pre, group, totals, inbox, outbox, entry,
    q_high, q_low, r_ref, normed, normed_in, whole,
    const_sem, own_sem, kv_send, kv_recv, q_send, q_recv, tot_send, tot_recv, fin_send, fin_recv, nrm_send, nrm_recv,
    wx_send, wx_recv, w1_send, w1_recv, w2_send, w2_recv, w3_send, w3_recv, sib_send, sib_recv,
):
    s = lax.axis_index("seq")
    h = lax.axis_index("head")
    x, c = h // 2, h % 2
    xs = heads // 2
    side = 4
    z, y = s // side, s % side
    rows = qkv.shape[1]
    width = pairs * PAIR
    chip_rows = 2 * rows
    group_batches = chip_rows // MB
    chains = 4 * pairs

    barrier = pltpu.get_barrier_semaphore()

    def greet_head(d, _):
        pl.semaphore_signal(barrier, inc=1, device_id=(s, (h + d) % heads), device_id_type=MESH)
        return 0

    def greet_seq(d, _):
        pl.semaphore_signal(barrier, inc=1, device_id=((s + d) % seqs, h), device_id_type=MESH)
        return 0

    lax.fori_loop(1, heads, greet_head, 0)
    lax.fori_loop(1, seqs, greet_seq, 0)

    constants = [
        pltpu.make_async_copy(eta_hbm, eta, const_sem.at[0]),
        pltpu.make_async_copy(initial_hbm, initial, const_sem.at[1]),
        pltpu.make_async_copy(gain_hbm, gain, const_sem.at[2]),
    ]
    for copy in constants:
        copy.start()

    def own_copy(first, count, sem):
        return pltpu.make_async_copy(
            qkv.at[pl.ds(first, count), :, pl.ds(pl.multiple_of(h * width, PAIR), width)],
            recv.at[pl.ds(first, count), pl.ds(pl.multiple_of(h * rows, rows), rows), :],
            sem,
        )

    own_kv = own_copy(1, 2, own_sem.at[0])
    own_q = own_copy(0, 1, own_sem.at[1])
    own_kv.start()
    own_q.start()
    base = c * width
    own_w = pltpu.make_async_copy(w_hbm, whole.at[0, pl.ds(pl.multiple_of(base, PAIR), width), :], own_sem.at[2])
    own_w.start()
    pl.semaphore_wait(barrier, heads + seqs - 2)

    def peer(d, sign):
        dx, dc = d // 2, d % 2
        return ((x + sign * dx + xs) % xs) * 2 + (c + dc) % 2

    half = width // 2
    step = half // side
    cols = w_hbm.shape[1] // side

    def piece(part, first, last, second):
        at = part * half + last * step
        return pl.ds(pl.multiple_of(first + at, 16), step), pl.ds(pl.multiple_of(second * cols, PAIR), cols)

    def wx_copy(part, i):
        last, second = (z, y) if part == 0 else (y, z)
        from_rows, at_cols = piece(part, 0, last, second)
        to_rows, _ = piece(part, base, last, second)
        return pltpu.make_async_remote_copy(
            src_ref=w_hbm.at[from_rows, at_cols],
            dst_ref=whole.at[i, to_rows, at_cols],
            send_sem=wx_send.at[part, i], recv_sem=wx_recv.at[part, i],
            device_id=(s, ((x + xs - i) % xs) * 2 + c), device_id_type=MESH,
        )

    def along(axis, d):
        return (z * side + (y + d) % side, h) if axis == 0 else (((z + d) % side) * side + y, h)

    def w1_copy(part, d):
        last, second = (z, y) if part == 0 else (y, z)
        at_rows, at_cols = piece(part, base, last, second)
        where = whole.at[pl.ds(1, xs - 1), at_rows, at_cols]
        return pltpu.make_async_remote_copy(
            src_ref=where, dst_ref=where,
            send_sem=w1_send.at[part, d], recv_sem=w1_recv.at[part, d],
            device_id=along(part, d), device_id_type=MESH,
        )

    def band(part, d, side_half, core_base):
        last = z if part == 0 else y
        at_rows, _ = piece(part, core_base, (last + side - d) % side, 0)
        return whole.at[pl.ds(1, xs - 1), at_rows, pl.ds(side_half * 2 * cols, 2 * cols)]

    passed = {1: 0, 3: 1}

    def w2_copy(part, d, order):
        where = band(part, 0, passed[d] if order == 0 else 1 - passed[d], base)
        return pltpu.make_async_remote_copy(
            src_ref=where, dst_ref=where,
            send_sem=w2_send.at[part, d, order], recv_sem=w2_recv.at[part, d, order],
            device_id=along(1 - part, d), device_id_type=MESH,
        )

    def w3_copy(part, d):
        where = band(part, d, passed[d], base)
        return pltpu.make_async_remote_copy(
            src_ref=where, dst_ref=where,
            send_sem=w3_send.at[part, d], recv_sem=w3_recv.at[part, d],
            device_id=along(1 - part, d), device_id_type=MESH,
        )

    sibling = (s, x * 2 + 1 - c)

    def sibling_band(part, d, side_half, core_base):
        where = band(part, d, side_half, core_base)
        return pltpu.make_async_remote_copy(
            src_ref=where, dst_ref=where,
            send_sem=sib_send.at[part, d, side_half], recv_sem=sib_recv.at[part, d, side_half],
            device_id=sibling, device_id_type=MESH,
        )

    sibling_own = pltpu.make_async_remote_copy(
        src_ref=w_hbm, dst_ref=whole.at[0, pl.ds(pl.multiple_of(base, PAIR), width), :],
        send_sem=sib_send.at[2, 0, 0], recv_sem=sib_recv.at[2, 0, 0],
        device_id=sibling, device_id_type=MESH,
    )

    def kv_copy(d):
        to = peer(d, 1)
        return pltpu.make_async_remote_copy(
            src_ref=qkv.at[pl.ds(1, 2), :, pl.ds(pl.multiple_of(to * width, PAIR), width)],
            dst_ref=recv.at[pl.ds(1, 2), pl.ds(pl.multiple_of(h * rows, rows), rows), :],
            send_sem=kv_send.at[d], recv_sem=kv_recv.at[d],
            device_id=(s, to), device_id_type=MESH,
        )

    def q_copy(d):
        to = peer(d, 1)
        return pltpu.make_async_remote_copy(
            src_ref=qkv.at[pl.ds(0, 1), :, pl.ds(pl.multiple_of(to * width, PAIR), width)],
            dst_ref=recv.at[pl.ds(0, 1), pl.ds(pl.multiple_of(h * rows, rows), rows), :],
            send_sem=q_send.at[d], recv_sem=q_recv.at[d],
            device_id=(s, to), device_id_type=MESH,
        )

    def loop(first, last, act):
        def run(i, _):
            act(i)
            return 0

        lax.fori_loop(first, last, run, 0)

    kv_copy(1).start()
    for part in range(2):
        for i in (2, 1, 3):
            wx_copy(part, i).start()
    q_copy(1).start()
    kv_copy(2).start()
    kv_copy(3).start()
    kv_copy(6).start()
    kv_copy(7).start()
    kv_copy(4).start()
    kv_copy(5).start()

    def near(i):
        return jnp.where(i < 2, i, xs + 1 - i)

    row = lax.broadcasted_iota(jnp.int32, (PAIR, PAIR), 0)
    lane = lax.broadcasted_iota(jnp.int32, (PAIR, PAIR), 1)
    own = (row >= HD) == (lane >= HD)
    eye = jnp.where(row == lane, 1.0, 0.0).astype(F32)

    for copy in constants:
        copy.wait()

    own_kv.wait()
    rates = [jnp.where(row < HD, eta[2 * p], eta[2 * p + 1]) for p in range(pairs)]

    def chip_maps(n):
        dx = near(n)
        at_x = (x + xs - dx) % xs

        @pl.when(n > 0)
        def _():
            kv_copy(2 * dx).wait_recv()

        kv_copy(2 * dx + 1).wait_recv()

        @pl.when(n == 1)
        def _():
            q_copy(4).start()
            q_copy(5).start()
            q_copy(2).start()
            q_copy(3).start()
            q_copy(6).start()
            q_copy(7).start()


        first = {}
        for i in range(group_batches):
            at = pl.ds(pl.multiple_of(at_x * chip_rows + i * MB, MB), MB)
            for p in range(pairs):
                lanes = slice(p * PAIR, (p + 1) * PAIR)
                keys = recv[1, at, lanes]
                values = recv[2, at, lanes]
                swapped = pltpu.roll(values.astype(F32), HD, 1).astype(BF)
                both = lax.dot_general(
                    keys, jnp.concatenate([keys, swapped], axis=1),
                    (((0,), (0,)), ((), ())), preferred_element_type=F32,
                )
                linear = jnp.where(own, rates[p] * both[:, :PAIR], 0.0)
                offset = jnp.where(own, 0.0, rates[p] * both[:, PAIR:])
                high, low = split(linear)
                a_ref[i, p, :, :PAIR] = high
                a_ref[i, p, :, PAIR:] = low
                b_ref[i, p] = offset
                if i in (0, group_batches - 1):
                    first[i, p] = eye - linear + offset
        base_batch = at_x * group_batches
        states = {}
        for p in range(pairs):
            for way in range(2):
                i = 0 if way == 0 else group_batches - 1
                states[way, p] = first[i, p]
                pre[way, base_batch + i, p] = first[i, p]
        for t in range(1, group_batches):
            for p in range(pairs):
                for way in range(2):
                    i = t if way == 0 else group_batches - 1 - t
                    state = states[way, p]
                    high, low = split(state)
                    a = a_ref[i, p]
                    change = dot(jnp.concatenate([a, a[:, :PAIR]], axis=1), triple(high, low, 0))
                    states[way, p] = state + b_ref[i, p] - change
                    pre[way, base_batch + i, p] = states[way, p]

        @pl.when(n == 0)
        def _():
            for part in range(2):
                for i in range(1, xs):
                    wx_copy(part, i).wait_send()
                for i in range(1, xs):
                    wx_copy(part, i).wait_recv()
                for d in (2, 1, 3):
                    w1_copy(part, d).start()
            sibling_own.start()
            for part in range(2):
                for d in (1, 2, 3):
                    w1_copy(part, d).wait_recv()
                for d in (1, 3):
                    w2_copy(part, d, 0).start()
            for part in range(2):
                for side_half in range(2):
                    sibling_band(part, 0, side_half, base).start()

    loop(0, xs, chip_maps)

    def linear_of(total):
        return triple(*split(jnp.where(own, total, 0.0)), 1)

    states = {}
    for t in range(xs):
        for p in range(pairs):
            for way in range(2):
                g = t if way == 0 else xs - 1 - t
                b = (g + 1) * group_batches - 1 if way == 0 else g * group_batches
                total = pre[way, b, p]
                if t:
                    change = dot(linear_of(total), triple(*split(states[way, p]), 0))
                    total = jnp.where(own, 0.0, total) + change
                states[way, p] = total
                group[way, g, p] = total
    for way in range(2):
        for p in range(pairs):
            totals[4 * p + way] = states[way, p][:HD]
            totals[4 * p + 2 + way] = states[way, p][HD:]

    shift = c * (seqs // 2)
    my_chain = (s + seqs - shift) % seqs
    is_owner = my_chain < chains

    def chain_at(k):
        return (k + shift) % seqs

    def tot_copy(k):
        return pltpu.make_async_remote_copy(
            src_ref=totals.at[k], dst_ref=inbox.at[s],
            send_sem=tot_send.at[k], recv_sem=tot_recv.at[s],
            device_id=(chain_at(k), h), device_id_type=MESH,
        )

    def tot_arrival(source):
        return pltpu.make_async_remote_copy(
            src_ref=totals.at[0], dst_ref=inbox.at[source],
            send_sem=tot_send.at[0], recv_sem=tot_recv.at[source],
            device_id=((s + 1) % seqs, h), device_id_type=MESH,
        )

    def send_total(d):
        k = (my_chain + d) % seqs

        @pl.when(k < chains)
        def _():
            tot_copy(k).start()

    loop(1, seqs, send_total)

    for part in range(2):
        for d in (1, 3):
            w2_copy(part, d, 1).start()

    def fin_copy(k, to):
        return pltpu.make_async_remote_copy(
            src_ref=outbox.at[to], dst_ref=entry.at[k],
            send_sem=fin_send.at[to], recv_sem=fin_recv.at[k],
            device_id=(to, h), device_id_type=MESH,
        )

    def multiply_queries(dx):
        at_x = (x + xs - dx) % xs

        @pl.when(dx > 0)
        def _():
            q_copy(2 * dx).wait_recv()

        q_copy(2 * dx + 1).wait_recv()

        def one(i):
            b = at_x * group_batches + i
            at = pl.ds(pl.multiple_of(b * MB, MB), MB)
            for p in range(pairs):
                query = recv[0, at, p * PAIR:(p + 1) * PAIR]
                ahead, behind = pre[0, b, p], pre[1, b, p]
                high, low = split(jnp.concatenate(
                    [jnp.where(own, ahead, 0.0), jnp.where(own, behind, 0.0), jnp.where(own, 0.0, ahead + behind)],
                    axis=1,
                ))
                product = dot(jnp.concatenate([query, query], axis=1), jnp.concatenate([high, low], axis=0))
                high, low = split(product[:, :2 * PAIR])
                q_high[p, at, :] = high
                q_low[p, at, :] = low
                r_ref[p, at, :] = product[:, 2 * PAIR:]

        loop(0, group_batches, one)

    own_q.wait()
    loop(0, xs - 1, lambda n: multiply_queries(near(n)))

    @pl.when(is_owner)
    def _():
        inbox[s] = totals[my_chain]
        way = my_chain % 2
        number = my_chain // 2
        odd = number % 2
        half_lane = lax.broadcasted_iota(jnp.int32, (HD, PAIR), 1)
        mine = half_lane // HD != odd
        start = initial[number]

        def place(t):
            return jnp.where(way == 0, t, seqs - 1 - t)

        def arrive(source):
            @pl.when(source != s)
            def _():
                tot_arrival(source).wait_recv()

        loop(0, seqs, arrive)

        def apply(total, high, low):
            linear_high, linear_low = split(jnp.where(mine, 0.0, total))
            return jnp.where(mine, total, 0.0) + dot(
                triple(linear_high, linear_low, 1),
                jnp.concatenate([high, high, high, high, low, low], axis=0),
            )

        def emit(t, state):
            high, low = split(state)
            outbox[place(t)] = (high.astype(F32) + pltpu.roll(low.astype(F32), HD, 1)).astype(BF)

        quads = seqs // side
        maps = [[None] * side for _ in range(quads)]
        for j in range(side):
            for g in range(quads):
                total = inbox[place(g * side + j)]
                maps[g][j] = total if j == 0 else apply(total, *split(maps[g][j - 1]))
        state = jnp.where(mine, jnp.concatenate([start, start], axis=1), 0.0)
        states = [state]
        for g in range(quads - 1):
            states.append(jnp.where(mine, apply(maps[g][side - 1], *split(states[-1])), 0.0))
        for g in range(quads):
            emit(g * side, states[g])
            parts = split(states[g])
            for j in range(side - 1):
                emit(g * side + j + 1, jnp.where(mine, apply(maps[g][j], *parts), 0.0))

        entry[my_chain] = outbox[s]
        loop(1, seqs, lambda d: fin_copy(my_chain, (s + d) % seqs).start())

    multiply_queries(jnp.int32(xs // 2))

    for part in range(2):
        for d in (1, 3):
            w2_copy(part, d, 0).wait_recv()
            w3_copy(part, d).start()
    for part in range(2):
        for d in (1, 3):
            sibling_band(part, d, passed[d], base).start()

    def wait_entry(k):
        @pl.when(chain_at(k) != s)
        def _():
            fin_copy(k, (s + 1) % seqs).wait_recv()

    loop(0, chains, wait_entry)

    half_upper = lax.broadcasted_iota(jnp.int32, (HD, PAIR), 1) >= HD
    mean = jnp.where(own, 1.0 / HD, 0.0).astype(BF)
    mean = jnp.concatenate([mean, mean], axis=0)
    entered = []
    for p in range(pairs):
        ways = []
        for way in range(2):
            highs, lows = [], []
            for odd in range(2):
                packed = entry[4 * p + 2 * odd + way].astype(F32)
                mine = half_upper if odd == 0 else jnp.logical_not(half_upper)
                highs.append(jnp.where(mine, packed, 0.0).astype(BF))
                lows.append(jnp.where(mine, pltpu.roll(packed, HD, 1), 0.0).astype(BF))
            ways.append((jnp.concatenate(highs, axis=0), jnp.concatenate(lows, axis=0)))
        entered.append(ways)

    def nrm_copy(d):
        to = peer(d, 1)
        return pltpu.make_async_remote_copy(
            src_ref=normed.at[pl.ds(pl.multiple_of(to * rows, rows), rows), :],
            dst_ref=normed_in.at[(xs - d // 2) % xs, :, pl.ds(pl.multiple_of(c * width, PAIR), width)],
            send_sem=nrm_send.at[d], recv_sem=nrm_recv.at[d],
            device_id=(s, to), device_id_type=MESH,
        )

    own_normed = pltpu.make_async_copy(
        normed.at[pl.ds(pl.multiple_of(h * rows, rows), rows), :],
        normed_in.at[0, :, pl.ds(pl.multiple_of(c * width, PAIR), width)],
        own_sem.at[3],
    )

    def read_chip(dx):
        at_x = (x + dx) % xs
        at = pl.ds(pl.multiple_of(at_x * chip_rows, chip_rows), chip_rows)
        for p in range(pairs):
            highs, lows = [], []
            for way in range(2):
                high, low = entered[p][way]
                before = (at_x + xs - 1) % xs if way == 0 else (at_x + 1) % xs
                total = group[way, before, p]
                moved = jnp.where(own, 0.0, total) + dot(linear_of(total), triple(high, low, 0))
                edge = at_x == (0 if way == 0 else xs - 1)
                moved_high, moved_low = split(jnp.where(own, 0.0, moved))
                highs.append(jnp.where(edge, high, moved_high))
                lows.append(jnp.where(edge, low, moved_low))
            weight = jnp.concatenate([jnp.concatenate(highs, axis=0), jnp.concatenate(lows, axis=0)], axis=1)
            product = dot(q_high[p, at, :], weight)
            read = product[:, :PAIR] + product[:, PAIR:] + dot(q_low[p, at, :], weight[:, :PAIR]) + r_ref[p, at, :]
            high, low = split(read * read)
            mean_square = dot(jnp.concatenate([high, low], axis=1), mean)
            value = pltpu.roll(read * lax.rsqrt(mean_square + 1e-06), HD, 1)
            value = value * gain[p * PAIR:(p + 1) * PAIR]
            normed[at, p * PAIR:(p + 1) * PAIR] = value.astype(BF)

    def read_and_send(n):
        dx = near(xs - 1 - n)
        read_chip(dx)

        @pl.when(dx > 0)
        def _():
            nrm_copy(2 * dx).start()

        nrm_copy(2 * dx + 1).start()

    loop(0, xs, read_and_send)
    own_normed.start()

    for part in range(2):
        for d in (1, 3):
            w2_copy(part, d, 1).wait_recv()
            sibling_band(part, d, 1 - passed[d], base).start()
    for part in range(2):
        for d in (1, 3):
            w3_copy(part, d).wait_recv()
            sibling_band(part, 2, passed[d], base).start()

    own_w.wait()
    sibling_own.wait_recv()
    own_normed.wait()
    for d in range(1, heads):
        nrm_copy(d).wait_recv()

    for part in range(2):
        for d in range(side):
            for side_half in range(2):
                sibling_band(part, d, side_half, width - base).wait_recv()

    tile = 512

    def project(j):
        at = pl.ds(pl.multiple_of(j * tile, tile), tile)
        total = dot(normed_in[0], whole[0, :, at])
        for i in range(1, xs):
            total = total + dot(normed_in[i], whole[i, :, at])
        out[:, at] = total

    loop(0, w_hbm.shape[1] // tile, project)

    for part in range(2):
        for i in range(1, xs):
            w1_copy(part, i).wait_send()
        for d in (1, 3):
            w2_copy(part, d, 0).wait_send()
            w2_copy(part, d, 1).wait_send()
            w3_copy(part, d).wait_send()
        for d in range(side):
            for side_half in range(2):
                sibling_band(part, d, side_half, base).wait_send()
    sibling_own.wait_send()

    def drain_head(d):
        kv_copy(d).wait_send()
        q_copy(d).wait_send()
        nrm_copy(d).wait_send()

    def drain_total(k):
        @pl.when(chain_at(k) != s)
        def _():
            tot_copy(k).wait_send()

    loop(1, heads, drain_head)
    loop(0, chains, drain_total)

    @pl.when(is_owner)
    def _():
        def drain_fin(to):
            @pl.when(to != s)
            def _():
                fin_copy(my_chain, to).wait_send()

        loop(0, seqs, drain_fin)


def layer(qkv, eta, initial, gain, w_out, seqs, heads):
    rows = qkv.shape[1]
    width, columns = w_out.shape
    pairs = width // PAIR
    tokens = rows * heads
    batches = tokens // MB
    xs = heads // 2
    anywhere = pl.BlockSpec(memory_space=pltpu.HBM)
    dma = pltpu.SemaphoreType.DMA
    return pl.pallas_call(
        functools.partial(layer_kernel, seqs, heads, pairs),
        out_shape=jax.ShapeDtypeStruct((rows, columns), F32),
        in_specs=[anywhere] * 5,
        out_specs=pl.BlockSpec(memory_space=pltpu.VMEM),
        scratch_shapes=[
            pltpu.SMEM(eta.shape, F32),
            pltpu.VMEM(initial.shape, F32),
            pltpu.VMEM(gain.shape, F32),
            pltpu.VMEM((3, tokens, width), BF),
            pltpu.VMEM((batches // xs, pairs, PAIR, 2 * PAIR), BF),
            pltpu.VMEM((batches // xs, pairs, PAIR, PAIR), F32),
            pltpu.VMEM((2, batches, pairs, PAIR, PAIR), F32),
            pltpu.VMEM((2, xs, pairs, PAIR, PAIR), F32),
            pltpu.VMEM((4 * pairs, HD, PAIR), F32),
            pltpu.VMEM((seqs, HD, PAIR), F32),
            pltpu.VMEM((seqs, HD, PAIR), BF),
            pltpu.VMEM((4 * pairs, HD, PAIR), BF),
            pltpu.VMEM((pairs, tokens, 2 * PAIR), BF),
            pltpu.VMEM((pairs, tokens, 2 * PAIR), BF),
            pltpu.VMEM((pairs, tokens, PAIR), F32),
            pltpu.VMEM((tokens, width), BF),
            pltpu.VMEM((xs, rows, 2 * width), BF),
            pltpu.VMEM((xs, 2 * width, columns), BF),
            dma((3,)), dma((4,)),
            dma((heads,)), dma((heads,)), dma((heads,)), dma((heads,)),
            dma((4 * pairs,)), dma((seqs,)), dma((seqs,)), dma((4 * pairs,)),
            dma((heads,)), dma((heads,)),
            dma((2, 4)), dma((2, 4)), dma((2, 4)), dma((2, 4)), dma((2, 4, 2)), dma((2, 4, 2)),
            dma((2, 4)), dma((2, 4)), dma((3, 4, 2)), dma((3, 4, 2)),
        ],
        compiler_params=pltpu.CompilerParams(
            collective_id=0, has_side_effects=True, vmem_limit_bytes=57 << 20
        ),
    )(qkv, eta, initial, gain, w_out)


def solution(mesh):
    seqs, heads = mesh.shape["seq"], mesh.shape["head"]

    def shards(qkv, eta, initial, gain, w_out):
        return layer(jnp.transpose(qkv, (1, 0, 2)), eta, initial, gain, w_out, seqs, heads)

    return jax.shard_map(
        shards,
        mesh=mesh,
        in_specs=(
            P(("seq", "head"), None, None),
            P("head"),
            P("head", None, None),
            P("head"),
            P("head", None),
        ),
        out_specs=P(("seq", "head"), None),
        check_vma=False,
    )
```

```python
import functools

import jax
import jax.numpy as jnp
from jax import lax
from jax.experimental import pallas as pl
from jax.experimental.pallas import tpu as pltpu
from jax.sharding import PartitionSpec as P

MESH = pl.DeviceIdType.MESH
MB = 64
HD = 64
PAIR = 2 * HD
BF = jnp.bfloat16
F32 = jnp.float32


def split(x):
    high = x.astype(BF)
    return high, (x - high.astype(F32)).astype(BF)


def dot(a, b):
    return lax.dot_general(a, b, (((1,), (0,)), ((), ())), preferred_element_type=F32)


def triple(high, low, axis):
    parts = [high, low, high] if axis == 1 else [high, high, low]
    return jnp.concatenate(parts, axis=axis)


def layer_kernel(
    seqs, heads, pairs,
    qkv, eta_hbm, initial_hbm, gain_hbm, w_hbm, out,
    eta, initial, gain, recv, a_ref, b_ref, pre, group, totals, inbox, outbox, entry,
    q_high, q_low, r_ref, normed, normed_in, whole,
    const_sem, own_sem, kv_send, kv_recv, q_send, q_recv, tot_send, tot_recv, fin_send, fin_recv, nrm_send, nrm_recv,
    wx_send, wx_recv, w1_send, w1_recv, w2_send, w2_recv, w3_send, w3_recv, sib_send, sib_recv,
):
    s = lax.axis_index("seq")
    h = lax.axis_index("head")
    x, c = h // 2, h % 2
    xs = heads // 2
    side = 4
    z, y = s // side, s % side
    rows = qkv.shape[1]
    width = pairs * PAIR
    chip_rows = 2 * rows
    group_batches = chip_rows // MB
    chains = 4 * pairs

    barrier = pltpu.get_barrier_semaphore()

    def greet_head(d, _):
        pl.semaphore_signal(barrier, inc=1, device_id=(s, (h + d) % heads), device_id_type=MESH)
        return 0

    def greet_seq(d, _):
        pl.semaphore_signal(barrier, inc=1, device_id=((s + d) % seqs, h), device_id_type=MESH)
        return 0

    lax.fori_loop(1, heads, greet_head, 0)
    lax.fori_loop(1, seqs, greet_seq, 0)

    constants = [
        pltpu.make_async_copy(eta_hbm, eta, const_sem.at[0]),
        pltpu.make_async_copy(initial_hbm, initial, const_sem.at[1]),
        pltpu.make_async_copy(gain_hbm, gain, const_sem.at[2]),
    ]
    for copy in constants:
        copy.start()

    def own_copy(first, count, sem):
        return pltpu.make_async_copy(
            qkv.at[pl.ds(first, count), :, pl.ds(pl.multiple_of(h * width, PAIR), width)],
            recv.at[pl.ds(first, count), pl.ds(pl.multiple_of(h * rows, rows), rows), :],
            sem,
        )

    own_kv = own_copy(1, 2, own_sem.at[0])
    own_q = own_copy(0, 1, own_sem.at[1])
    own_kv.start()
    own_q.start()
    base = c * width
    own_w = pltpu.make_async_copy(w_hbm, whole.at[0, pl.ds(pl.multiple_of(base, PAIR), width), :], own_sem.at[2])
    own_w.start()
    pl.semaphore_wait(barrier, heads + seqs - 2)

    def peer(d, sign):
        dx, dc = d // 2, d % 2
        return ((x + sign * dx + xs) % xs) * 2 + (c + dc) % 2

    half = width // 2
    step = half // side
    cols = w_hbm.shape[1] // side

    def piece(part, first, last, second, k=0):
        at = part * half + last * step
        return (
            pl.ds(pl.multiple_of(first + at, 16), step),
            pl.ds(pl.multiple_of((2 * second + k) * (cols // 2), PAIR), cols // 2),
        )

    def wx_copy(part, i, k):
        last, second = (z, y) if part == 0 else (y, z)
        from_rows, at_cols = piece(part, 0, last, second, k)
        to_rows, _ = piece(part, base, last, second, k)
        return pltpu.make_async_remote_copy(
            src_ref=w_hbm.at[from_rows, at_cols],
            dst_ref=whole.at[i, to_rows, at_cols],
            send_sem=wx_send.at[part, i, k], recv_sem=wx_recv.at[part, i, k],
            device_id=(s, ((x + xs - i) % xs) * 2 + c), device_id_type=MESH,
        )

    def along(axis, d):
        return (z * side + (y + d) % side, h) if axis == 0 else (((z + d) % side) * side + y, h)

    def w1_copy(part, d, k):
        last, second = (z, y) if part == 0 else (y, z)
        at_rows, at_cols = piece(part, base, last, second, k)
        where = whole.at[pl.ds(1, xs - 1), at_rows, at_cols]
        return pltpu.make_async_remote_copy(
            src_ref=where, dst_ref=where,
            send_sem=w1_send.at[part, d, k], recv_sem=w1_recv.at[part, d, k],
            device_id=along(part, d), device_id_type=MESH,
        )

    def band(part, d, side_half, core_base):
        last = z if part == 0 else y
        at_rows, _ = piece(part, core_base, (last + side - d) % side, 0)
        return whole.at[pl.ds(1, xs - 1), at_rows, pl.ds(side_half * 2 * cols, 2 * cols)]

    passed = {1: 0, 3: 1}

    def w2_copy(part, d, order):
        if order == 0:
            where = band(part, 0, passed[d], base)
        else:
            at_rows, _ = piece(part, base, z if part == 0 else y, 0)
            at_cols = pl.ds((2 * (1 - passed[d]) + order - 1) * cols, cols)
            where = whole.at[pl.ds(1, xs - 1), at_rows, at_cols]
        return pltpu.make_async_remote_copy(
            src_ref=where, dst_ref=where,
            send_sem=w2_send.at[part, d, order], recv_sem=w2_recv.at[part, d, order],
            device_id=along(1 - part, d), device_id_type=MESH,
        )

    def w3_copy(part, d):
        where = band(part, d, passed[d], base)
        return pltpu.make_async_remote_copy(
            src_ref=where, dst_ref=where,
            send_sem=w3_send.at[part, d], recv_sem=w3_recv.at[part, d],
            device_id=along(1 - part, d), device_id_type=MESH,
        )

    sibling = (s, x * 2 + 1 - c)

    def sibling_band(part, d, side_half, core_base):
        where = band(part, d, side_half, core_base)
        return pltpu.make_async_remote_copy(
            src_ref=where, dst_ref=where,
            send_sem=sib_send.at[part, d, side_half], recv_sem=sib_recv.at[part, d, side_half],
            device_id=sibling, device_id_type=MESH,
        )

    sibling_own = pltpu.make_async_remote_copy(
        src_ref=w_hbm, dst_ref=whole.at[0, pl.ds(pl.multiple_of(base, PAIR), width), :],
        send_sem=sib_send.at[2, 0, 0], recv_sem=sib_recv.at[2, 0, 0],
        device_id=sibling, device_id_type=MESH,
    )

    def kv_copy(d):
        to = peer(d, 1)
        return pltpu.make_async_remote_copy(
            src_ref=qkv.at[pl.ds(1, 2), :, pl.ds(pl.multiple_of(to * width, PAIR), width)],
            dst_ref=recv.at[pl.ds(1, 2), pl.ds(pl.multiple_of(h * rows, rows), rows), :],
            send_sem=kv_send.at[d], recv_sem=kv_recv.at[d],
            device_id=(s, to), device_id_type=MESH,
        )

    def q_copy(d):
        to = peer(d, 1)
        return pltpu.make_async_remote_copy(
            src_ref=qkv.at[pl.ds(0, 1), :, pl.ds(pl.multiple_of(to * width, PAIR), width)],
            dst_ref=recv.at[pl.ds(0, 1), pl.ds(pl.multiple_of(h * rows, rows), rows), :],
            send_sem=q_send.at[d], recv_sem=q_recv.at[d],
            device_id=(s, to), device_id_type=MESH,
        )

    def loop(first, last, act):
        def run(i, _):
            act(i)
            return 0

        lax.fori_loop(first, last, run, 0)

    kv_copy(1).start()
    for k in range(2):
        for part in range(2):
            for i in (2, 1, 3):
                wx_copy(part, i, k).start()
    q_copy(1).start()
    kv_copy(2).start()
    kv_copy(3).start()
    kv_copy(6).start()
    kv_copy(7).start()
    kv_copy(4).start()
    kv_copy(5).start()

    def near(i):
        return jnp.where(i < 2, i, xs + 1 - i)

    row = lax.broadcasted_iota(jnp.int32, (PAIR, PAIR), 0)
    lane = lax.broadcasted_iota(jnp.int32, (PAIR, PAIR), 1)
    own = (row >= HD) == (lane >= HD)
    eye = jnp.where(row == lane, 1.0, 0.0).astype(F32)

    for copy in constants:
        copy.wait()

    own_kv.wait()
    rates = [jnp.where(row < HD, eta[2 * p], eta[2 * p + 1]) for p in range(pairs)]

    def chip_maps(n):
        dx = near(n)
        at_x = (x + xs - dx) % xs

        @pl.when(n > 0)
        def _():
            kv_copy(2 * dx).wait_recv()

        kv_copy(2 * dx + 1).wait_recv()

        @pl.when(n == 1)
        def _():
            q_copy(4).start()
            q_copy(5).start()
            q_copy(2).start()
            q_copy(3).start()
            q_copy(6).start()
            q_copy(7).start()


        first = {}
        for i in range(group_batches):
            at = pl.ds(pl.multiple_of(at_x * chip_rows + i * MB, MB), MB)
            for p in range(pairs):
                lanes = slice(p * PAIR, (p + 1) * PAIR)
                keys = recv[1, at, lanes]
                values = recv[2, at, lanes]
                swapped = pltpu.roll(values.astype(F32), HD, 1).astype(BF)
                both = lax.dot_general(
                    keys, jnp.concatenate([keys, swapped], axis=1),
                    (((0,), (0,)), ((), ())), preferred_element_type=F32,
                )
                linear = jnp.where(own, rates[p] * both[:, :PAIR], 0.0)
                offset = jnp.where(own, 0.0, rates[p] * both[:, PAIR:])
                high, low = split(linear)
                a_ref[i, p, :, :PAIR] = high
                a_ref[i, p, :, PAIR:] = low
                b_ref[i, p] = offset
                if i in (0, group_batches - 1):
                    first[i, p] = eye - linear + offset
        base_batch = at_x * group_batches
        states = {}
        for p in range(pairs):
            for way in range(2):
                i = 0 if way == 0 else group_batches - 1
                states[way, p] = first[i, p]
                pre[way, base_batch + i, p] = first[i, p]
        for t in range(1, group_batches):
            for p in range(pairs):
                for way in range(2):
                    i = t if way == 0 else group_batches - 1 - t
                    state = states[way, p]
                    high, low = split(state)
                    a = a_ref[i, p]
                    change = dot(jnp.concatenate([a, a[:, :PAIR]], axis=1), triple(high, low, 0))
                    states[way, p] = state + b_ref[i, p] - change
                    pre[way, base_batch + i, p] = states[way, p]

        @pl.when(n == 0)
        def _():
            for k in range(2):
                for part in range(2):
                    for i in range(1, xs):
                        wx_copy(part, i, k).wait_recv()
                    for d in (2, 1, 3):
                        w1_copy(part, d, k).start()
            sibling_own.start()
            for part in range(2):
                for d in (1, 2, 3):
                    for k in range(2):
                        w1_copy(part, d, k).wait_recv()
                for d in (1, 3):
                    w2_copy(part, d, 0).start()
            for part in range(2):
                for d in (1, 3):
                    w2_copy(part, d, 1).start()
            for part in range(2):
                for side_half in range(2):
                    sibling_band(part, 0, side_half, base).start()

    loop(0, xs, chip_maps)

    def linear_of(total):
        return triple(*split(jnp.where(own, total, 0.0)), 1)

    states = {}
    for t in range(xs):
        for p in range(pairs):
            for way in range(2):
                g = t if way == 0 else xs - 1 - t
                b = (g + 1) * group_batches - 1 if way == 0 else g * group_batches
                total = pre[way, b, p]
                if t:
                    change = dot(linear_of(total), triple(*split(states[way, p]), 0))
                    total = jnp.where(own, 0.0, total) + change
                states[way, p] = total
                group[way, g, p] = total
    for way in range(2):
        for p in range(pairs):
            totals[4 * p + way] = states[way, p][:HD]
            totals[4 * p + 2 + way] = states[way, p][HD:]

    shift = c * (seqs // 2)
    my_chain = (s + seqs - shift) % seqs
    is_owner = my_chain < chains

    def chain_at(k):
        return (k + shift) % seqs

    def tot_copy(k):
        return pltpu.make_async_remote_copy(
            src_ref=totals.at[k], dst_ref=inbox.at[s],
            send_sem=tot_send.at[k], recv_sem=tot_recv.at[s],
            device_id=(chain_at(k), h), device_id_type=MESH,
        )

    def tot_arrival(source):
        return pltpu.make_async_remote_copy(
            src_ref=totals.at[0], dst_ref=inbox.at[source],
            send_sem=tot_send.at[0], recv_sem=tot_recv.at[source],
            device_id=((s + 1) % seqs, h), device_id_type=MESH,
        )

    def send_total(d):
        k = (my_chain + d) % seqs

        @pl.when(k < chains)
        def _():
            tot_copy(k).start()

    loop(1, seqs, send_total)

    for part in range(2):
        for d in (1, 3):
            w2_copy(part, d, 2).start()

    def fin_copy(k, to):
        return pltpu.make_async_remote_copy(
            src_ref=outbox.at[to], dst_ref=entry.at[k],
            send_sem=fin_send.at[to], recv_sem=fin_recv.at[k],
            device_id=(to, h), device_id_type=MESH,
        )

    def multiply_queries(dx):
        at_x = (x + xs - dx) % xs

        @pl.when(dx > 0)
        def _():
            q_copy(2 * dx).wait_recv()

        q_copy(2 * dx + 1).wait_recv()

        def one(i):
            b = at_x * group_batches + i
            at = pl.ds(pl.multiple_of(b * MB, MB), MB)
            for p in range(pairs):
                query = recv[0, at, p * PAIR:(p + 1) * PAIR]
                ahead, behind = pre[0, b, p], pre[1, b, p]
                high, low = split(jnp.concatenate(
                    [jnp.where(own, ahead, 0.0), jnp.where(own, behind, 0.0), jnp.where(own, 0.0, ahead + behind)],
                    axis=1,
                ))
                product = dot(jnp.concatenate([query, query], axis=1), jnp.concatenate([high, low], axis=0))
                high, low = split(product[:, :2 * PAIR])
                q_high[p, at, :] = high
                q_low[p, at, :] = low
                r_ref[p, at, :] = product[:, 2 * PAIR:]

        loop(0, group_batches, one)

    own_q.wait()
    loop(0, xs - 1, lambda n: multiply_queries(near(n)))

    @pl.when(is_owner)
    def _():
        inbox[s] = totals[my_chain]
        way = my_chain % 2
        number = my_chain // 2
        odd = number % 2
        half_lane = lax.broadcasted_iota(jnp.int32, (HD, PAIR), 1)
        mine = half_lane // HD != odd
        start = initial[number]

        def place(t):
            return jnp.where(way == 0, t, seqs - 1 - t)

        def arrive(source):
            @pl.when(source != s)
            def _():
                tot_arrival(source).wait_recv()

        loop(0, seqs, arrive)

        def apply(total, high, low):
            linear_high, linear_low = split(jnp.where(mine, 0.0, total))
            return jnp.where(mine, total, 0.0) + dot(
                triple(linear_high, linear_low, 1),
                jnp.concatenate([high, high, high, high, low, low], axis=0),
            )

        def emit(t, state):
            high, low = split(state)
            outbox[place(t)] = (high.astype(F32) + pltpu.roll(low.astype(F32), HD, 1)).astype(BF)

        quads = seqs // side
        maps = [[None] * side for _ in range(quads)]
        for j in range(side):
            for g in range(quads):
                total = inbox[place(g * side + j)]
                maps[g][j] = total if j == 0 else apply(total, *split(maps[g][j - 1]))
        state = jnp.where(mine, jnp.concatenate([start, start], axis=1), 0.0)
        states = [state]
        for g in range(quads - 1):
            states.append(jnp.where(mine, apply(maps[g][side - 1], *split(states[-1])), 0.0))
        for g in range(quads):
            emit(g * side, states[g])
            parts = split(states[g])
            for j in range(side - 1):
                emit(g * side + j + 1, jnp.where(mine, apply(maps[g][j], *parts), 0.0))

        entry[my_chain] = outbox[s]
        loop(1, seqs, lambda d: fin_copy(my_chain, (s + d) % seqs).start())

    multiply_queries(jnp.int32(xs // 2))

    for part in range(2):
        for d in (1, 3):
            w2_copy(part, d, 0).wait_recv()
            w3_copy(part, d).start()
    for part in range(2):
        for d in (1, 3):
            sibling_band(part, d, passed[d], base).start()

    def wait_entry(k):
        @pl.when(chain_at(k) != s)
        def _():
            fin_copy(k, (s + 1) % seqs).wait_recv()

    loop(0, chains, wait_entry)

    half_upper = lax.broadcasted_iota(jnp.int32, (HD, PAIR), 1) >= HD
    mean = jnp.where(own, 1.0 / HD, 0.0).astype(BF)
    mean = jnp.concatenate([mean, mean], axis=0)
    entered = []
    for p in range(pairs):
        ways = []
        for way in range(2):
            highs, lows = [], []
            for odd in range(2):
                packed = entry[4 * p + 2 * odd + way].astype(F32)
                mine = half_upper if odd == 0 else jnp.logical_not(half_upper)
                highs.append(jnp.where(mine, packed, 0.0).astype(BF))
                lows.append(jnp.where(mine, pltpu.roll(packed, HD, 1), 0.0).astype(BF))
            ways.append((jnp.concatenate(highs, axis=0), jnp.concatenate(lows, axis=0)))
        entered.append(ways)

    def nrm_copy(d):
        to = peer(d, 1)
        return pltpu.make_async_remote_copy(
            src_ref=normed.at[pl.ds(pl.multiple_of(to * rows, rows), rows), :],
            dst_ref=normed_in.at[(xs - d // 2) % xs, :, pl.ds(pl.multiple_of(c * width, PAIR), width)],
            send_sem=nrm_send.at[d], recv_sem=nrm_recv.at[d],
            device_id=(s, to), device_id_type=MESH,
        )

    own_normed = pltpu.make_async_copy(
        normed.at[pl.ds(pl.multiple_of(h * rows, rows), rows), :],
        normed_in.at[0, :, pl.ds(pl.multiple_of(c * width, PAIR), width)],
        own_sem.at[3],
    )

    def read_chip(dx):
        at_x = (x + dx) % xs
        at = pl.ds(pl.multiple_of(at_x * chip_rows, chip_rows), chip_rows)
        for p in range(pairs):
            highs, lows = [], []
            for way in range(2):
                high, low = entered[p][way]
                before = (at_x + xs - 1) % xs if way == 0 else (at_x + 1) % xs
                total = group[way, before, p]
                moved = jnp.where(own, 0.0, total) + dot(linear_of(total), triple(high, low, 0))
                edge = at_x == (0 if way == 0 else xs - 1)
                moved_high, moved_low = split(jnp.where(own, 0.0, moved))
                highs.append(jnp.where(edge, high, moved_high))
                lows.append(jnp.where(edge, low, moved_low))
            weight = jnp.concatenate([jnp.concatenate(highs, axis=0), jnp.concatenate(lows, axis=0)], axis=1)
            product = dot(q_high[p, at, :], weight)
            read = product[:, :PAIR] + product[:, PAIR:] + dot(q_low[p, at, :], weight[:, :PAIR]) + r_ref[p, at, :]
            high, low = split(read * read)
            mean_square = dot(jnp.concatenate([high, low], axis=1), mean)
            value = pltpu.roll(read * lax.rsqrt(mean_square + 1e-06), HD, 1)
            value = value * gain[p * PAIR:(p + 1) * PAIR]
            normed[at, p * PAIR:(p + 1) * PAIR] = value.astype(BF)

    def read_and_send(n):
        dx = near(xs - 1 - n)
        read_chip(dx)

        @pl.when(dx > 0)
        def _():
            nrm_copy(2 * dx).start()

        nrm_copy(2 * dx + 1).start()

    loop(0, xs, read_and_send)
    own_normed.start()

    for part in range(2):
        for d in (1, 3):
            w2_copy(part, d, 1).wait_recv()
            w2_copy(part, d, 2).wait_recv()
            sibling_band(part, d, 1 - passed[d], base).start()
    for part in range(2):
        for d in (1, 3):
            w3_copy(part, d).wait_recv()
            sibling_band(part, 2, passed[d], base).start()

    own_w.wait()
    sibling_own.wait_recv()
    own_normed.wait()
    for d in range(1, heads):
        nrm_copy(d).wait_recv()

    for part in range(2):
        for d in range(side):
            for side_half in range(2):
                sibling_band(part, d, side_half, width - base).wait_recv()

    tile = 512

    def project(j):
        at = pl.ds(pl.multiple_of(j * tile, tile), tile)
        total = dot(normed_in[0], whole[0, :, at])
        for i in range(1, xs):
            total = total + dot(normed_in[i], whole[i, :, at])
        out[:, at] = total

    loop(0, w_hbm.shape[1] // tile, project)

    for part in range(2):
        for i in range(1, xs):
            for k in range(2):
                wx_copy(part, i, k).wait_send()
                w1_copy(part, i, k).wait_send()
        for d in (1, 3):
            w2_copy(part, d, 0).wait_send()
            w2_copy(part, d, 1).wait_send()
            w2_copy(part, d, 2).wait_send()
            w3_copy(part, d).wait_send()
        for d in range(side):
            for side_half in range(2):
                sibling_band(part, d, side_half, base).wait_send()
    sibling_own.wait_send()

    def drain_head(d):
        kv_copy(d).wait_send()
        q_copy(d).wait_send()
        nrm_copy(d).wait_send()

    def drain_total(k):
        @pl.when(chain_at(k) != s)
        def _():
            tot_copy(k).wait_send()

    loop(1, heads, drain_head)
    loop(0, chains, drain_total)

    @pl.when(is_owner)
    def _():
        def drain_fin(to):
            @pl.when(to != s)
            def _():
                fin_copy(my_chain, to).wait_send()

        loop(0, seqs, drain_fin)


def layer(qkv, eta, initial, gain, w_out, seqs, heads):
    rows = qkv.shape[1]
    width, columns = w_out.shape
    pairs = width // PAIR
    tokens = rows * heads
    batches = tokens // MB
    xs = heads // 2
    anywhere = pl.BlockSpec(memory_space=pltpu.HBM)
    dma = pltpu.SemaphoreType.DMA
    return pl.pallas_call(
        functools.partial(layer_kernel, seqs, heads, pairs),
        out_shape=jax.ShapeDtypeStruct((rows, columns), F32),
        in_specs=[anywhere] * 5,
        out_specs=pl.BlockSpec(memory_space=pltpu.VMEM),
        scratch_shapes=[
            pltpu.SMEM(eta.shape, F32),
            pltpu.VMEM(initial.shape, F32),
            pltpu.VMEM(gain.shape, F32),
            pltpu.VMEM((3, tokens, width), BF),
            pltpu.VMEM((batches // xs, pairs, PAIR, 2 * PAIR), BF),
            pltpu.VMEM((batches // xs, pairs, PAIR, PAIR), F32),
            pltpu.VMEM((2, batches, pairs, PAIR, PAIR), F32),
            pltpu.VMEM((2, xs, pairs, PAIR, PAIR), F32),
            pltpu.VMEM((4 * pairs, HD, PAIR), F32),
            pltpu.VMEM((seqs, HD, PAIR), F32),
            pltpu.VMEM((seqs, HD, PAIR), BF),
            pltpu.VMEM((4 * pairs, HD, PAIR), BF),
            pltpu.VMEM((pairs, tokens, 2 * PAIR), BF),
            pltpu.VMEM((pairs, tokens, 2 * PAIR), BF),
            pltpu.VMEM((pairs, tokens, PAIR), F32),
            pltpu.VMEM((tokens, width), BF),
            pltpu.VMEM((xs, rows, 2 * width), BF),
            pltpu.VMEM((xs, 2 * width, columns), BF),
            dma((3,)), dma((4,)),
            dma((heads,)), dma((heads,)), dma((heads,)), dma((heads,)),
            dma((4 * pairs,)), dma((seqs,)), dma((seqs,)), dma((4 * pairs,)),
            dma((heads,)), dma((heads,)),
            dma((2, 4, 2)), dma((2, 4, 2)), dma((2, 4, 2)), dma((2, 4, 2)), dma((2, 4, 3)), dma((2, 4, 3)),
            dma((2, 4)), dma((2, 4)), dma((3, 4, 2)), dma((3, 4, 2)),
        ],
        compiler_params=pltpu.CompilerParams(
            collective_id=0, has_side_effects=True, vmem_limit_bytes=50 << 20
        ),
    )(qkv, eta, initial, gain, w_out)


def solution(mesh):
    seqs, heads = mesh.shape["seq"], mesh.shape["head"]

    def shards(qkv, eta, initial, gain, w_out):
        return layer(jnp.transpose(qkv, (1, 0, 2)), eta, initial, gain, w_out, seqs, heads)

    return jax.shard_map(
        shards,
        mesh=mesh,
        in_specs=(
            P(("seq", "head"), None, None),
            P("head"),
            P("head", None, None),
            P("head"),
            P("head", None),
        ),
        out_specs=P(("seq", "head"), None),
        check_vma=False,
    )
```

```python
import functools

import jax
import jax.numpy as jnp
from jax import lax
from jax.experimental import pallas as pl
from jax.experimental.pallas import tpu as pltpu
from jax.sharding import PartitionSpec as P

MESH = pl.DeviceIdType.MESH
MB = 64
HD = 64
PAIR = 2 * HD
BF = jnp.bfloat16
F32 = jnp.float32


def split(x):
    high = x.astype(BF)
    return high, (x - high.astype(F32)).astype(BF)


def dot(a, b):
    return lax.dot_general(a, b, (((1,), (0,)), ((), ())), preferred_element_type=F32)


def triple(high, low, axis):
    parts = [high, low, high] if axis == 1 else [high, high, low]
    return jnp.concatenate(parts, axis=axis)


def layer_kernel(
    seqs, heads, pairs,
    qkv, eta_hbm, initial_hbm, gain_hbm, w_hbm, out,
    eta, initial, gain, recv, a_ref, b_ref, pre, group, totals, inbox, outbox, entry,
    q_high, q_low, r_ref, normed, normed_in, whole, mixed,
    const_sem, own_sem, kv_send, kv_recv, q_send, q_recv, tot_send, tot_recv, fin_send, fin_recv, nrm_send, nrm_recv,
    wx_send, wx_recv, w1_send, w1_recv, w2_send, w2_recv, w3_send, w3_recv, sib_send, sib_recv, last_send, last_recv,
    out_sem, wd_send, wd_recv, direct_send, direct_recv,
):
    s = lax.axis_index("seq")
    h = lax.axis_index("head")
    x, c = h // 2, h % 2
    xs = heads // 2
    side = 4
    z, y = s // side, s % side
    rows = qkv.shape[1]
    width = pairs * PAIR
    chip_rows = 2 * rows
    group_batches = chip_rows // MB
    chains = 4 * pairs

    barrier = pltpu.get_barrier_semaphore()

    def greet_head(d, _):
        pl.semaphore_signal(barrier, inc=1, device_id=(s, (h + d) % heads), device_id_type=MESH)
        return 0

    def greet_seq(d, _):
        pl.semaphore_signal(barrier, inc=1, device_id=((s + d) % seqs, h), device_id_type=MESH)
        return 0

    lax.fori_loop(1, heads, greet_head, 0)
    lax.fori_loop(1, seqs, greet_seq, 0)

    constants = [
        pltpu.make_async_copy(eta_hbm, eta, const_sem.at[0]),
        pltpu.make_async_copy(initial_hbm, initial, const_sem.at[1]),
        pltpu.make_async_copy(gain_hbm, gain, const_sem.at[2]),
    ]
    for copy in constants:
        copy.start()

    def own_copy(first, count, sem):
        return pltpu.make_async_copy(
            qkv.at[pl.ds(first, count), :, pl.ds(pl.multiple_of(h * width, PAIR), width)],
            recv.at[pl.ds(first, count), pl.ds(pl.multiple_of(h * rows, rows), rows), :],
            sem,
        )

    own_kv = own_copy(1, 2, own_sem.at[0])
    own_q = own_copy(0, 1, own_sem.at[1])
    own_kv.start()
    own_q.start()
    base = c * width
    own_w = pltpu.make_async_copy(w_hbm, whole.at[0, pl.ds(pl.multiple_of(base, PAIR), width), :], own_sem.at[2])
    own_w.start()
    pl.semaphore_wait(barrier, heads + seqs - 2)

    def peer(d, sign):
        dx, dc = d // 2, d % 2
        return ((x + sign * dx + xs) % xs) * 2 + (c + dc) % 2

    half = width // 2
    step = half // side
    cols = w_hbm.shape[1] // side

    def piece(part, first, last, second, k=0):
        at = part * half + last * step
        return (
            pl.ds(pl.multiple_of(first + at, 16), step),
            pl.ds(pl.multiple_of((2 * second + k) * (cols // 2), PAIR), cols // 2),
        )

    def wx_copy(part, i, k):
        last, second = (z, y) if part == 0 else (y, z)
        from_rows, at_cols = piece(part, 0, last, second, k)
        to_rows, _ = piece(part, base, last, second, k)
        return pltpu.make_async_remote_copy(
            src_ref=w_hbm.at[from_rows, at_cols],
            dst_ref=whole.at[i, to_rows, at_cols],
            send_sem=wx_send.at[part, i, k], recv_sem=wx_recv.at[part, i, k],
            device_id=(s, ((x + xs - i) % xs) * 2 + c), device_id_type=MESH,
        )

    def along(axis, d):
        return (z * side + (y + d) % side, h) if axis == 0 else (((z + d) % side) * side + y, h)

    def w1_copy(part, d, k):
        last, second = (z, y) if part == 0 else (y, z)
        at_rows, at_cols = piece(part, base, last, second, k)
        where = whole.at[pl.ds(1, xs - 1), at_rows, at_cols]
        return pltpu.make_async_remote_copy(
            src_ref=where, dst_ref=where,
            send_sem=w1_send.at[part, d, k], recv_sem=w1_recv.at[part, d, k],
            device_id=along(part, d), device_id_type=MESH,
        )

    def band(part, d, side_half, core_base):
        last = z if part == 0 else y
        at_rows, _ = piece(part, core_base, (last + side - d) % side, 0)
        return whole.at[pl.ds(1, xs - 1), at_rows, pl.ds(side_half * 2 * cols, 2 * cols)]

    passed = {1: 0, 3: 1}

    def w2_copy(part, d, order):
        if order == 0:
            where = band(part, 0, passed[d], base)
        else:
            at_rows, _ = piece(part, base, z if part == 0 else y, 0)
            at_cols = pl.ds((2 * (1 - passed[d]) + order - 1) * cols, cols)
            where = whole.at[pl.ds(1, xs - 1), at_rows, at_cols]
        return pltpu.make_async_remote_copy(
            src_ref=where, dst_ref=where,
            send_sem=w2_send.at[part, d, order], recv_sem=w2_recv.at[part, d, order],
            device_id=along(1 - part, d), device_id_type=MESH,
        )

    def quarter(part, d, side_half, k, core_base):
        last = z if part == 0 else y
        at_rows, _ = piece(part, core_base, (last + side - d) % side, 0)
        at_cols = pl.ds((2 * side_half + k) * cols, cols if k == 0 else cols // 2)
        return whole.at[pl.ds(1, xs - 1), at_rows, at_cols]

    def left_over(part, side_half, core_base):
        last = z if part == 0 else y
        at_rows, _ = piece(part, core_base, (last + 2) % side, 0)
        return at_rows, pl.ds((2 * side_half + 1) * cols + cols // 2, cols // 2)

    def wd_copy(part, side_half, i):
        from_rows, at_cols = left_over(part, side_half, 0)
        to_rows, _ = left_over(part, side_half, base)
        return pltpu.make_async_remote_copy(
            src_ref=w_hbm.at[from_rows, at_cols],
            dst_ref=whole.at[i, to_rows, at_cols],
            send_sem=wd_send.at[part, side_half, i], recv_sem=wd_recv.at[part, side_half, i],
            device_id=(s, ((x + xs - i) % xs) * 2 + c), device_id_type=MESH,
        )

    def w3_copy(part, d, k):
        where = quarter(part, d, passed[d], k, base)
        return pltpu.make_async_remote_copy(
            src_ref=where, dst_ref=where,
            send_sem=w3_send.at[part, d, k], recv_sem=w3_recv.at[part, d, k],
            device_id=along(1 - part, d), device_id_type=MESH,
        )

    sibling = (s, x * 2 + 1 - c)

    def sibling_band(part, d, side_half, core_base):
        where = band(part, d, side_half, core_base)
        return pltpu.make_async_remote_copy(
            src_ref=where, dst_ref=where,
            send_sem=sib_send.at[part, d, side_half], recv_sem=sib_recv.at[part, d, side_half],
            device_id=sibling, device_id_type=MESH,
        )

    def sibling_quarter(part, d, k, core_base):
        where = quarter(part, 2, passed[d], k, core_base)
        return pltpu.make_async_remote_copy(
            src_ref=where, dst_ref=where,
            send_sem=last_send.at[part, d, k], recv_sem=last_recv.at[part, d, k],
            device_id=sibling, device_id_type=MESH,
        )

    def sibling_direct(part, side_half, core_base):
        at_rows, at_cols = left_over(part, side_half, core_base)
        where = whole.at[pl.ds(1, xs - 1), at_rows, at_cols]
        return pltpu.make_async_remote_copy(
            src_ref=where, dst_ref=where,
            send_sem=direct_send.at[part, side_half], recv_sem=direct_recv.at[part, side_half],
            device_id=sibling, device_id_type=MESH,
        )

    sibling_own = pltpu.make_async_remote_copy(
        src_ref=w_hbm, dst_ref=whole.at[0, pl.ds(pl.multiple_of(base, PAIR), width), :],
        send_sem=sib_send.at[2, 0, 0], recv_sem=sib_recv.at[2, 0, 0],
        device_id=sibling, device_id_type=MESH,
    )

    def kv_copy(d):
        to = peer(d, 1)
        return pltpu.make_async_remote_copy(
            src_ref=qkv.at[pl.ds(1, 2), :, pl.ds(pl.multiple_of(to * width, PAIR), width)],
            dst_ref=recv.at[pl.ds(1, 2), pl.ds(pl.multiple_of(h * rows, rows), rows), :],
            send_sem=kv_send.at[d], recv_sem=kv_recv.at[d],
            device_id=(s, to), device_id_type=MESH,
        )

    def q_copy(d):
        to = peer(d, 1)
        return pltpu.make_async_remote_copy(
            src_ref=qkv.at[pl.ds(0, 1), :, pl.ds(pl.multiple_of(to * width, PAIR), width)],
            dst_ref=recv.at[pl.ds(0, 1), pl.ds(pl.multiple_of(h * rows, rows), rows), :],
            send_sem=q_send.at[d], recv_sem=q_recv.at[d],
            device_id=(s, to), device_id_type=MESH,
        )

    def loop(first, last, act):
        def run(i, _):
            act(i)
            return 0

        lax.fori_loop(first, last, run, 0)

    kv_copy(1).start()
    for k in range(2):
        for part in range(2):
            for i in (2, 1, 3):
                wx_copy(part, i, k).start()
    q_copy(1).start()
    kv_copy(2).start()
    kv_copy(3).start()
    kv_copy(6).start()
    kv_copy(7).start()
    kv_copy(4).start()
    kv_copy(5).start()

    def near(i):
        return jnp.where(i < 2, i, xs + 1 - i)

    row = lax.broadcasted_iota(jnp.int32, (PAIR, PAIR), 0)
    lane = lax.broadcasted_iota(jnp.int32, (PAIR, PAIR), 1)
    own = (row >= HD) == (lane >= HD)
    eye = jnp.where(row == lane, 1.0, 0.0).astype(F32)

    for copy in constants:
        copy.wait()

    own_kv.wait()
    rates = [jnp.where(row < HD, eta[2 * p], eta[2 * p + 1]) for p in range(pairs)]

    def chip_maps(n):
        dx = near(n)
        at_x = (x + xs - dx) % xs

        @pl.when(n > 0)
        def _():
            kv_copy(2 * dx).wait_recv()

        kv_copy(2 * dx + 1).wait_recv()

        @pl.when(n == 1)
        def _():
            q_copy(4).start()
            q_copy(5).start()
            q_copy(2).start()
            q_copy(3).start()
            q_copy(6).start()
            q_copy(7).start()
            for part in range(2):
                for side_half in range(2):
                    for i in (2, 1, 3):
                        wd_copy(part, side_half, i).start()


        first = {}
        for i in range(group_batches):
            at = pl.ds(pl.multiple_of(at_x * chip_rows + i * MB, MB), MB)
            for p in range(pairs):
                lanes = slice(p * PAIR, (p + 1) * PAIR)
                keys = recv[1, at, lanes]
                values = recv[2, at, lanes]
                swapped = pltpu.roll(values.astype(F32), HD, 1).astype(BF)
                both = lax.dot_general(
                    keys, jnp.concatenate([keys, swapped], axis=1),
                    (((0,), (0,)), ((), ())), preferred_element_type=F32,
                )
                linear = jnp.where(own, rates[p] * both[:, :PAIR], 0.0)
                offset = jnp.where(own, 0.0, rates[p] * both[:, PAIR:])
                high, low = split(linear)
                a_ref[i, p, :, :PAIR] = high
                a_ref[i, p, :, PAIR:] = low
                b_ref[i, p] = offset
                if i in (0, group_batches - 1):
                    first[i, p] = eye - linear + offset
        base_batch = at_x * group_batches
        states = {}
        for p in range(pairs):
            for way in range(2):
                i = 0 if way == 0 else group_batches - 1
                states[way, p] = first[i, p]
                pre[way, base_batch + i, p] = first[i, p]
        for t in range(1, group_batches):
            for p in range(pairs):
                for way in range(2):
                    i = t if way == 0 else group_batches - 1 - t
                    state = states[way, p]
                    high, low = split(state)
                    a = a_ref[i, p]
                    change = dot(jnp.concatenate([a, a[:, :PAIR]], axis=1), triple(high, low, 0))
                    states[way, p] = state + b_ref[i, p] - change
                    pre[way, base_batch + i, p] = states[way, p]

        @pl.when(n == 0)
        def _():
            for k in range(2):
                for part in range(2):
                    for i in range(1, xs):
                        wx_copy(part, i, k).wait_recv()
                    for d in (2, 1, 3):
                        w1_copy(part, d, k).start()
            sibling_own.start()
            for part in range(2):
                for d in (1, 2, 3):
                    for k in range(2):
                        w1_copy(part, d, k).wait_recv()
                for d in (1, 3):
                    w2_copy(part, d, 0).start()
            for part in range(2):
                for side_half in range(2):
                    sibling_band(part, 0, side_half, base).start()

    loop(0, xs, chip_maps)

    def linear_of(total):
        return triple(*split(jnp.where(own, total, 0.0)), 1)

    states = {}
    for t in range(xs):
        for p in range(pairs):
            for way in range(2):
                g = t if way == 0 else xs - 1 - t
                b = (g + 1) * group_batches - 1 if way == 0 else g * group_batches
                total = pre[way, b, p]
                if t:
                    change = dot(linear_of(total), triple(*split(states[way, p]), 0))
                    total = jnp.where(own, 0.0, total) + change
                states[way, p] = total
                group[way, g, p] = total
    for way in range(2):
        for p in range(pairs):
            totals[4 * p + way] = states[way, p][:HD]
            totals[4 * p + 2 + way] = states[way, p][HD:]

    shift = c * (seqs // 2)
    my_chain = (s + seqs - shift) % seqs
    is_owner = my_chain < chains

    def chain_at(k):
        return (k + shift) % seqs

    def tot_copy(k):
        return pltpu.make_async_remote_copy(
            src_ref=totals.at[k], dst_ref=inbox.at[s],
            send_sem=tot_send.at[k], recv_sem=tot_recv.at[s],
            device_id=(chain_at(k), h), device_id_type=MESH,
        )

    def tot_arrival(source):
        return pltpu.make_async_remote_copy(
            src_ref=totals.at[0], dst_ref=inbox.at[source],
            send_sem=tot_send.at[0], recv_sem=tot_recv.at[source],
            device_id=((s + 1) % seqs, h), device_id_type=MESH,
        )

    def send_total(d):
        k = (my_chain + d) % seqs

        @pl.when(k < chains)
        def _():
            tot_copy(k).start()

    loop(1, seqs, send_total)

    for part in range(2):
        for d in (1, 3):
            w2_copy(part, d, 1).start()


    def fin_copy(k, to):
        return pltpu.make_async_remote_copy(
            src_ref=outbox.at[to], dst_ref=entry.at[k],
            send_sem=fin_send.at[to], recv_sem=fin_recv.at[k],
            device_id=(to, h), device_id_type=MESH,
        )

    def multiply_queries(dx):
        at_x = (x + xs - dx) % xs

        @pl.when(dx > 0)
        def _():
            q_copy(2 * dx).wait_recv()

        q_copy(2 * dx + 1).wait_recv()

        def one(i):
            b = at_x * group_batches + i
            at = pl.ds(pl.multiple_of(b * MB, MB), MB)
            for p in range(pairs):
                query = recv[0, at, p * PAIR:(p + 1) * PAIR]
                ahead, behind = pre[0, b, p], pre[1, b, p]
                high, low = split(jnp.concatenate(
                    [jnp.where(own, ahead, 0.0), jnp.where(own, behind, 0.0), jnp.where(own, 0.0, ahead + behind)],
                    axis=1,
                ))
                product = dot(jnp.concatenate([query, query], axis=1), jnp.concatenate([high, low], axis=0))
                high, low = split(product[:, :2 * PAIR])
                q_high[p, at, :] = high
                q_low[p, at, :] = low
                r_ref[p, at, :] = product[:, 2 * PAIR:]

        loop(0, group_batches, one)

    own_q.wait()
    loop(0, xs - 1, lambda n: multiply_queries(near(n)))

    @pl.when(is_owner)
    def _():
        inbox[s] = totals[my_chain]
        way = my_chain % 2
        number = my_chain // 2
        odd = number % 2
        half_lane = lax.broadcasted_iota(jnp.int32, (HD, PAIR), 1)
        mine = half_lane // HD != odd
        start = initial[number]

        def place(t):
            return jnp.where(way == 0, t, seqs - 1 - t)

        def arrive(source):
            @pl.when(source != s)
            def _():
                tot_arrival(source).wait_recv()

        loop(0, seqs, arrive)

        def apply(total, high, low):
            linear_high, linear_low = split(jnp.where(mine, 0.0, total))
            return jnp.where(mine, total, 0.0) + dot(
                triple(linear_high, linear_low, 1),
                jnp.concatenate([high, high, high, high, low, low], axis=0),
            )

        def emit(t, state):
            high, low = split(state)
            outbox[place(t)] = (high.astype(F32) + pltpu.roll(low.astype(F32), HD, 1)).astype(BF)

        quads = seqs // side
        maps = [[None] * side for _ in range(quads)]
        for j in range(side):
            for g in range(quads):
                total = inbox[place(g * side + j)]
                maps[g][j] = total if j == 0 else apply(total, *split(maps[g][j - 1]))
        state = jnp.where(mine, jnp.concatenate([start, start], axis=1), 0.0)
        states = [state]
        for g in range(quads - 1):
            states.append(jnp.where(mine, apply(maps[g][side - 1], *split(states[-1])), 0.0))
        for g in range(quads):
            emit(g * side, states[g])
            parts = split(states[g])
            for j in range(side - 1):
                emit(g * side + j + 1, jnp.where(mine, apply(maps[g][j], *parts), 0.0))

        entry[my_chain] = outbox[s]
        loop(1, seqs, lambda d: fin_copy(my_chain, (s + d) % seqs).start())

    multiply_queries(jnp.int32(xs // 2))

    for part in range(2):
        for d in (1, 3):
            w2_copy(part, d, 2).start()

    for part in range(2):
        for d in (1, 3):
            w2_copy(part, d, 0).wait_recv()
            w3_copy(part, d, 0).start()
    for part in range(2):
        for d in (1, 3):
            w3_copy(part, d, 1).start()
    for part in range(2):
        for d in (1, 3):
            sibling_band(part, d, passed[d], base).start()

    def wait_entry(k):
        @pl.when(chain_at(k) != s)
        def _():
            fin_copy(k, (s + 1) % seqs).wait_recv()

    loop(0, chains, wait_entry)

    half_upper = lax.broadcasted_iota(jnp.int32, (HD, PAIR), 1) >= HD
    mean = jnp.where(own, 1.0 / HD, 0.0).astype(BF)
    mean = jnp.concatenate([mean, mean], axis=0)
    entered = []
    for p in range(pairs):
        ways = []
        for way in range(2):
            highs, lows = [], []
            for odd in range(2):
                packed = entry[4 * p + 2 * odd + way].astype(F32)
                mine = half_upper if odd == 0 else jnp.logical_not(half_upper)
                highs.append(jnp.where(mine, packed, 0.0).astype(BF))
                lows.append(jnp.where(mine, pltpu.roll(packed, HD, 1), 0.0).astype(BF))
            ways.append((jnp.concatenate(highs, axis=0), jnp.concatenate(lows, axis=0)))
        entered.append(ways)

    def nrm_copy(d):
        to = peer(d, 1)
        return pltpu.make_async_remote_copy(
            src_ref=normed.at[pl.ds(pl.multiple_of(to * rows, rows), rows), :],
            dst_ref=normed_in.at[(xs - d // 2) % xs, :, pl.ds(pl.multiple_of(c * width, PAIR), width)],
            send_sem=nrm_send.at[d], recv_sem=nrm_recv.at[d],
            device_id=(s, to), device_id_type=MESH,
        )

    own_normed = pltpu.make_async_copy(
        normed.at[pl.ds(pl.multiple_of(h * rows, rows), rows), :],
        normed_in.at[0, :, pl.ds(pl.multiple_of(c * width, PAIR), width)],
        own_sem.at[3],
    )

    def read_chip(dx):
        at_x = (x + dx) % xs
        at = pl.ds(pl.multiple_of(at_x * chip_rows, chip_rows), chip_rows)
        for p in range(pairs):
            highs, lows = [], []
            for way in range(2):
                high, low = entered[p][way]
                before = (at_x + xs - 1) % xs if way == 0 else (at_x + 1) % xs
                total = group[way, before, p]
                moved = jnp.where(own, 0.0, total) + dot(linear_of(total), triple(high, low, 0))
                edge = at_x == (0 if way == 0 else xs - 1)
                moved_high, moved_low = split(jnp.where(own, 0.0, moved))
                highs.append(jnp.where(edge, high, moved_high))
                lows.append(jnp.where(edge, low, moved_low))
            weight = jnp.concatenate([jnp.concatenate(highs, axis=0), jnp.concatenate(lows, axis=0)], axis=1)
            product = dot(q_high[p, at, :], weight)
            read = product[:, :PAIR] + product[:, PAIR:] + dot(q_low[p, at, :], weight[:, :PAIR]) + r_ref[p, at, :]
            high, low = split(read * read)
            mean_square = dot(jnp.concatenate([high, low], axis=1), mean)
            value = pltpu.roll(read * lax.rsqrt(mean_square + 1e-06), HD, 1)
            value = value * gain[p * PAIR:(p + 1) * PAIR]
            normed[at, p * PAIR:(p + 1) * PAIR] = value.astype(BF)

    def read_and_send(n):
        dx = near(xs - 1 - n)
        read_chip(dx)

        @pl.when(dx > 0)
        def _():
            nrm_copy(2 * dx).start()

        nrm_copy(2 * dx + 1).start()

    loop(0, xs, read_and_send)
    own_normed.start()

    for part in range(2):
        for d in (1, 3):
            w2_copy(part, d, 1).wait_recv()
            w2_copy(part, d, 2).wait_recv()
            sibling_band(part, d, 1 - passed[d], base).start()
    for part in range(2):
        for side_half in range(2):
            for i in range(1, xs):
                wd_copy(part, side_half, i).wait_recv()
            sibling_direct(part, side_half, base).start()
    for k in range(2):
        for part in range(2):
            for d in (1, 3):
                w3_copy(part, d, k).wait_recv()
                sibling_quarter(part, d, k, base).start()

    own_w.wait()
    sibling_own.wait_recv()
    own_normed.wait()
    for d in range(1, heads):
        nrm_copy(d).wait_recv()

    outgoing = []
    for k in range(2):
        if k == 0:
            for part in range(2):
                for d in (0, 1, 3):
                    for side_half in range(2):
                        sibling_band(part, d, side_half, width - base).wait_recv()
                for side_half in range(2):
                    sibling_direct(part, side_half, width - base).wait_recv()
        for part in range(2):
            for d in (1, 3):
                sibling_quarter(part, d, k, width - base).wait_recv()

        def project(side_half):
            at = pl.ds(pl.multiple_of((2 * side_half + k) * cols, PAIR), cols)
            total = dot(normed_in[0], whole[0, :, at])
            for i in range(1, xs):
                total = total + dot(normed_in[i], whole[i, :, at])
            mixed[2 * side_half + k] = total
            pltpu.make_async_copy(mixed.at[2 * side_half + k], out.at[:, at], out_sem.at[2 * side_half + k]).start()

        loop(0, 2, project)

    for j in range(side):
        pltpu.make_async_copy(mixed.at[j], out.at[:, pl.ds(j * cols, cols)], out_sem.at[j]).wait()

    for part in range(2):
        for i in range(1, xs):
            for k in range(2):
                wx_copy(part, i, k).wait_send()
                w1_copy(part, i, k).wait_send()
        for d in (1, 3):
            w2_copy(part, d, 0).wait_send()
            w2_copy(part, d, 1).wait_send()
            w2_copy(part, d, 2).wait_send()
            for k in range(2):
                w3_copy(part, d, k).wait_send()
                sibling_quarter(part, d, k, base).wait_send()
        for side_half in range(2):
            for i in range(1, xs):
                wd_copy(part, side_half, i).wait_send()
            sibling_direct(part, side_half, base).wait_send()
        for d in (0, 1, 3):
            for side_half in range(2):
                sibling_band(part, d, side_half, base).wait_send()
    sibling_own.wait_send()

    def drain_head(d):
        kv_copy(d).wait_send()
        q_copy(d).wait_send()
        nrm_copy(d).wait_send()

    def drain_total(k):
        @pl.when(chain_at(k) != s)
        def _():
            tot_copy(k).wait_send()

    loop(1, heads, drain_head)
    loop(0, chains, drain_total)

    @pl.when(is_owner)
    def _():
        def drain_fin(to):
            @pl.when(to != s)
            def _():
                fin_copy(my_chain, to).wait_send()

        loop(0, seqs, drain_fin)


def layer(qkv, eta, initial, gain, w_out, seqs, heads):
    rows = qkv.shape[1]
    width, columns = w_out.shape
    pairs = width // PAIR
    tokens = rows * heads
    batches = tokens // MB
    xs = heads // 2
    anywhere = pl.BlockSpec(memory_space=pltpu.HBM)
    dma = pltpu.SemaphoreType.DMA
    return pl.pallas_call(
        functools.partial(layer_kernel, seqs, heads, pairs),
        out_shape=jax.ShapeDtypeStruct((rows, columns), F32),
        in_specs=[anywhere] * 5,
        out_specs=anywhere,
        scratch_shapes=[
            pltpu.SMEM(eta.shape, F32),
            pltpu.VMEM(initial.shape, F32),
            pltpu.VMEM(gain.shape, F32),
            pltpu.VMEM((3, tokens, width), BF),
            pltpu.VMEM((batches // xs, pairs, PAIR, 2 * PAIR), BF),
            pltpu.VMEM((batches // xs, pairs, PAIR, PAIR), F32),
            pltpu.VMEM((2, batches, pairs, PAIR, PAIR), F32),
            pltpu.VMEM((2, xs, pairs, PAIR, PAIR), F32),
            pltpu.VMEM((4 * pairs, HD, PAIR), F32),
            pltpu.VMEM((seqs, HD, PAIR), F32),
            pltpu.VMEM((seqs, HD, PAIR), BF),
            pltpu.VMEM((4 * pairs, HD, PAIR), BF),
            pltpu.VMEM((pairs, tokens, 2 * PAIR), BF),
            pltpu.VMEM((pairs, tokens, 2 * PAIR), BF),
            pltpu.VMEM((pairs, tokens, PAIR), F32),
            pltpu.VMEM((tokens, width), BF),
            pltpu.VMEM((xs, rows, 2 * width), BF),
            pltpu.VMEM((xs, 2 * width, columns), BF),
            pltpu.VMEM((4, rows, columns // 4), F32),
            dma((3,)), dma((4,)),
            dma((heads,)), dma((heads,)), dma((heads,)), dma((heads,)),
            dma((4 * pairs,)), dma((seqs,)), dma((seqs,)), dma((4 * pairs,)),
            dma((heads,)), dma((heads,)),
            dma((2, 4, 2)), dma((2, 4, 2)), dma((2, 4, 2)), dma((2, 4, 2)), dma((2, 4, 3)), dma((2, 4, 3)),
            dma((2, 4, 2)), dma((2, 4, 2)), dma((3, 4, 2)), dma((3, 4, 2)), dma((2, 4, 2)), dma((2, 4, 2)),
            dma((4,)), dma((2, 2, 4)), dma((2, 2, 4)), dma((2, 2)), dma((2, 2)),
        ],
        compiler_params=pltpu.CompilerParams(
            collective_id=0, has_side_effects=True, vmem_limit_bytes=57 << 20
        ),
    )(qkv, eta, initial, gain, w_out)


def solution(mesh):
    seqs, heads = mesh.shape["seq"], mesh.shape["head"]

    def shards(qkv, eta, initial, gain, w_out):
        return layer(jnp.transpose(qkv, (1, 0, 2)), eta, initial, gain, w_out, seqs, heads)

    return jax.shard_map(
        shards,
        mesh=mesh,
        in_specs=(
            P(("seq", "head"), None, None),
            P("head"),
            P("head", None, None),
            P("head"),
            P("head", None),
        ),
        out_specs=P(("seq", "head"), None),
        check_vma=False,
    )
```

```python
import functools

import jax
import jax.numpy as jnp
from jax import lax
from jax.experimental import pallas as pl
from jax.experimental.pallas import tpu as pltpu
from jax.sharding import PartitionSpec as P

MESH = pl.DeviceIdType.MESH
MB = 64
HD = 64
PAIR = 2 * HD
BF = jnp.bfloat16
F32 = jnp.float32


def split(x):
    high = x.astype(BF)
    return high, (x - high.astype(F32)).astype(BF)


def dot(a, b):
    return lax.dot_general(a, b, (((1,), (0,)), ((), ())), preferred_element_type=F32)


def triple(high, low, axis):
    parts = [high, low, high] if axis == 1 else [high, high, low]
    return jnp.concatenate(parts, axis=axis)


def layer_kernel(
    seqs, heads, pairs,
    qkv, eta_hbm, initial_hbm, gain_hbm, w_hbm, out,
    eta, initial, gain, recv, a_ref, b_ref, pre, group, totals, inbox, outbox, entry,
    q_high, q_low, r_ref, normed, normed_in, whole, mixed,
    const_sem, own_sem, kv_send, kv_recv, q_send, q_recv, tot_send, tot_recv, fin_send, fin_recv, nrm_send, nrm_recv,
    wx_send, wx_recv, w1_send, w1_recv, w2_send, w2_recv, w3_send, w3_recv, sib_send, sib_recv, last_send, last_recv,
    plane, out_sem, wd_send, wd_recv, direct_send, direct_recv,
):
    s = lax.axis_index("seq")
    h = lax.axis_index("head")
    x, c = h // 2, h % 2
    xs = heads // 2
    side = 4
    z, y = s // side, s % side
    rows = qkv.shape[1]
    width = pairs * PAIR
    chip_rows = 2 * rows
    group_batches = chip_rows // MB
    chains = 4 * pairs

    barrier = pltpu.get_barrier_semaphore()

    def greet_head(d, _):
        pl.semaphore_signal(barrier, inc=1, device_id=(s, (h + d) % heads), device_id_type=MESH)
        return 0

    def greet_sides(d, _):
        pl.semaphore_signal(barrier, inc=1, device_id=(z * side + (y + d) % side, h), device_id_type=MESH)
        pl.semaphore_signal(barrier, inc=1, device_id=(((z + d) % side) * side + y, h), device_id_type=MESH)
        return 0

    lax.fori_loop(1, side, greet_sides, 0)
    lax.fori_loop(1, heads, greet_head, 0)

    constants = [
        pltpu.make_async_copy(eta_hbm, eta, const_sem.at[0]),
        pltpu.make_async_copy(initial_hbm, initial, const_sem.at[1]),
        pltpu.make_async_copy(gain_hbm, gain, const_sem.at[2]),
    ]
    for copy in constants:
        copy.start()

    def own_copy(first, count, sem):
        return pltpu.make_async_copy(
            qkv.at[pl.ds(first, count), :, pl.ds(pl.multiple_of(h * width, PAIR), width)],
            recv.at[pl.ds(first, count), pl.ds(pl.multiple_of(h * rows, rows), rows), :],
            sem,
        )

    own_kv = own_copy(1, 2, own_sem.at[0])
    own_q = own_copy(0, 1, own_sem.at[1])
    own_kv.start()
    own_q.start()
    base = c * width
    own_w = pltpu.make_async_copy(w_hbm, whole.at[0, pl.ds(pl.multiple_of(base, PAIR), width), :], own_sem.at[2])
    own_w.start()
    pl.semaphore_wait(barrier, heads - 1 + 2 * (side - 1))

    def tell(d, _):
        pl.semaphore_signal(plane, inc=1, device_id=(z * side + (y + d) % side, h), device_id_type=MESH)
        return 0

    lax.fori_loop(1, side, tell, 0)

    def peer(d, sign):
        dx, dc = d // 2, d % 2
        return ((x + sign * dx + xs) % xs) * 2 + (c + dc) % 2

    half = width // 2
    step = half // side
    cols = w_hbm.shape[1] // side

    def piece(part, first, last, second, k=0):
        at = part * half + last * step
        return (
            pl.ds(pl.multiple_of(first + at, 16), step),
            pl.ds(pl.multiple_of((2 * second + k) * (cols // 2), PAIR), cols // 2),
        )

    def wx_copy(part, i, k):
        last, second = (z, y) if part == 0 else (y, z)
        from_rows, at_cols = piece(part, 0, last, second, k)
        to_rows, _ = piece(part, base, last, second, k)
        return pltpu.make_async_remote_copy(
            src_ref=w_hbm.at[from_rows, at_cols],
            dst_ref=whole.at[i, to_rows, at_cols],
            send_sem=wx_send.at[part, i, k], recv_sem=wx_recv.at[part, i, k],
            device_id=(s, ((x + xs - i) % xs) * 2 + c), device_id_type=MESH,
        )

    def along(axis, d):
        return (z * side + (y + d) % side, h) if axis == 0 else (((z + d) % side) * side + y, h)

    def w1_copy(part, d, k):
        last, second = (z, y) if part == 0 else (y, z)
        at_rows, at_cols = piece(part, base, last, second, k)
        where = whole.at[pl.ds(1, xs - 1), at_rows, at_cols]
        return pltpu.make_async_remote_copy(
            src_ref=where, dst_ref=where,
            send_sem=w1_send.at[part, d, k], recv_sem=w1_recv.at[part, d, k],
            device_id=along(part, d), device_id_type=MESH,
        )

    def band(part, d, side_half, core_base):
        last = z if part == 0 else y
        at_rows, _ = piece(part, core_base, (last + side - d) % side, 0)
        return whole.at[pl.ds(1, xs - 1), at_rows, pl.ds(side_half * 2 * cols, 2 * cols)]

    passed = {1: 0, 3: 1}

    def w2_copy(part, d, order):
        if order == 0:
            where = band(part, 0, passed[d], base)
        else:
            at_rows, _ = piece(part, base, z if part == 0 else y, 0)
            at_cols = pl.ds((2 * (1 - passed[d]) + order - 1) * cols, cols)
            where = whole.at[pl.ds(1, xs - 1), at_rows, at_cols]
        return pltpu.make_async_remote_copy(
            src_ref=where, dst_ref=where,
            send_sem=w2_send.at[part, d, order], recv_sem=w2_recv.at[part, d, order],
            device_id=along(1 - part, d), device_id_type=MESH,
        )

    def quarter(part, d, side_half, k, core_base):
        last = z if part == 0 else y
        at_rows, _ = piece(part, core_base, (last + side - d) % side, 0)
        at_cols = pl.ds((2 * side_half + k) * cols, cols if k == 0 else cols // 3)
        return whole.at[pl.ds(1, xs - 1), at_rows, at_cols]

    def left_over(part, side_half, core_base):
        last = z if part == 0 else y
        at_rows, _ = piece(part, core_base, (last + 2) % side, 0)
        return at_rows, pl.ds((2 * side_half + 1) * cols + cols // 3, cols - cols // 3)

    def wd_copy(part, side_half, i):
        from_rows, at_cols = left_over(part, side_half, 0)
        to_rows, _ = left_over(part, side_half, base)
        return pltpu.make_async_remote_copy(
            src_ref=w_hbm.at[from_rows, at_cols],
            dst_ref=whole.at[i, to_rows, at_cols],
            send_sem=wd_send.at[part, side_half, i], recv_sem=wd_recv.at[part, side_half, i],
            device_id=(s, ((x + xs - i) % xs) * 2 + c), device_id_type=MESH,
        )

    def w3_copy(part, d, k):
        where = quarter(part, d, passed[d], k, base)
        return pltpu.make_async_remote_copy(
            src_ref=where, dst_ref=where,
            send_sem=w3_send.at[part, d, k], recv_sem=w3_recv.at[part, d, k],
            device_id=along(1 - part, d), device_id_type=MESH,
        )

    sibling = (s, x * 2 + 1 - c)

    def sibling_band(part, d, side_half, core_base):
        where = band(part, d, side_half, core_base)
        return pltpu.make_async_remote_copy(
            src_ref=where, dst_ref=where,
            send_sem=sib_send.at[part, d, side_half], recv_sem=sib_recv.at[part, d, side_half],
            device_id=sibling, device_id_type=MESH,
        )

    def sibling_quarter(part, d, k, core_base):
        where = quarter(part, 2, passed[d], k, core_base)
        return pltpu.make_async_remote_copy(
            src_ref=where, dst_ref=where,
            send_sem=last_send.at[part, d, k], recv_sem=last_recv.at[part, d, k],
            device_id=sibling, device_id_type=MESH,
        )

    def sibling_direct(part, side_half, core_base):
        at_rows, at_cols = left_over(part, side_half, core_base)
        where = whole.at[pl.ds(1, xs - 1), at_rows, at_cols]
        return pltpu.make_async_remote_copy(
            src_ref=where, dst_ref=where,
            send_sem=direct_send.at[part, side_half], recv_sem=direct_recv.at[part, side_half],
            device_id=sibling, device_id_type=MESH,
        )

    sibling_own = pltpu.make_async_remote_copy(
        src_ref=w_hbm, dst_ref=whole.at[0, pl.ds(pl.multiple_of(base, PAIR), width), :],
        send_sem=sib_send.at[2, 0, 0], recv_sem=sib_recv.at[2, 0, 0],
        device_id=sibling, device_id_type=MESH,
    )

    def kv_copy(d):
        to = peer(d, 1)
        return pltpu.make_async_remote_copy(
            src_ref=qkv.at[pl.ds(1, 2), :, pl.ds(pl.multiple_of(to * width, PAIR), width)],
            dst_ref=recv.at[pl.ds(1, 2), pl.ds(pl.multiple_of(h * rows, rows), rows), :],
            send_sem=kv_send.at[d], recv_sem=kv_recv.at[d],
            device_id=(s, to), device_id_type=MESH,
        )

    def q_copy(d):
        to = peer(d, 1)
        return pltpu.make_async_remote_copy(
            src_ref=qkv.at[pl.ds(0, 1), :, pl.ds(pl.multiple_of(to * width, PAIR), width)],
            dst_ref=recv.at[pl.ds(0, 1), pl.ds(pl.multiple_of(h * rows, rows), rows), :],
            send_sem=q_send.at[d], recv_sem=q_recv.at[d],
            device_id=(s, to), device_id_type=MESH,
        )

    def loop(first, last, act):
        def run(i, _):
            act(i)
            return 0

        lax.fori_loop(first, last, run, 0)

    kv_copy(1).start()
    for k in range(2):
        for part in range(2):
            for i in (2, 1, 3):
                wx_copy(part, i, k).start()
    q_copy(1).start()
    kv_copy(2).start()
    kv_copy(3).start()
    kv_copy(6).start()
    kv_copy(7).start()
    kv_copy(4).start()
    kv_copy(5).start()

    def near(i):
        return jnp.where(i < 2, i, xs + 1 - i)

    row = lax.broadcasted_iota(jnp.int32, (PAIR, PAIR), 0)
    lane = lax.broadcasted_iota(jnp.int32, (PAIR, PAIR), 1)
    own = (row >= HD) == (lane >= HD)
    eye = jnp.where(row == lane, 1.0, 0.0).astype(F32)

    for copy in constants:
        copy.wait()

    own_kv.wait()
    rates = [jnp.where(row < HD, eta[2 * p], eta[2 * p + 1]) for p in range(pairs)]

    def chip_maps(n):
        dx = near(n)
        at_x = (x + xs - dx) % xs

        @pl.when(n > 0)
        def _():
            kv_copy(2 * dx).wait_recv()

        kv_copy(2 * dx + 1).wait_recv()

        @pl.when(n == 1)
        def _():
            q_copy(4).start()
            q_copy(5).start()
            q_copy(2).start()
            q_copy(3).start()
            q_copy(6).start()
            q_copy(7).start()
            for part in range(2):
                for side_half in range(2):
                    for i in (2, 1, 3):
                        wd_copy(part, side_half, i).start()


        first = {}
        for i in range(group_batches):
            at = pl.ds(pl.multiple_of(at_x * chip_rows + i * MB, MB), MB)
            for p in range(pairs):
                lanes = slice(p * PAIR, (p + 1) * PAIR)
                keys = recv[1, at, lanes]
                values = recv[2, at, lanes]
                swapped = pltpu.roll(values.astype(F32), HD, 1).astype(BF)
                both = lax.dot_general(
                    keys, jnp.concatenate([keys, swapped], axis=1),
                    (((0,), (0,)), ((), ())), preferred_element_type=F32,
                )
                linear = jnp.where(own, rates[p] * both[:, :PAIR], 0.0)
                offset = jnp.where(own, 0.0, rates[p] * both[:, PAIR:])
                high, low = split(linear)
                a_ref[i, p, :, :PAIR] = high
                a_ref[i, p, :, PAIR:] = low
                b_ref[i, p] = offset
                if i in (0, group_batches - 1):
                    first[i, p] = eye - linear + offset
        base_batch = at_x * group_batches
        states = {}
        for p in range(pairs):
            for way in range(2):
                i = 0 if way == 0 else group_batches - 1
                states[way, p] = first[i, p]
                pre[way, base_batch + i, p] = first[i, p]
        for t in range(1, group_batches):
            for p in range(pairs):
                for way in range(2):
                    i = t if way == 0 else group_batches - 1 - t
                    state = states[way, p]
                    high, low = split(state)
                    a = a_ref[i, p]
                    change = dot(jnp.concatenate([a, a[:, :PAIR]], axis=1), triple(high, low, 0))
                    states[way, p] = state + b_ref[i, p] - change
                    pre[way, base_batch + i, p] = states[way, p]

        @pl.when(n == 0)
        def _():
            for k in range(2):
                for part in range(2):
                    for i in range(1, xs):
                        wx_copy(part, i, k).wait_recv()
                    for d in (2, 1, 3):
                        w1_copy(part, d, k).start()
            sibling_own.start()
            for part in range(2):
                for d in (1, 2, 3):
                    for k in range(2):
                        w1_copy(part, d, k).wait_recv()
                for d in (1, 3):
                    w2_copy(part, d, 0).start()
            for part in range(2):
                for side_half in range(2):
                    sibling_band(part, 0, side_half, base).start()

    loop(0, xs, chip_maps)

    def linear_of(total):
        return triple(*split(jnp.where(own, total, 0.0)), 1)

    states = {}
    for t in range(xs):
        for p in range(pairs):
            for way in range(2):
                g = t if way == 0 else xs - 1 - t
                b = (g + 1) * group_batches - 1 if way == 0 else g * group_batches
                total = pre[way, b, p]
                if t:
                    change = dot(linear_of(total), triple(*split(states[way, p]), 0))
                    total = jnp.where(own, 0.0, total) + change
                states[way, p] = total
                group[way, g, p] = total
    for way in range(2):
        for p in range(pairs):
            totals[4 * p + way] = states[way, p][:HD]
            totals[4 * p + 2 + way] = states[way, p][HD:]

    shift = c * (seqs // 2)
    my_chain = (s + seqs - shift) % seqs
    is_owner = my_chain < chains

    def chain_at(k):
        return (k + shift) % seqs

    def tot_copy(k):
        return pltpu.make_async_remote_copy(
            src_ref=totals.at[k], dst_ref=inbox.at[s],
            send_sem=tot_send.at[k], recv_sem=tot_recv.at[s],
            device_id=(chain_at(k), h), device_id_type=MESH,
        )

    def tot_arrival(source):
        return pltpu.make_async_remote_copy(
            src_ref=totals.at[0], dst_ref=inbox.at[source],
            send_sem=tot_send.at[0], recv_sem=tot_recv.at[source],
            device_id=((s + 1) % seqs, h), device_id_type=MESH,
        )

    def send_total(d):
        k = (my_chain + d) % seqs

        @pl.when(k < chains)
        def _():
            tot_copy(k).start()

    pl.semaphore_wait(plane, side - 1)
    loop(1, seqs, send_total)

    for part in range(2):
        for d in (1, 3):
            w2_copy(part, d, 1).start()


    def fin_copy(k, to):
        return pltpu.make_async_remote_copy(
            src_ref=outbox.at[to], dst_ref=entry.at[k],
            send_sem=fin_send.at[to], recv_sem=fin_recv.at[k],
            device_id=(to, h), device_id_type=MESH,
        )

    def multiply_queries(dx):
        at_x = (x + xs - dx) % xs

        @pl.when(dx > 0)
        def _():
            q_copy(2 * dx).wait_recv()

        q_copy(2 * dx + 1).wait_recv()

        def one(i):
            b = at_x * group_batches + i
            at = pl.ds(pl.multiple_of(b * MB, MB), MB)
            for p in range(pairs):
                query = recv[0, at, p * PAIR:(p + 1) * PAIR]
                ahead, behind = pre[0, b, p], pre[1, b, p]
                high, low = split(jnp.concatenate(
                    [jnp.where(own, ahead, 0.0), jnp.where(own, behind, 0.0), jnp.where(own, 0.0, ahead + behind)],
                    axis=1,
                ))
                product = dot(jnp.concatenate([query, query], axis=1), jnp.concatenate([high, low], axis=0))
                high, low = split(product[:, :2 * PAIR])
                q_high[p, at, :] = high
                q_low[p, at, :] = low
                r_ref[p, at, :] = product[:, 2 * PAIR:]

        loop(0, group_batches, one)

    own_q.wait()
    loop(0, xs - 1, lambda n: multiply_queries(near(n)))

    @pl.when(is_owner)
    def _():
        inbox[s] = totals[my_chain]
        way = my_chain % 2
        number = my_chain // 2
        odd = number % 2
        half_lane = lax.broadcasted_iota(jnp.int32, (HD, PAIR), 1)
        mine = half_lane // HD != odd
        start = initial[number]

        def place(t):
            return jnp.where(way == 0, t, seqs - 1 - t)

        def arrive(source):
            @pl.when(source != s)
            def _():
                tot_arrival(source).wait_recv()

        loop(0, seqs, arrive)

        def apply(total, high, low):
            linear_high, linear_low = split(jnp.where(mine, 0.0, total))
            return jnp.where(mine, total, 0.0) + dot(
                triple(linear_high, linear_low, 1),
                jnp.concatenate([high, high, high, high, low, low], axis=0),
            )

        def emit(t, state):
            high, low = split(state)
            outbox[place(t)] = (high.astype(F32) + pltpu.roll(low.astype(F32), HD, 1)).astype(BF)

        quads = seqs // side
        maps = [[None] * side for _ in range(quads)]
        for j in range(side):
            for g in range(quads):
                total = inbox[place(g * side + j)]
                maps[g][j] = total if j == 0 else apply(total, *split(maps[g][j - 1]))
        state = jnp.where(mine, jnp.concatenate([start, start], axis=1), 0.0)
        states = [state]
        for g in range(quads - 1):
            states.append(jnp.where(mine, apply(maps[g][side - 1], *split(states[-1])), 0.0))
        for g in range(quads):
            emit(g * side, states[g])
            parts = split(states[g])
            for j in range(side - 1):
                emit(g * side + j + 1, jnp.where(mine, apply(maps[g][j], *parts), 0.0))

        entry[my_chain] = outbox[s]
        loop(1, seqs, lambda d: fin_copy(my_chain, (s + d) % seqs).start())

    multiply_queries(jnp.int32(xs // 2))

    for part in range(2):
        for d in (1, 3):
            w2_copy(part, d, 2).start()

    for part in range(2):
        for d in (1, 3):
            w2_copy(part, d, 0).wait_recv()
            w3_copy(part, d, 0).start()
    for part in range(2):
        for d in (1, 3):
            w3_copy(part, d, 1).start()
    for part in range(2):
        for d in (1, 3):
            sibling_band(part, d, passed[d], base).start()

    def wait_entry(k):
        @pl.when(chain_at(k) != s)
        def _():
            fin_copy(k, (s + 1) % seqs).wait_recv()

    loop(0, chains, wait_entry)

    half_upper = lax.broadcasted_iota(jnp.int32, (HD, PAIR), 1) >= HD
    mean = jnp.where(own, 1.0 / HD, 0.0).astype(BF)
    mean = jnp.concatenate([mean, mean], axis=0)
    entered = []
    for p in range(pairs):
        ways = []
        for way in range(2):
            highs, lows = [], []
            for odd in range(2):
                packed = entry[4 * p + 2 * odd + way].astype(F32)
                mine = half_upper if odd == 0 else jnp.logical_not(half_upper)
                highs.append(jnp.where(mine, packed, 0.0).astype(BF))
                lows.append(jnp.where(mine, pltpu.roll(packed, HD, 1), 0.0).astype(BF))
            ways.append((jnp.concatenate(highs, axis=0), jnp.concatenate(lows, axis=0)))
        entered.append(ways)

    def nrm_copy(d):
        to = peer(d, 1)
        return pltpu.make_async_remote_copy(
            src_ref=normed.at[pl.ds(pl.multiple_of(to * rows, rows), rows), :],
            dst_ref=normed_in.at[(xs - d // 2) % xs, :, pl.ds(pl.multiple_of(c * width, PAIR), width)],
            send_sem=nrm_send.at[d], recv_sem=nrm_recv.at[d],
            device_id=(s, to), device_id_type=MESH,
        )

    own_normed = pltpu.make_async_copy(
        normed.at[pl.ds(pl.multiple_of(h * rows, rows), rows), :],
        normed_in.at[0, :, pl.ds(pl.multiple_of(c * width, PAIR), width)],
        own_sem.at[3],
    )

    def read_chip(dx):
        at_x = (x + dx) % xs
        at = pl.ds(pl.multiple_of(at_x * chip_rows, chip_rows), chip_rows)
        for p in range(pairs):
            highs, lows = [], []
            for way in range(2):
                high, low = entered[p][way]
                before = (at_x + xs - 1) % xs if way == 0 else (at_x + 1) % xs
                total = group[way, before, p]
                moved = jnp.where(own, 0.0, total) + dot(linear_of(total), triple(high, low, 0))
                edge = at_x == (0 if way == 0 else xs - 1)
                moved_high, moved_low = split(jnp.where(own, 0.0, moved))
                highs.append(jnp.where(edge, high, moved_high))
                lows.append(jnp.where(edge, low, moved_low))
            weight = jnp.concatenate([jnp.concatenate(highs, axis=0), jnp.concatenate(lows, axis=0)], axis=1)
            product = dot(q_high[p, at, :], weight)
            read = product[:, :PAIR] + product[:, PAIR:] + dot(q_low[p, at, :], weight[:, :PAIR]) + r_ref[p, at, :]
            high, low = split(read * read)
            mean_square = dot(jnp.concatenate([high, low], axis=1), mean)
            value = pltpu.roll(read * lax.rsqrt(mean_square + 1e-06), HD, 1)
            value = value * gain[p * PAIR:(p + 1) * PAIR]
            normed[at, p * PAIR:(p + 1) * PAIR] = value.astype(BF)

    def read_and_send(n):
        dx = near(xs - 1 - n)
        read_chip(dx)

        @pl.when(dx > 0)
        def _():
            nrm_copy(2 * dx).start()

        nrm_copy(2 * dx + 1).start()

    loop(0, xs, read_and_send)
    own_normed.start()

    for part in range(2):
        for d in (1, 3):
            w2_copy(part, d, 1).wait_recv()
            w2_copy(part, d, 2).wait_recv()
            sibling_band(part, d, 1 - passed[d], base).start()
    for part in range(2):
        for side_half in range(2):
            for i in range(1, xs):
                wd_copy(part, side_half, i).wait_recv()
            sibling_direct(part, side_half, base).start()
    for k in range(2):
        for part in range(2):
            for d in (1, 3):
                w3_copy(part, d, k).wait_recv()
                sibling_quarter(part, d, k, base).start()

    own_w.wait()
    sibling_own.wait_recv()
    own_normed.wait()
    nrm_copy(1).wait_recv()

    def project_own(j):
        mixed[j] = dot(normed_in[0], whole[0, :, pl.ds(pl.multiple_of(j * cols, PAIR), cols)])

    loop(0, side, project_own)
    for d in range(2, heads):
        nrm_copy(d).wait_recv()

    outgoing = []
    for k in range(2):
        if k == 0:
            for part in range(2):
                for d in (0, 1, 3):
                    for side_half in range(2):
                        sibling_band(part, d, side_half, width - base).wait_recv()
                for side_half in range(2):
                    sibling_direct(part, side_half, width - base).wait_recv()
        for part in range(2):
            for d in (1, 3):
                sibling_quarter(part, d, k, width - base).wait_recv()

        def project(side_half):
            at = pl.ds(pl.multiple_of((2 * side_half + k) * cols, PAIR), cols)
            total = mixed[2 * side_half + k]
            for i in range(1, xs):
                total = total + dot(normed_in[i], whole[i, :, at])
            mixed[2 * side_half + k] = total
            pltpu.make_async_copy(mixed.at[2 * side_half + k], out.at[:, at], out_sem.at[2 * side_half + k]).start()

        loop(0, 2, project)

    for j in range(side):
        pltpu.make_async_copy(mixed.at[j], out.at[:, pl.ds(j * cols, cols)], out_sem.at[j]).wait()

    for part in range(2):
        for i in range(1, xs):
            for k in range(2):
                wx_copy(part, i, k).wait_send()
                w1_copy(part, i, k).wait_send()
        for d in (1, 3):
            w2_copy(part, d, 0).wait_send()
            w2_copy(part, d, 1).wait_send()
            w2_copy(part, d, 2).wait_send()
            for k in range(2):
                w3_copy(part, d, k).wait_send()
                sibling_quarter(part, d, k, base).wait_send()
        for side_half in range(2):
            for i in range(1, xs):
                wd_copy(part, side_half, i).wait_send()
            sibling_direct(part, side_half, base).wait_send()
        for d in (0, 1, 3):
            for side_half in range(2):
                sibling_band(part, d, side_half, base).wait_send()
    sibling_own.wait_send()

    def drain_head(d):
        kv_copy(d).wait_send()
        q_copy(d).wait_send()
        nrm_copy(d).wait_send()

    def drain_total(k):
        @pl.when(chain_at(k) != s)
        def _():
            tot_copy(k).wait_send()

    loop(1, heads, drain_head)
    loop(0, chains, drain_total)

    @pl.when(is_owner)
    def _():
        def drain_fin(to):
            @pl.when(to != s)
            def _():
                fin_copy(my_chain, to).wait_send()

        loop(0, seqs, drain_fin)


def layer(qkv, eta, initial, gain, w_out, seqs, heads):
    rows = qkv.shape[1]
    width, columns = w_out.shape
    pairs = width // PAIR
    tokens = rows * heads
    batches = tokens // MB
    xs = heads // 2
    anywhere = pl.BlockSpec(memory_space=pltpu.HBM)
    dma = pltpu.SemaphoreType.DMA
    return pl.pallas_call(
        functools.partial(layer_kernel, seqs, heads, pairs),
        out_shape=jax.ShapeDtypeStruct((rows, columns), F32),
        in_specs=[anywhere] * 5,
        out_specs=anywhere,
        scratch_shapes=[
            pltpu.SMEM(eta.shape, F32),
            pltpu.VMEM(initial.shape, F32),
            pltpu.VMEM(gain.shape, F32),
            pltpu.VMEM((3, tokens, width), BF),
            pltpu.VMEM((batches // xs, pairs, PAIR, 2 * PAIR), BF),
            pltpu.VMEM((batches // xs, pairs, PAIR, PAIR), F32),
            pltpu.VMEM((2, batches, pairs, PAIR, PAIR), F32),
            pltpu.VMEM((2, xs, pairs, PAIR, PAIR), F32),
            pltpu.VMEM((4 * pairs, HD, PAIR), F32),
            pltpu.VMEM((seqs, HD, PAIR), F32),
            pltpu.VMEM((seqs, HD, PAIR), BF),
            pltpu.VMEM((4 * pairs, HD, PAIR), BF),
            pltpu.VMEM((pairs, tokens, 2 * PAIR), BF),
            pltpu.VMEM((pairs, tokens, 2 * PAIR), BF),
            pltpu.VMEM((pairs, tokens, PAIR), F32),
            pltpu.VMEM((tokens, width), BF),
            pltpu.VMEM((xs, rows, 2 * width), BF),
            pltpu.VMEM((xs, 2 * width, columns), BF),
            pltpu.VMEM((4, rows, columns // 4), F32),
            dma((3,)), dma((4,)),
            dma((heads,)), dma((heads,)), dma((heads,)), dma((heads,)),
            dma((4 * pairs,)), dma((seqs,)), dma((seqs,)), dma((4 * pairs,)),
            dma((heads,)), dma((heads,)),
            dma((2, 4, 2)), dma((2, 4, 2)), dma((2, 4, 2)), dma((2, 4, 2)), dma((2, 4, 3)), dma((2, 4, 3)),
            dma((2, 4, 2)), dma((2, 4, 2)), dma((3, 4, 2)), dma((3, 4, 2)), dma((2, 4, 2)), dma((2, 4, 2)),
            pltpu.SemaphoreType.REGULAR, dma((4,)), dma((2, 2, 4)), dma((2, 2, 4)), dma((2, 2)), dma((2, 2)),
        ],
        compiler_params=pltpu.CompilerParams(
            collective_id=0, has_side_effects=True, vmem_limit_bytes=57 << 20
        ),
    )(qkv, eta, initial, gain, w_out)


def solution(mesh):
    seqs, heads = mesh.shape["seq"], mesh.shape["head"]

    def shards(qkv, eta, initial, gain, w_out):
        return layer(jnp.transpose(qkv, (1, 0, 2)), eta, initial, gain, w_out, seqs, heads)

    return jax.shard_map(
        shards,
        mesh=mesh,
        in_specs=(
            P(("seq", "head"), None, None),
            P("head"),
            P("head", None, None),
            P("head"),
            P("head", None),
        ),
        out_specs=P(("seq", "head"), None),
        check_vma=False,
    )
```

```python
import functools

import jax
import jax.numpy as jnp
from jax import lax
from jax.experimental import pallas as pl
from jax.experimental.pallas import tpu as pltpu
from jax.sharding import PartitionSpec as P

MESH = pl.DeviceIdType.MESH
MB = 64
HD = 64
PAIR = 2 * HD
BF = jnp.bfloat16
F32 = jnp.float32


def split(x):
    high = x.astype(BF)
    return high, (x - high.astype(F32)).astype(BF)


def dot(a, b):
    return lax.dot_general(a, b, (((1,), (0,)), ((), ())), preferred_element_type=F32)


def triple(high, low, axis):
    parts = [high, low, high] if axis == 1 else [high, high, low]
    return jnp.concatenate(parts, axis=axis)


def layer_kernel(
    seqs, heads, pairs,
    qkv, eta_hbm, initial_hbm, gain_hbm, w_hbm, out,
    eta, initial, gain, recv, a_ref, b_ref, pre, group, totals, inbox, outbox, entry,
    q_high, q_low, r_ref, normed, normed_in, whole, mixed,
    const_sem, own_sem, kv_send, kv_recv, q_send, q_recv, tot_send, tot_recv, fin_send, fin_recv, nrm_send, nrm_recv,
    wx_send, wx_recv, w1_send, w1_recv, w2_send, w2_recv, w3_send, w3_recv, sib_send, sib_recv, last_send, last_recv,
    plane, out_sem, wd_send, wd_recv, direct_send, direct_recv,
):
    s = lax.axis_index("seq")
    h = lax.axis_index("head")
    x, c = h // 2, h % 2
    xs = heads // 2
    side = 4
    z, y = s // side, s % side
    rows = qkv.shape[1]
    width = pairs * PAIR
    chip_rows = 2 * rows
    group_batches = chip_rows // MB
    chains = 4 * pairs

    barrier = pltpu.get_barrier_semaphore()

    def greet_head(d, _):
        pl.semaphore_signal(barrier, inc=1, device_id=(s, (h + d) % heads), device_id_type=MESH)
        return 0

    def greet_sides(d, _):
        pl.semaphore_signal(barrier, inc=1, device_id=(z * side + (y + d) % side, h), device_id_type=MESH)
        pl.semaphore_signal(barrier, inc=1, device_id=(((z + d) % side) * side + y, h), device_id_type=MESH)
        return 0

    lax.fori_loop(1, side, greet_sides, 0)
    lax.fori_loop(1, heads, greet_head, 0)

    constants = [
        pltpu.make_async_copy(eta_hbm, eta, const_sem.at[0]),
        pltpu.make_async_copy(initial_hbm, initial, const_sem.at[1]),
        pltpu.make_async_copy(gain_hbm, gain, const_sem.at[2]),
    ]
    for copy in constants:
        copy.start()

    def own_copy(first, count, sem):
        return pltpu.make_async_copy(
            qkv.at[pl.ds(first, count), :, pl.ds(pl.multiple_of(h * width, PAIR), width)],
            recv.at[pl.ds(first, count), pl.ds(pl.multiple_of(h * rows, rows), rows), :],
            sem,
        )

    own_kv = own_copy(1, 2, own_sem.at[0])
    own_q = own_copy(0, 1, own_sem.at[1])
    own_kv.start()
    own_q.start()
    base = c * width
    own_w = pltpu.make_async_copy(w_hbm, whole.at[0, pl.ds(pl.multiple_of(base, PAIR), width), :], own_sem.at[2])
    own_w.start()
    pl.semaphore_wait(barrier, heads - 1 + 2 * (side - 1))

    def tell(d, _):
        pl.semaphore_signal(plane, inc=1, device_id=(z * side + (y + d) % side, h), device_id_type=MESH)
        return 0

    lax.fori_loop(1, side, tell, 0)

    def peer(d, sign):
        dx, dc = d // 2, d % 2
        return ((x + sign * dx + xs) % xs) * 2 + (c + dc) % 2

    half = width // 2
    step = half // side
    cols = w_hbm.shape[1] // side

    def piece(part, first, last, second, k=0):
        at = part * half + last * step
        return (
            pl.ds(pl.multiple_of(first + at, 16), step),
            pl.ds(pl.multiple_of((2 * second + k) * (cols // 2), PAIR), cols // 2),
        )

    def wx_copy(part, i, k):
        last, second = (z, y) if part == 0 else (y, z)
        from_rows, at_cols = piece(part, 0, last, second, k)
        to_rows, _ = piece(part, base, last, second, k)
        return pltpu.make_async_remote_copy(
            src_ref=w_hbm.at[from_rows, at_cols],
            dst_ref=whole.at[i, to_rows, at_cols],
            send_sem=wx_send.at[part, i, k], recv_sem=wx_recv.at[part, i, k],
            device_id=(s, ((x + xs - i) % xs) * 2 + c), device_id_type=MESH,
        )

    def along(axis, d):
        return (z * side + (y + d) % side, h) if axis == 0 else (((z + d) % side) * side + y, h)

    def w1_copy(part, d, k):
        last, second = (z, y) if part == 0 else (y, z)
        at_rows, at_cols = piece(part, base, last, second, k)
        where = whole.at[pl.ds(1, xs - 1), at_rows, at_cols]
        return pltpu.make_async_remote_copy(
            src_ref=where, dst_ref=where,
            send_sem=w1_send.at[part, d, k], recv_sem=w1_recv.at[part, d, k],
            device_id=along(part, d), device_id_type=MESH,
        )

    def band(part, d, side_half, core_base):
        last = z if part == 0 else y
        at_rows, _ = piece(part, core_base, (last + side - d) % side, 0)
        return whole.at[pl.ds(1, xs - 1), at_rows, pl.ds(side_half * 2 * cols, 2 * cols)]

    passed = {1: 0, 3: 1}

    def w2_copy(part, d, order):
        if order == 0:
            where = band(part, 0, passed[d], base)
        else:
            at_rows, _ = piece(part, base, z if part == 0 else y, 0)
            at_cols = pl.ds((2 * (1 - passed[d]) + order - 1) * cols, cols)
            where = whole.at[pl.ds(1, xs - 1), at_rows, at_cols]
        return pltpu.make_async_remote_copy(
            src_ref=where, dst_ref=where,
            send_sem=w2_send.at[part, d, order], recv_sem=w2_recv.at[part, d, order],
            device_id=along(1 - part, d), device_id_type=MESH,
        )

    def quarter(part, d, side_half, k, core_base):
        last = z if part == 0 else y
        at_rows, _ = piece(part, core_base, (last + side - d) % side, 0)
        at_cols = pl.ds((2 * side_half + k) * cols, cols if k == 0 else cols // 3)
        return whole.at[pl.ds(1, xs - 1), at_rows, at_cols]

    def left_over(part, side_half, core_base):
        last = z if part == 0 else y
        at_rows, _ = piece(part, core_base, (last + 2) % side, 0)
        return at_rows, pl.ds((2 * side_half + 1) * cols + cols // 3, cols - cols // 3)

    def wd_copy(part, side_half, i):
        from_rows, at_cols = left_over(part, side_half, 0)
        to_rows, _ = left_over(part, side_half, base)
        return pltpu.make_async_remote_copy(
            src_ref=w_hbm.at[from_rows, at_cols],
            dst_ref=whole.at[i, to_rows, at_cols],
            send_sem=wd_send.at[part, side_half, i], recv_sem=wd_recv.at[part, side_half, i],
            device_id=(s, ((x + xs - i) % xs) * 2 + c), device_id_type=MESH,
        )

    def w3_copy(part, d, k):
        where = quarter(part, d, passed[d], k, base)
        return pltpu.make_async_remote_copy(
            src_ref=where, dst_ref=where,
            send_sem=w3_send.at[part, d, k], recv_sem=w3_recv.at[part, d, k],
            device_id=along(1 - part, d), device_id_type=MESH,
        )

    sibling = (s, x * 2 + 1 - c)

    def sibling_band(part, d, side_half, core_base):
        where = band(part, d, side_half, core_base)
        return pltpu.make_async_remote_copy(
            src_ref=where, dst_ref=where,
            send_sem=sib_send.at[part, d, side_half], recv_sem=sib_recv.at[part, d, side_half],
            device_id=sibling, device_id_type=MESH,
        )

    def sibling_quarter(part, d, k, core_base):
        where = quarter(part, 2, passed[d], k, core_base)
        return pltpu.make_async_remote_copy(
            src_ref=where, dst_ref=where,
            send_sem=last_send.at[part, d, k], recv_sem=last_recv.at[part, d, k],
            device_id=sibling, device_id_type=MESH,
        )

    def sibling_direct(part, side_half, core_base):
        at_rows, at_cols = left_over(part, side_half, core_base)
        where = whole.at[pl.ds(1, xs - 1), at_rows, at_cols]
        return pltpu.make_async_remote_copy(
            src_ref=where, dst_ref=where,
            send_sem=direct_send.at[part, side_half], recv_sem=direct_recv.at[part, side_half],
            device_id=sibling, device_id_type=MESH,
        )

    sibling_own = pltpu.make_async_remote_copy(
        src_ref=w_hbm, dst_ref=whole.at[0, pl.ds(pl.multiple_of(base, PAIR), width), :],
        send_sem=sib_send.at[2, 0, 0], recv_sem=sib_recv.at[2, 0, 0],
        device_id=sibling, device_id_type=MESH,
    )

    def kv_copy(d):
        to = peer(d, 1)
        return pltpu.make_async_remote_copy(
            src_ref=qkv.at[pl.ds(1, 2), :, pl.ds(pl.multiple_of(to * width, PAIR), width)],
            dst_ref=recv.at[pl.ds(1, 2), pl.ds(pl.multiple_of(h * rows, rows), rows), :],
            send_sem=kv_send.at[d], recv_sem=kv_recv.at[d],
            device_id=(s, to), device_id_type=MESH,
        )

    def q_copy(d):
        to = peer(d, 1)
        return pltpu.make_async_remote_copy(
            src_ref=qkv.at[pl.ds(0, 1), :, pl.ds(pl.multiple_of(to * width, PAIR), width)],
            dst_ref=recv.at[pl.ds(0, 1), pl.ds(pl.multiple_of(h * rows, rows), rows), :],
            send_sem=q_send.at[d], recv_sem=q_recv.at[d],
            device_id=(s, to), device_id_type=MESH,
        )

    def loop(first, last, act):
        def run(i, _):
            act(i)
            return 0

        lax.fori_loop(first, last, run, 0)

    kv_copy(1).start()
    for k in range(2):
        for part in range(2):
            for i in (2, 1, 3):
                wx_copy(part, i, k).start()
    q_copy(1).start()
    kv_copy(2).start()
    kv_copy(3).start()
    kv_copy(6).start()
    kv_copy(7).start()
    kv_copy(4).start()
    kv_copy(5).start()

    def near(i):
        return jnp.where(i < 2, i, xs + 1 - i)

    row = lax.broadcasted_iota(jnp.int32, (PAIR, PAIR), 0)
    lane = lax.broadcasted_iota(jnp.int32, (PAIR, PAIR), 1)
    own = (row >= HD) == (lane >= HD)
    eye = jnp.where(row == lane, 1.0, 0.0).astype(F32)

    for copy in constants:
        copy.wait()

    own_kv.wait()
    rates = [jnp.where(row < HD, eta[2 * p], eta[2 * p + 1]) for p in range(pairs)]

    def chip_maps(n):
        dx = near(n)
        at_x = (x + xs - dx) % xs

        @pl.when(n > 0)
        def _():
            kv_copy(2 * dx).wait_recv()

        kv_copy(2 * dx + 1).wait_recv()

        @pl.when(n == 1)
        def _():
            q_copy(2).start()
            q_copy(3).start()
            q_copy(6).start()
            q_copy(7).start()
            q_copy(4).start()
            q_copy(5).start()
            for part in range(2):
                for side_half in range(2):
                    for i in (2, 1, 3):
                        wd_copy(part, side_half, i).start()


        first = {}
        for i in range(group_batches):
            at = pl.ds(pl.multiple_of(at_x * chip_rows + i * MB, MB), MB)
            for p in range(pairs):
                lanes = slice(p * PAIR, (p + 1) * PAIR)
                keys = recv[1, at, lanes]
                values = recv[2, at, lanes]
                swapped = pltpu.roll(values.astype(F32), HD, 1).astype(BF)
                both = lax.dot_general(
                    keys, jnp.concatenate([keys, swapped], axis=1),
                    (((0,), (0,)), ((), ())), preferred_element_type=F32,
                )
                linear = jnp.where(own, rates[p] * both[:, :PAIR], 0.0)
                offset = jnp.where(own, 0.0, rates[p] * both[:, PAIR:])
                high, low = split(linear)
                a_ref[i, p, :, :PAIR] = high
                a_ref[i, p, :, PAIR:] = low
                b_ref[i, p] = offset
                if i in (0, group_batches - 1):
                    first[i, p] = eye - linear + offset
        base_batch = at_x * group_batches
        states = {}
        for p in range(pairs):
            for way in range(2):
                i = 0 if way == 0 else group_batches - 1
                states[way, p] = first[i, p]
                pre[way, base_batch + i, p] = first[i, p]
        for t in range(1, group_batches):
            for p in range(pairs):
                for way in range(2):
                    i = t if way == 0 else group_batches - 1 - t
                    state = states[way, p]
                    high, low = split(state)
                    a = a_ref[i, p]
                    change = dot(jnp.concatenate([a, a[:, :PAIR]], axis=1), triple(high, low, 0))
                    states[way, p] = state + b_ref[i, p] - change
                    pre[way, base_batch + i, p] = states[way, p]

        @pl.when(n == 0)
        def _():
            for k in range(2):
                for part in range(2):
                    for i in range(1, xs):
                        wx_copy(part, i, k).wait_recv()
                    for d in (2, 1, 3):
                        w1_copy(part, d, k).start()
            sibling_own.start()
            for part in range(2):
                for d in (1, 2, 3):
                    for k in range(2):
                        w1_copy(part, d, k).wait_recv()
                for d in (1, 3):
                    w2_copy(part, d, 0).start()
            for part in range(2):
                for side_half in range(2):
                    sibling_band(part, 0, side_half, base).start()

    loop(0, xs, chip_maps)

    def linear_of(total):
        return triple(*split(jnp.where(own, total, 0.0)), 1)

    states = {}
    for t in range(xs):
        for p in range(pairs):
            for way in range(2):
                g = t if way == 0 else xs - 1 - t
                b = (g + 1) * group_batches - 1 if way == 0 else g * group_batches
                total = pre[way, b, p]
                if t:
                    change = dot(linear_of(total), triple(*split(states[way, p]), 0))
                    total = jnp.where(own, 0.0, total) + change
                states[way, p] = total
                group[way, g, p] = total
    for way in range(2):
        for p in range(pairs):
            totals[4 * p + way] = states[way, p][:HD]
            totals[4 * p + 2 + way] = states[way, p][HD:]

    shift = c * (seqs // 2)
    my_chain = (s + seqs - shift) % seqs
    is_owner = my_chain < chains

    def chain_at(k):
        return (k + shift) % seqs

    def tot_copy(k):
        return pltpu.make_async_remote_copy(
            src_ref=totals.at[k], dst_ref=inbox.at[s],
            send_sem=tot_send.at[k], recv_sem=tot_recv.at[s],
            device_id=(chain_at(k), h), device_id_type=MESH,
        )

    def tot_arrival(source):
        return pltpu.make_async_remote_copy(
            src_ref=totals.at[0], dst_ref=inbox.at[source],
            send_sem=tot_send.at[0], recv_sem=tot_recv.at[source],
            device_id=((s + 1) % seqs, h), device_id_type=MESH,
        )

    def send_total(d):
        k = (my_chain + d) % seqs

        @pl.when(k < chains)
        def _():
            tot_copy(k).start()

    pl.semaphore_wait(plane, side - 1)
    loop(1, seqs, send_total)

    for part in range(2):
        for d in (1, 3):
            w2_copy(part, d, 1).start()


    def fin_copy(k, to):
        return pltpu.make_async_remote_copy(
            src_ref=outbox.at[to], dst_ref=entry.at[k],
            send_sem=fin_send.at[to], recv_sem=fin_recv.at[k],
            device_id=(to, h), device_id_type=MESH,
        )

    def multiply_queries(dx):
        at_x = (x + xs - dx) % xs

        @pl.when(dx > 0)
        def _():
            q_copy(2 * dx).wait_recv()

        q_copy(2 * dx + 1).wait_recv()

        def one(i):
            b = at_x * group_batches + i
            at = pl.ds(pl.multiple_of(b * MB, MB), MB)
            for p in range(pairs):
                query = recv[0, at, p * PAIR:(p + 1) * PAIR]
                ahead, behind = pre[0, b, p], pre[1, b, p]
                high, low = split(jnp.concatenate(
                    [jnp.where(own, ahead, 0.0), jnp.where(own, behind, 0.0), jnp.where(own, 0.0, ahead + behind)],
                    axis=1,
                ))
                product = dot(jnp.concatenate([query, query], axis=1), jnp.concatenate([high, low], axis=0))
                high, low = split(product[:, :2 * PAIR])
                q_high[p, at, :] = high
                q_low[p, at, :] = low
                r_ref[p, at, :] = product[:, 2 * PAIR:]

        loop(0, group_batches, one)

    own_q.wait()
    loop(0, xs - 1, lambda n: multiply_queries(near(n)))

    @pl.when(is_owner)
    def _():
        inbox[s] = totals[my_chain]
        way = my_chain % 2
        number = my_chain // 2
        odd = number % 2
        half_lane = lax.broadcasted_iota(jnp.int32, (HD, PAIR), 1)
        mine = half_lane // HD != odd
        start = initial[number]

        def place(t):
            return jnp.where(way == 0, t, seqs - 1 - t)

        def arrive(source):
            @pl.when(source != s)
            def _():
                tot_arrival(source).wait_recv()

        loop(0, seqs, arrive)

        def apply(total, high, low):
            linear_high, linear_low = split(jnp.where(mine, 0.0, total))
            return jnp.where(mine, total, 0.0) + dot(
                triple(linear_high, linear_low, 1),
                jnp.concatenate([high, high, high, high, low, low], axis=0),
            )

        def emit(t, state):
            high, low = split(state)
            outbox[place(t)] = (high.astype(F32) + pltpu.roll(low.astype(F32), HD, 1)).astype(BF)

        quads = seqs // side
        maps = [[None] * side for _ in range(quads)]
        for j in range(side):
            for g in range(quads):
                total = inbox[place(g * side + j)]
                maps[g][j] = total if j == 0 else apply(total, *split(maps[g][j - 1]))
        state = jnp.where(mine, jnp.concatenate([start, start], axis=1), 0.0)
        states = [state]
        for g in range(quads - 1):
            states.append(jnp.where(mine, apply(maps[g][side - 1], *split(states[-1])), 0.0))
        for g in range(quads):
            emit(g * side, states[g])
            parts = split(states[g])
            for j in range(side - 1):
                emit(g * side + j + 1, jnp.where(mine, apply(maps[g][j], *parts), 0.0))

        entry[my_chain] = outbox[s]
        loop(1, seqs, lambda d: fin_copy(my_chain, (s + d) % seqs).start())

    multiply_queries(jnp.int32(xs // 2))

    for part in range(2):
        for d in (1, 3):
            w2_copy(part, d, 2).start()

    for part in range(2):
        for d in (1, 3):
            w2_copy(part, d, 0).wait_recv()
            w3_copy(part, d, 0).start()
    for part in range(2):
        for d in (1, 3):
            w3_copy(part, d, 1).start()
    for part in range(2):
        for d in (1, 3):
            sibling_band(part, d, passed[d], base).start()

    def wait_entry(k):
        @pl.when(chain_at(k) != s)
        def _():
            fin_copy(k, (s + 1) % seqs).wait_recv()

    loop(0, chains, wait_entry)

    half_upper = lax.broadcasted_iota(jnp.int32, (HD, PAIR), 1) >= HD
    mean = jnp.where(own, 1.0 / HD, 0.0).astype(BF)
    mean = jnp.concatenate([mean, mean], axis=0)
    entered = []
    for p in range(pairs):
        ways = []
        for way in range(2):
            highs, lows = [], []
            for odd in range(2):
                packed = entry[4 * p + 2 * odd + way].astype(F32)
                mine = half_upper if odd == 0 else jnp.logical_not(half_upper)
                highs.append(jnp.where(mine, packed, 0.0).astype(BF))
                lows.append(jnp.where(mine, pltpu.roll(packed, HD, 1), 0.0).astype(BF))
            ways.append((jnp.concatenate(highs, axis=0), jnp.concatenate(lows, axis=0)))
        entered.append(ways)

    def nrm_copy(d):
        to = peer(d, 1)
        return pltpu.make_async_remote_copy(
            src_ref=normed.at[pl.ds(pl.multiple_of(to * rows, rows), rows), :],
            dst_ref=normed_in.at[(xs - d // 2) % xs, :, pl.ds(pl.multiple_of(c * width, PAIR), width)],
            send_sem=nrm_send.at[d], recv_sem=nrm_recv.at[d],
            device_id=(s, to), device_id_type=MESH,
        )

    own_normed = pltpu.make_async_copy(
        normed.at[pl.ds(pl.multiple_of(h * rows, rows), rows), :],
        normed_in.at[0, :, pl.ds(pl.multiple_of(c * width, PAIR), width)],
        own_sem.at[3],
    )

    def read_chip(dx):
        at_x = (x + dx) % xs
        at = pl.ds(pl.multiple_of(at_x * chip_rows, chip_rows), chip_rows)
        for p in range(pairs):
            highs, lows = [], []
            for way in range(2):
                high, low = entered[p][way]
                before = (at_x + xs - 1) % xs if way == 0 else (at_x + 1) % xs
                total = group[way, before, p]
                moved = jnp.where(own, 0.0, total) + dot(linear_of(total), triple(high, low, 0))
                edge = at_x == (0 if way == 0 else xs - 1)
                moved_high, moved_low = split(jnp.where(own, 0.0, moved))
                highs.append(jnp.where(edge, high, moved_high))
                lows.append(jnp.where(edge, low, moved_low))
            weight = jnp.concatenate([jnp.concatenate(highs, axis=0), jnp.concatenate(lows, axis=0)], axis=1)
            product = dot(q_high[p, at, :], weight)
            read = product[:, :PAIR] + product[:, PAIR:] + dot(q_low[p, at, :], weight[:, :PAIR]) + r_ref[p, at, :]
            high, low = split(read * read)
            mean_square = dot(jnp.concatenate([high, low], axis=1), mean)
            value = pltpu.roll(read * lax.rsqrt(mean_square + 1e-06), HD, 1)
            value = value * gain[p * PAIR:(p + 1) * PAIR]
            normed[at, p * PAIR:(p + 1) * PAIR] = value.astype(BF)

    def read_and_send(n):
        dx = near(xs - 1 - n)
        read_chip(dx)

        @pl.when(dx > 0)
        def _():
            nrm_copy(2 * dx).start()

        nrm_copy(2 * dx + 1).start()

    loop(0, xs, read_and_send)
    own_normed.start()

    for part in range(2):
        for d in (1, 3):
            w2_copy(part, d, 1).wait_recv()
            w2_copy(part, d, 2).wait_recv()
            sibling_band(part, d, 1 - passed[d], base).start()
    for part in range(2):
        for side_half in range(2):
            for i in range(1, xs):
                wd_copy(part, side_half, i).wait_recv()
            sibling_direct(part, side_half, base).start()
    for k in range(2):
        for part in range(2):
            for d in (1, 3):
                w3_copy(part, d, k).wait_recv()
                sibling_quarter(part, d, k, base).start()

    own_w.wait()
    sibling_own.wait_recv()
    own_normed.wait()
    nrm_copy(1).wait_recv()

    def project_own(j):
        mixed[j] = dot(normed_in[0], whole[0, :, pl.ds(pl.multiple_of(j * cols, PAIR), cols)])

    loop(0, side, project_own)
    for d in range(2, heads):
        nrm_copy(d).wait_recv()

    outgoing = []
    for k in range(2):
        if k == 0:
            for part in range(2):
                for d in (0, 1, 3):
                    for side_half in range(2):
                        sibling_band(part, d, side_half, width - base).wait_recv()
                for side_half in range(2):
                    sibling_direct(part, side_half, width - base).wait_recv()
        for part in range(2):
            for d in (1, 3):
                sibling_quarter(part, d, k, width - base).wait_recv()

        def project(side_half):
            at = pl.ds(pl.multiple_of((2 * side_half + k) * cols, PAIR), cols)
            total = mixed[2 * side_half + k]
            for i in range(1, xs):
                total = total + dot(normed_in[i], whole[i, :, at])
            mixed[2 * side_half + k] = total
            pltpu.make_async_copy(mixed.at[2 * side_half + k], out.at[:, at], out_sem.at[2 * side_half + k]).start()

        loop(0, 2, project)

    for j in range(side):
        pltpu.make_async_copy(mixed.at[j], out.at[:, pl.ds(j * cols, cols)], out_sem.at[j]).wait()

    for part in range(2):
        for i in range(1, xs):
            for k in range(2):
                wx_copy(part, i, k).wait_send()
                w1_copy(part, i, k).wait_send()
        for d in (1, 3):
            w2_copy(part, d, 0).wait_send()
            w2_copy(part, d, 1).wait_send()
            w2_copy(part, d, 2).wait_send()
            for k in range(2):
                w3_copy(part, d, k).wait_send()
                sibling_quarter(part, d, k, base).wait_send()
        for side_half in range(2):
            for i in range(1, xs):
                wd_copy(part, side_half, i).wait_send()
            sibling_direct(part, side_half, base).wait_send()
        for d in (0, 1, 3):
            for side_half in range(2):
                sibling_band(part, d, side_half, base).wait_send()
    sibling_own.wait_send()

    def drain_head(d):
        kv_copy(d).wait_send()
        q_copy(d).wait_send()
        nrm_copy(d).wait_send()

    def drain_total(k):
        @pl.when(chain_at(k) != s)
        def _():
            tot_copy(k).wait_send()

    loop(1, heads, drain_head)
    loop(0, chains, drain_total)

    @pl.when(is_owner)
    def _():
        def drain_fin(to):
            @pl.when(to != s)
            def _():
                fin_copy(my_chain, to).wait_send()

        loop(0, seqs, drain_fin)


def layer(qkv, eta, initial, gain, w_out, seqs, heads):
    rows = qkv.shape[1]
    width, columns = w_out.shape
    pairs = width // PAIR
    tokens = rows * heads
    batches = tokens // MB
    xs = heads // 2
    anywhere = pl.BlockSpec(memory_space=pltpu.HBM)
    dma = pltpu.SemaphoreType.DMA
    return pl.pallas_call(
        functools.partial(layer_kernel, seqs, heads, pairs),
        out_shape=jax.ShapeDtypeStruct((rows, columns), F32),
        in_specs=[anywhere] * 5,
        out_specs=anywhere,
        scratch_shapes=[
            pltpu.SMEM(eta.shape, F32),
            pltpu.VMEM(initial.shape, F32),
            pltpu.VMEM(gain.shape, F32),
            pltpu.VMEM((3, tokens, width), BF),
            pltpu.VMEM((batches // xs, pairs, PAIR, 2 * PAIR), BF),
            pltpu.VMEM((batches // xs, pairs, PAIR, PAIR), F32),
            pltpu.VMEM((2, batches, pairs, PAIR, PAIR), F32),
            pltpu.VMEM((2, xs, pairs, PAIR, PAIR), F32),
            pltpu.VMEM((4 * pairs, HD, PAIR), F32),
            pltpu.VMEM((seqs, HD, PAIR), F32),
            pltpu.VMEM((seqs, HD, PAIR), BF),
            pltpu.VMEM((4 * pairs, HD, PAIR), BF),
            pltpu.VMEM((pairs, tokens, 2 * PAIR), BF),
            pltpu.VMEM((pairs, tokens, 2 * PAIR), BF),
            pltpu.VMEM((pairs, tokens, PAIR), F32),
            pltpu.VMEM((tokens, width), BF),
            pltpu.VMEM((xs, rows, 2 * width), BF),
            pltpu.VMEM((xs, 2 * width, columns), BF),
            pltpu.VMEM((4, rows, columns // 4), F32),
            dma((3,)), dma((4,)),
            dma((heads,)), dma((heads,)), dma((heads,)), dma((heads,)),
            dma((4 * pairs,)), dma((seqs,)), dma((seqs,)), dma((4 * pairs,)),
            dma((heads,)), dma((heads,)),
            dma((2, 4, 2)), dma((2, 4, 2)), dma((2, 4, 2)), dma((2, 4, 2)), dma((2, 4, 3)), dma((2, 4, 3)),
            dma((2, 4, 2)), dma((2, 4, 2)), dma((3, 4, 2)), dma((3, 4, 2)), dma((2, 4, 2)), dma((2, 4, 2)),
            pltpu.SemaphoreType.REGULAR, dma((4,)), dma((2, 2, 4)), dma((2, 2, 4)), dma((2, 2)), dma((2, 2)),
        ],
        compiler_params=pltpu.CompilerParams(
            collective_id=0, has_side_effects=True, vmem_limit_bytes=57 << 20
        ),
    )(qkv, eta, initial, gain, w_out)


def solution(mesh):
    seqs, heads = mesh.shape["seq"], mesh.shape["head"]

    def shards(qkv, eta, initial, gain, w_out):
        return layer(jnp.transpose(qkv, (1, 0, 2)), eta, initial, gain, w_out, seqs, heads)

    return jax.shard_map(
        shards,
        mesh=mesh,
        in_specs=(
            P(("seq", "head"), None, None),
            P("head"),
            P("head", None, None),
            P("head"),
            P("head", None),
        ),
        out_specs=P(("seq", "head"), None),
        check_vma=False,
    )
```
